128 devices in a mesh: seq: 32 (over y, z, core), batch: 4 (over x).
Axes of the slice: x: 4, y: 4, z: 4, core: 2. Of those that a mesh axis runs over, the one named last changes fastest.
Arguments:
- signal: bfloat16 [4, 4096, 8192], P('batch', 'seq'), may hold values from -6 to 6
- out_grad: bfloat16 [4, 4096, 8192], P('batch', 'seq'), may hold values from -6 to 6
- residues: float32 [8, 8192], replicated, may hold values from -0.3 to 0.3
- log_rates: float32 [8, 512], replicated, as said below
Outputs:
- mixed: bfloat16 [4, 4096, 8192], P('batch', 'seq')
- grad_signal: bfloat16 [4, 4096, 8192], P('batch', 'seq')
- grad_residues: float32 [8, 8192], replicated
- grad_rates: float32 [8, 512], replicated
The draws below stay inside these ranges and needn't reach their ends.
Inputs may be any that keep to these rules, and one draw needn't show every extreme that they name: Each decay rate exp(log_rates) lies between 0.2 / 4096 and 1 / 30.
All inputs are finite; a program needn't handle non-finite values.
Results may differ from the reference program's by a relative error of at most 0.0012.
Values sent between devices are 32-bit elements; how exact they have to be, the bound alone decides.
No kernel may reach another device: no remote copies, remote signals or barrier semaphores. Data moves between devices by JAX's collectives and lax.ppermute only.
A program may use at most 384 MiB of HBM per device.

```python
import jax
import jax.numpy as jnp
from jax import lax

D = 8192
M = 8
GROUP = 16
LEN = 4096
BATCH = 4


def draw_log_rates(key, part):
    key_coin, key_slow, key_fast = jax.random.split(key, 3)
    shape = (M, D // GROUP)
    slow_share = 0.125
    coin = jax.random.uniform(key_coin, shape, jnp.float32) < slow_share
    slow_low = jnp.log(0.2 / LEN)
    slow_high = jnp.log(2.0 / LEN)
    fast_low = jnp.log(0.01)
    fast_high = jnp.log(1.0 / 30.0)
    slow_value = slow_low + jax.random.uniform(key_slow, shape, jnp.float32) * (slow_high - slow_low)
    fast_value = fast_low + jax.random.uniform(key_fast, shape, jnp.float32) * (fast_high - fast_low)
    return jnp.where(coin, slow_value, fast_value).astype(jnp.float32)


def steps_of(rng, shape, shards, smallest, high):
    def one(position, blocks):
        draws = jax.random.uniform(jax.random.fold_in(jax.random.fold_in(rng, 6), position), (blocks,), jnp.float32, smallest / len(shards), high / len(shards))
        return jnp.repeat(jnp.exp(draws), shape[position] // blocks).reshape((-1,) + (1,) * (len(shape) - position - 1))

    loudness = one(*shards[0])
    for cut in shards[1:]:
        loudness = loudness * one(*cut)
    return loudness


def normal_values(key, extent, scale, most, cuts=(), held_as=jnp.bfloat16):
    drawn = scale * jax.random.normal(key, extent, jnp.float32)
    if cuts:
        drawn = drawn * steps_of(key, extent, cuts, -0.22, 0.18)
    return jnp.clip(drawn, -most, most).astype(held_as)


def setup_inputs(seed: int = 0) -> dict:
    splits = jax.random.split(jax.random.key(seed), 5)
    signal = normal_values(splits[0], (BATCH, LEN, D), 1.0, 6.0, ((0, 4), (1, 32)))
    out_grad = normal_values(splits[1], (BATCH, LEN, D), 1.0, 6.0, ((0, 4), (1, 32)))
    residues = normal_values(splits[2], (M, D), 0.05, 0.3, (), jnp.float32)
    log_rates = draw_log_rates(jax.random.fold_in(splits[4], 71), 0)
    return dict(signal=signal, out_grad=out_grad, residues=residues, log_rates=log_rates)


def expand(values):
    return jnp.repeat(values, GROUP, axis=1)


def reference(signal, out_grad, residues, log_rates):
    decay_rate = jnp.exp(log_rates)
    pole_values = expand(jnp.exp(-decay_rate))
    empty_state = jnp.zeros((BATCH, M, D), jnp.float32)
    empty_sum = jnp.zeros((M, D), jnp.float32)

    def forward_step(carried, rows):
        modal_state, moment, sum_residue, sum_moment = carried
        signal_row = rows[0].astype(jnp.float32)[:, None, :]
        grad_row = rows[1].astype(jnp.float32)[:, None, :]
        moment = pole_values * (moment + modal_state)
        modal_state = pole_values * modal_state + signal_row
        out_row = jnp.sum(residues * modal_state, axis=1)
        sum_residue = sum_residue + jnp.sum(grad_row * modal_state, axis=0)
        sum_moment = sum_moment + jnp.sum(grad_row * moment, axis=0)
        return (modal_state, moment, sum_residue, sum_moment), out_row.astype(jnp.bfloat16)

    rows = (jnp.swapaxes(signal, 0, 1), jnp.swapaxes(out_grad, 0, 1))
    finals, outputs = lax.scan(forward_step, (empty_state, empty_state, empty_sum, empty_sum), rows)

    def backward_step(adjoint, grad_in):
        adjoint = pole_values * adjoint + grad_in.astype(jnp.float32)[:, None, :]
        return adjoint, jnp.sum(residues * adjoint, axis=1).astype(jnp.bfloat16)

    unused, grads = lax.scan(backward_step, empty_state, rows[1], reverse=True)
    norm_factor = 1.0 / (BATCH * LEN)
    grad_residues = finals[2] * norm_factor
    grad_rates = -decay_rate * jnp.sum((residues * finals[3]).reshape(M, D // GROUP, GROUP), axis=2) * norm_factor
    return jnp.swapaxes(outputs, 0, 1), jnp.swapaxes(grads, 0, 1), grad_residues, grad_rates
```

```python
import functools

import jax
import jax.numpy as jnp
import numpy as np
from jax import lax
from jax.experimental import pallas as pl
from jax.experimental.pallas import tpu as pltpu
from jax.sharding import PartitionSpec as P

M = 8
GROUP = 16
SPAN = 128
SLICE = 256
GROUPS = SLICE // GROUP
WIDE = 512
PER = WIDE // SLICE
F32 = jnp.float32
BF16 = jnp.bfloat16


def split_np(values):
    high = values.astype(np.float32).astype(jnp.bfloat16)
    low = (values - high.astype(np.float64)).astype(np.float32).astype(jnp.bfloat16)
    return high, low


def transforms():
    time = np.arange(SPAN)
    angle = 2 * np.pi * np.outer(np.arange(SPAN) + 0.5, time) / (2 * SPAN)
    forward = np.concatenate([np.cos(angle), -np.sin(angle)], 0)
    inverse = np.concatenate([np.cos(angle.T), -np.sin(angle.T)], 1) / SPAN
    fh, fl = split_np(forward)
    ih, il = split_np(inverse)
    return np.concatenate([fh, fl, fh], 1), np.concatenate([ih, il, ih], 1)


def split(values):
    high = values.astype(BF16)
    return high, (values - high.astype(F32)).astype(BF16)


def dot(a, b):
    return jnp.dot(a, b, preferred_element_type=F32)


def twice(values):
    return jnp.concatenate([values, values], 0)


def stacked(values):
    high, low = split(values)
    return jnp.concatenate([high, high, low], 0)


def lane_group(rows, lanes):
    return lax.broadcasted_iota(jnp.int32, (rows, lanes), 1) // GROUP


def spread(values):
    high = values.astype(BF16).astype(F32)
    low = values - high
    owner = lane_group(M, SLICE)

    def rows(part):
        return jnp.concatenate([jnp.where(owner == g, part, 0.0) for g in range(GROUPS)], 0).astype(BF16)

    top = rows(high)
    return jnp.concatenate([top, top, rows(low)], 0)


def powers(rate_row, reverse):
    t = lax.broadcasted_iota(jnp.int32, (SPAN, SPAN), 0)
    t = (SPAN - 1 - t if reverse else t).astype(F32)
    high, low = split(jnp.exp(-rate_row[0:1, :] * t))
    return jnp.concatenate([high, low, high], 1)


def first_kernel(x_ref, g_ref, rate_ref, res_ref, fwd_ref, inv_ref, send_ref):
    x, g = x_ref[0], g_ref[0]
    xx, gg = twice(x), twice(g)
    forward = fwd_ref[:, : 2 * SPAN]
    xf = dot(forward, xx)
    gf = dot(forward, gg)
    xr, xi, gr, gi = xf[:SPAN], xf[SPAN:], gf[:SPAN], gf[SPAN:]
    lags = dot(inv_ref[...], stacked(jnp.concatenate([gr * xr + gi * xi, gi * xr - gr * xi], 0)))
    lag3 = stacked(lags)
    lag = lax.broadcasted_iota(jnp.int32, (SPAN, SPAN), 1).astype(F32)
    back = (SPAN - 1) - lag
    half = SPAN // GROUP
    owner = lane_group(M, SPAN)
    row = lax.broadcasted_iota(jnp.int32, (SPAN, SPAN), 0) // GROUP
    col = lax.broadcasted_iota(jnp.int32, (SPAN, SPAN), 1)

    def pick(values, q):
        at = q * half * M
        chosen = values[at : at + M]
        for k in range(1, half):
            chosen = jnp.where(owner == k, values[at + k * M : at + (k + 1) * M], chosen)
        return chosen

    for s in range(PER):
        rates = jnp.transpose(jnp.broadcast_to(rate_ref[s, 0:1, :], (SPAN, SPAN)))
        early, late = jnp.exp(-rates * lag), jnp.exp(-rates * back)
        rate_sum = jnp.zeros((M, SPAN), F32)
        for h in range(2):
            rows = slice(h * half * M, (h + 1) * half * M)
            cols = slice(s * SLICE + h * SPAN, s * SLICE + (h + 1) * SPAN)
            eh, el = split(jnp.concatenate([early[rows], lag[rows] * early[rows]], 0))
            lh, ll = split(jnp.concatenate([late[rows], back[rows] * late[rows]], 0))
            ends = dot(jnp.concatenate([lh, ll], 1), xx[:, cols])
            starts = dot(jnp.concatenate([eh, el], 1), gg[:, cols])
            sums = dot(jnp.concatenate([eh, el, eh], 1), lag3[:, cols])
            for q, values in enumerate((pick(ends, 0), pick(starts, 0), pick(ends, 1), pick(starts, 1), pick(sums, 0))):
                at = (2 * q + h) * M
                send_ref[s, at : at + M, :] = values
            weighted = res_ref[:, cols] * pick(sums, 1)
            place = jnp.where(row + h * half == col, 1.0, 0.0).astype(BF16)
            wh, wl = split(weighted)
            rate_sum = rate_sum + dot(wh, place) + dot(wl, place)
        send_ref[s, 10 * M : 11 * M, :] = rate_sum


def second_kernel(x_ref, g_ref, rate_ref, res_ref, fwd_ref, inv_ref, mixed_ref, grad_ref):
    forward = fwd_ref[:, : 2 * SPAN]
    for s in range(PER):
        cols = slice(s * SLICE, (s + 1) * SLICE)
        taps = dot(powers(rate_ref[s], False), spread(res_ref[:, cols]))
        kf = dot(fwd_ref[...], stacked(taps))
        xf = dot(forward, twice(x_ref[0, :, cols]))
        gf = dot(forward, twice(g_ref[0, :, cols]))
        kr, ki, xr, xi, gr, gi = kf[:SPAN], kf[SPAN:], xf[:SPAN], xf[SPAN:], gf[:SPAN], gf[SPAN:]
        mixed_ref[:, cols] = dot(inv_ref[...], stacked(jnp.concatenate([kr * xr - ki * xi, kr * xi + ki * xr], 0)))
        grad_ref[:, cols] = dot(inv_ref[...], stacked(jnp.concatenate([kr * gr + ki * gi, kr * gi - ki * gr], 0)))


def middle_kernel(chunks, got_ref, rate_ref, res_ref, back_ref, sums_ref):
    rate_sum = jnp.zeros((M, SPAN), F32)
    for k in range(chunks):
        rate_sum = rate_sum + got_ref[k, 10 * M : 11 * M, :]
    row = lax.broadcasted_iota(jnp.int32, (SPAN, SPAN), 0) // GROUP
    col = lax.broadcasted_iota(jnp.int32, (SPAN, SPAN), 1)
    for h in range(2):
        cols = slice(h * SPAN, (h + 1) * SPAN)
        rate, res = rate_ref[:, cols], res_ref[:, cols]
        pole = jnp.exp(-rate)
        across = jnp.exp(-rate * SPAN)
        handed = res * pole

        def part(k, q):
            at = (2 * q + h) * M
            return got_ref[k, at : at + M, :]

        zero = jnp.zeros((M, SPAN), F32)
        state, moment, res_part, res_carry, rate_carry = zero, zero, zero, zero, zero
        for k in range(chunks):
            back_ref[k, h * M : (h + 1) * M, :] = handed * state
            start = part(k, 1)
            res_part = res_part + part(k, 4)
            res_carry = res_carry + state * start
            rate_carry = rate_carry + state * (part(k, 3) + start) + moment * start
            moment = across * (moment + SPAN * state) + part(k, 2)
            state = across * state + part(k, 0)
        adjoint = zero
        for k in reversed(range(chunks)):
            back_ref[k, (2 + h) * M : (3 + h) * M, :] = handed * adjoint
            adjoint = across * adjoint + part(k, 1)
        sums_ref[h * M : (h + 1) * M, :] = res_part + pole * res_carry
        weighted = handed * rate_carry
        place = jnp.where(row + h * (SPAN // GROUP) == col, 1.0, 0.0).astype(BF16)
        wh, wl = split(weighted)
        rate_sum = rate_sum + dot(wh, place) + dot(wl, place)
    sums_ref[2 * M : 3 * M, :] = rate_sum


def last_kernel(mixed_ref, grad_ref, rate_ref, got_ref, mixed_out, grad_out):
    for s in range(PER):
        cols = slice(s * SLICE, (s + 1) * SLICE)
        state = jnp.concatenate([got_ref[s, 0:M, :], got_ref[s, M : 2 * M, :]], 1)
        adjoint = jnp.concatenate([got_ref[s, 2 * M : 3 * M, :], got_ref[s, 3 * M : 4 * M, :]], 1)
        more = dot(powers(rate_ref[s], False), spread(state))
        mixed_out[0, :, cols] = (mixed_ref[:, cols] + more).astype(BF16)
        more = dot(powers(rate_ref[s], True), spread(adjoint))
        grad_out[0, :, cols] = (grad_ref[:, cols] + more).astype(BF16)


def local(signal, out_grad, residues, log_rates):
    channels = signal.shape[2]
    chunks, rows = lax.axis_size("seq"), lax.axis_size("batch")
    index = lax.axis_index("seq")
    steps = channels // WIDE
    fwd, inv = (jnp.asarray(v) for v in transforms())
    decay_rate = jnp.exp(log_rates)
    rate_rows = jnp.broadcast_to(decay_rate.T.reshape(chunks, 1, SPAN), (chunks, M, SPAN))
    own_rate = jnp.repeat(lax.dynamic_slice_in_dim(decay_rate, index * GROUPS, GROUPS, 1), GROUP, axis=1)
    own_res = lax.dynamic_slice_in_dim(residues, index * SLICE, SLICE, 1)

    seq_block = pl.BlockSpec((1, SPAN, WIDE), lambda i: (0, 0, i))
    flat_block = pl.BlockSpec((SPAN, WIDE), lambda i: (0, i))
    rate_block = pl.BlockSpec((PER, M, SPAN), lambda i: (i, 0, 0))
    res_block = pl.BlockSpec((M, WIDE), lambda i: (0, i))
    whole = lambda a: pl.BlockSpec(a.shape, lambda i: (0,) * a.ndim)
    params = pltpu.CompilerParams(vmem_limit_bytes=32 * 2**20)
    both = 2 * SPAN * channels

    send = pl.pallas_call(
        first_kernel,
        grid=(steps,),
        in_specs=[seq_block, seq_block, rate_block, res_block, whole(fwd), whole(inv)],
        out_specs=pl.BlockSpec((PER, 11 * M, SPAN), lambda i: (i, 0, 0)),
        out_shape=jax.ShapeDtypeStruct((chunks, 11 * M, SPAN), F32),
        compiler_params=params,
        name="ends_and_lags",
    )(signal, out_grad, rate_rows, residues, fwd, inv)
    got = lax.all_to_all(send, "seq", 0, 0, tiled=True)

    mixed_part, grad_part = pl.pallas_call(
        second_kernel,
        grid=(steps,),
        in_specs=[seq_block, seq_block, rate_block, res_block, whole(fwd), whole(inv)],
        out_specs=[flat_block, flat_block],
        out_shape=[jax.ShapeDtypeStruct((SPAN, channels), F32)] * 2,
        compiler_params=params,
        cost_estimate=pl.CostEstimate(flops=both * 3000, bytes_accessed=both * 8, transcendentals=both),
        name="local_convolutions",
    )(signal, out_grad, rate_rows, residues, fwd, inv)

    back, sums = pl.pallas_call(
        functools.partial(middle_kernel, chunks),
        out_shape=[
            jax.ShapeDtypeStruct((chunks, 4 * M, SPAN), F32),
            jax.ShapeDtypeStruct((3 * M, SPAN), F32),
        ],
        name="carries",
    )(got, own_rate, own_res)
    carried = lax.all_to_all(back, "seq", 0, 0, tiled=True)
    total = sums
    for k in range(1, rows):
        total = total + lax.ppermute(sums, "batch", [(i, (i + k) % rows) for i in range(rows)])
    total = total * (1.0 / (rows * chunks * SPAN))
    everyone = lax.all_to_all(jnp.broadcast_to(total[None], (chunks, 3 * M, SPAN)), "seq", 0, 0, tiled=True)

    mixed, grad_signal = pl.pallas_call(
        last_kernel,
        grid=(steps,),
        in_specs=[
            flat_block,
            flat_block,
            rate_block,
            pl.BlockSpec((PER, 4 * M, SPAN), lambda i: (i, 0, 0)),
        ],
        out_specs=[seq_block, seq_block],
        out_shape=[jax.ShapeDtypeStruct(signal.shape, BF16)] * 2,
        compiler_params=params,
        cost_estimate=pl.CostEstimate(flops=both * 800, bytes_accessed=both * 6, transcendentals=both),
        name="add_carries",
    )(mixed_part, grad_part, rate_rows, carried)
    grad_residues = everyone[:, : 2 * M].reshape(chunks, 2, M, SPAN).transpose(2, 0, 1, 3).reshape(M, channels)
    grad_rates = -decay_rate * everyone[:, 2 * M :, :GROUPS].transpose(1, 0, 2).reshape(M, chunks * GROUPS)
    return mixed, grad_signal, grad_residues, grad_rates


def solution(mesh):
    placed = P("batch", "seq", None)
    return jax.shard_map(
        local,
        mesh=mesh,
        in_specs=(placed, placed, P(), P()),
        out_specs=(placed, placed, P(), P()),
        check_vma=False,
    )
```

```python
import functools

import jax
import jax.numpy as jnp
import numpy as np
from jax import lax
from jax.experimental import pallas as pl
from jax.experimental.pallas import tpu as pltpu
from jax.sharding import PartitionSpec as P

M = 8
GROUP = 16
SPAN = 128
SLICE = 256
GROUPS = SLICE // GROUP
WIDE = 2048
F32 = jnp.float32
BF16 = jnp.bfloat16


def split_np(values):
    high = values.astype(np.float32).astype(jnp.bfloat16)
    low = (values - high.astype(np.float64)).astype(np.float32).astype(jnp.bfloat16)
    return high, low


def transforms():
    time = np.arange(SPAN)
    angle = 2 * np.pi * np.outer(np.arange(SPAN) + 0.5, time) / (2 * SPAN)
    forward = np.concatenate([np.cos(angle), -np.sin(angle)], 0)
    inverse = np.concatenate([np.cos(angle.T), -np.sin(angle.T)], 1) / SPAN
    fh, fl = split_np(forward)
    ih, il = split_np(inverse)
    return np.concatenate([fh, fl, fh, fl], 1), np.concatenate([ih, il, ih], 1)


def split(values):
    high = values.astype(BF16)
    return high, (values - high.astype(F32)).astype(BF16)


def dot(a, b):
    return jnp.dot(a, b, preferred_element_type=F32)


def paired(values):
    high, low = split(values)
    return jnp.concatenate([high, high, low, low], 0)


def twice(values):
    return jnp.concatenate([values, values], 0)


def stacked(values):
    high, low = split(values)
    return jnp.concatenate([high, high, low], 0)


def lane_group(rows, lanes):
    return lax.broadcasted_iota(jnp.int32, (rows, lanes), 1) // GROUP


def spread(values):
    high = values.astype(BF16).astype(F32)
    low = values - high
    owner = lane_group(M, SLICE)

    def rows(part):
        return jnp.concatenate([jnp.where(owner == g, part, 0.0) for g in range(GROUPS)], 0).astype(BF16)

    top, bottom = rows(high), rows(low)
    return jnp.concatenate([top, top, bottom, bottom], 0)


def powers(rate_row, reverse):
    t = lax.broadcasted_iota(jnp.int32, (SPAN, SPAN), 0)
    t = (SPAN - 1 - t if reverse else t).astype(F32)
    high, low = split(jnp.exp(-rate_row[0:1, :] * t))
    return jnp.concatenate([high, low, high, low], 1)


def first_kernel(x_ref, g_ref, rate_ref, res_ref, fwd_ref, inv_ref, send_ref):
    x, g = x_ref[0], g_ref[0]
    xx, gg = twice(x), twice(g)
    forward = fwd_ref[:, : 2 * SPAN]
    xf = dot(forward, xx)
    gf = dot(forward, gg)
    xr, xi, gr, gi = xf[:SPAN], xf[SPAN:], gf[:SPAN], gf[SPAN:]
    lags = dot(inv_ref[...], stacked(jnp.concatenate([gr * xr + gi * xi, gi * xr - gr * xi], 0)))
    lag_high, lag_low = split(lags)
    lag_high, lag_low = twice(lag_high), twice(lag_low)
    flip = jnp.where(lax.broadcasted_iota(jnp.int32, (SPAN, SPAN), 0) + lax.broadcasted_iota(jnp.int32, (SPAN, SPAN), 1) == SPAN - 1, 1.0, 0.0).astype(BF16)
    backward = twice(dot(flip, x).astype(BF16))
    lag = lax.broadcasted_iota(jnp.int32, (SPAN, SPAN), 1).astype(F32)
    half = SPAN // GROUP
    owner = lane_group(M, SPAN)
    row = lax.broadcasted_iota(jnp.int32, (SPAN, SPAN), 0) // GROUP
    col = lax.broadcasted_iota(jnp.int32, (SPAN, SPAN), 1)

    def pick(values, q):
        at = q * half * M
        chosen = values[at : at + M]
        for k in range(1, half):
            chosen = jnp.where(owner == k, values[at + k * M : at + (k + 1) * M], chosen)
        return chosen

    for s in range(rate_ref.shape[0]):
        rates = jnp.transpose(jnp.broadcast_to(rate_ref[s, 0:1, :], (SPAN, SPAN)))
        early = jnp.exp(-rates * lag)
        rate_sum = jnp.zeros((M, SPAN), F32)
        for h in range(2):
            rows = slice(h * half * M, (h + 1) * half * M)
            cols = slice(s * SLICE + h * SPAN, s * SLICE + (h + 1) * SPAN)
            eh, el = split(jnp.concatenate([early[rows], lag[rows] * early[rows]], 0))
            found = dot(
                jnp.concatenate([eh, el], 1),
                jnp.concatenate([backward[:, cols], gg[:, cols], lag_high[:, cols], lag_low[:, cols]], 1),
            )
            ends, starts = found[:, :SPAN], found[:, SPAN : 2 * SPAN]
            sums = found[:, 2 * SPAN : 3 * SPAN] + found[:, 3 * SPAN :]
            for q, values in enumerate((pick(ends, 0), pick(starts, 0), pick(ends, 1), pick(starts, 1), pick(sums, 0))):
                at = (2 * q + h) * M
                send_ref[s, at : at + M, :] = values
            weighted = res_ref[:, cols] * pick(sums, 1)
            place = jnp.where(row + h * half == col, 1.0, 0.0).astype(BF16)
            wh, wl = split(weighted)
            rate_sum = rate_sum + dot(wh, place) + dot(wl, place)
        send_ref[s, 10 * M : 11 * M, :] = rate_sum


def second_kernel(x_ref, g_ref, rate_ref, res_ref, fwd_ref, inv_ref, mixed_ref, grad_ref):
    forward = fwd_ref[:, : 2 * SPAN]
    for s in range(rate_ref.shape[0]):
        cols = slice(s * SLICE, (s + 1) * SLICE)
        taps = dot(powers(rate_ref[s], False), spread(res_ref[:, cols]))
        kf = dot(fwd_ref[...], paired(taps))
        xf = dot(forward, twice(x_ref[0, :, cols]))
        gf = dot(forward, twice(g_ref[0, :, cols]))
        kr, ki, xr, xi, gr, gi = kf[:SPAN], kf[SPAN:], xf[:SPAN], xf[SPAN:], gf[:SPAN], gf[SPAN:]
        mixed_ref[:, cols] = dot(inv_ref[...], stacked(jnp.concatenate([kr * xr - ki * xi, kr * xi + ki * xr], 0)))
        grad_ref[:, cols] = dot(inv_ref[...], stacked(jnp.concatenate([kr * gr + ki * gi, kr * gi - ki * gr], 0)))


def middle_kernel(chunks, index_ref, got_ref, rate_ref, res_ref, back_ref, sums_ref):
    offset = lax.rem(index_ref[0], SPAN // GROUPS) * GROUPS
    rate_sum = jnp.zeros((M, SPAN), F32)
    for k in range(chunks):
        rate_sum = rate_sum + got_ref[k, 10 * M : 11 * M, :]
    rate_sum = pltpu.roll(rate_sum, offset, 1)
    row = lax.broadcasted_iota(jnp.int32, (SPAN, SPAN), 0) // GROUP
    col = lax.broadcasted_iota(jnp.int32, (SPAN, SPAN), 1)
    for h in range(2):
        cols = slice(h * SPAN, (h + 1) * SPAN)
        rate, res = rate_ref[:, cols], res_ref[:, cols]
        pole = jnp.exp(-rate)
        across = jnp.exp(-rate * SPAN)
        handed = res * pole

        def part(k, q):
            at = (2 * q + h) * M
            return got_ref[k, at : at + M, :]

        zero = jnp.zeros((M, SPAN), F32)
        state, moment, res_part, res_carry, rate_carry = zero, zero, zero, zero, zero
        for k in range(chunks):
            back_ref[k, h * M : (h + 1) * M, :] = handed * state
            start = part(k, 1)
            res_part = res_part + part(k, 4)
            res_carry = res_carry + state * start
            rate_carry = rate_carry + state * (part(k, 3) + start) + moment * start
            moment = across * (moment + SPAN * state) + part(k, 2)
            state = across * state + part(k, 0)
        adjoint = zero
        for k in reversed(range(chunks)):
            back_ref[k, (2 + h) * M : (3 + h) * M, :] = handed * adjoint
            adjoint = across * adjoint + part(k, 1)
        sums_ref[h * M : (h + 1) * M, :] = res_part + pole * res_carry
        weighted = handed * rate_carry
        place = jnp.where(row + (h * (SPAN // GROUP) + offset) == col, 1.0, 0.0).astype(BF16)
        wh, wl = split(weighted)
        rate_sum = rate_sum + dot(wh, place) + dot(wl, place)
    sums_ref[2 * M : 3 * M, :] = rate_sum


def last_kernel(mixed_ref, grad_ref, rate_ref, got_ref, mixed_out, grad_out):
    for s in range(rate_ref.shape[0]):
        cols = slice(s * SLICE, (s + 1) * SLICE)
        state = jnp.concatenate([got_ref[s, 0:M, :], got_ref[s, M : 2 * M, :]], 1)
        adjoint = jnp.concatenate([got_ref[s, 2 * M : 3 * M, :], got_ref[s, 3 * M : 4 * M, :]], 1)
        more = dot(powers(rate_ref[s], False), spread(state))
        mixed_out[0, :, cols] = (mixed_ref[:, cols] + more).astype(BF16)
        more = dot(powers(rate_ref[s], True), spread(adjoint))
        grad_out[0, :, cols] = (grad_ref[:, cols] + more).astype(BF16)


def gather_kernel(chunks, all_ref, log_ref, res_out, rate_out):
    for k in range(chunks):
        for h in range(2):
            res_out[:, k * SLICE + h * SPAN : k * SLICE + (h + 1) * SPAN] = all_ref[k, h * M : (h + 1) * M, :]
    width = min(SPAN, chunks * GROUPS)
    per = width // GROUPS
    for j in range(chunks // per):
        parts = all_ref[j * per, 2 * M : 3 * M, :]
        for k in range(j * per + 1, (j + 1) * per):
            parts = parts + all_ref[k, 2 * M : 3 * M, :]
        cols = slice(j * width, (j + 1) * width)
        rate_out[:, cols] = -jnp.exp(log_ref[:, cols]) * parts[:, :width]


def local(signal, out_grad, residues, log_rates):
    channels = signal.shape[2]
    chunks, rows = lax.axis_size("seq"), lax.axis_size("batch")
    index = lax.axis_index("seq")
    wide = min(WIDE, channels)
    steps = channels // wide
    fwd, inv = (jnp.asarray(v) for v in transforms())
    decay_rate = jnp.exp(log_rates)
    rate_rows = jnp.broadcast_to(decay_rate.T.reshape(chunks, 1, SPAN), (chunks, M, SPAN))
    own_rate = jnp.repeat(lax.dynamic_slice_in_dim(decay_rate, index * GROUPS, GROUPS, 1), GROUP, axis=1)
    own_res = lax.dynamic_slice_in_dim(residues, index * SLICE, SLICE, 1)

    seq_block = pl.BlockSpec((1, SPAN, wide), lambda i: (0, 0, i))
    flat_block = pl.BlockSpec((SPAN, wide), lambda i: (0, i))
    rate_block = pl.BlockSpec((wide // SLICE, M, SPAN), lambda i: (i, 0, 0))
    res_block = pl.BlockSpec((M, wide), lambda i: (0, i))
    whole = lambda a: pl.BlockSpec(a.shape, lambda i: (0,) * a.ndim)
    params = pltpu.CompilerParams(vmem_limit_bytes=58 * 2**20)
    both = 2 * SPAN * channels

    send = pl.pallas_call(
        first_kernel,
        grid=(steps,),
        in_specs=[seq_block, seq_block, rate_block, res_block, whole(fwd), whole(inv)],
        out_specs=pl.BlockSpec((wide // SLICE, 11 * M, SPAN), lambda i: (i, 0, 0)),
        out_shape=jax.ShapeDtypeStruct((chunks, 11 * M, SPAN), F32),
        compiler_params=params,
        name="ends_and_lags",
    )(signal, out_grad, rate_rows, residues, fwd, inv)
    got = lax.all_to_all(send, "seq", 0, 0, tiled=True)

    mixed_part, grad_part = pl.pallas_call(
        second_kernel,
        grid=(steps,),
        in_specs=[seq_block, seq_block, rate_block, res_block, whole(fwd), whole(inv)],
        out_specs=[flat_block, flat_block],
        out_shape=[jax.ShapeDtypeStruct((SPAN, channels), F32)] * 2,
        compiler_params=params,
        cost_estimate=pl.CostEstimate(flops=both * 3000, bytes_accessed=both * 8, transcendentals=both),
        name="local_convolutions",
    )(signal, out_grad, rate_rows, residues, fwd, inv)

    got, mixed_part, grad_part = lax.optimization_barrier((got, mixed_part, grad_part))
    vmem = pl.BlockSpec(memory_space=pltpu.VMEM)
    back, sums = pl.pallas_call(
        functools.partial(middle_kernel, chunks),
        out_shape=[
            jax.ShapeDtypeStruct((chunks, 4 * M, SPAN), F32),
            jax.ShapeDtypeStruct((3 * M, SPAN), F32),
        ],
        in_specs=[pl.BlockSpec(memory_space=pltpu.SMEM), vmem, vmem, vmem],
        name="carries",
    )(index.astype(jnp.int32)[None], got, own_rate, own_res)
    carried = lax.all_to_all(back, "seq", 0, 0, tiled=True)
    total = sums
    for k in range(1, rows):
        total = total + lax.ppermute(sums, "batch", [(i, (i + k) % rows) for i in range(rows)])
    total = total * (1.0 / (rows * chunks * SPAN))
    carried, total = lax.optimization_barrier((carried, total))
    everyone = lax.all_to_all(jnp.broadcast_to(total[None], (chunks, 3 * M, SPAN)), "seq", 0, 0, tiled=True)

    mixed, grad_signal = pl.pallas_call(
        last_kernel,
        grid=(steps,),
        in_specs=[
            flat_block,
            flat_block,
            rate_block,
            pl.BlockSpec((wide // SLICE, 4 * M, SPAN), lambda i: (i, 0, 0)),
        ],
        out_specs=[seq_block, seq_block],
        out_shape=[jax.ShapeDtypeStruct(signal.shape, BF16)] * 2,
        compiler_params=params,
        cost_estimate=pl.CostEstimate(flops=both * 800, bytes_accessed=both * 6, transcendentals=both),
        name="add_carries",
    )(mixed_part, grad_part, rate_rows, carried)
    grad_residues, grad_rates = pl.pallas_call(
        functools.partial(gather_kernel, chunks),
        out_shape=[jax.ShapeDtypeStruct(residues.shape, F32), jax.ShapeDtypeStruct(log_rates.shape, F32)],
        name="unpack",
    )(everyone, log_rates)
    return mixed, grad_signal, grad_residues, grad_rates


def solution(mesh):
    placed = P("batch", "seq", None)
    return jax.shard_map(
        local,
        mesh=mesh,
        in_specs=(placed, placed, P(), P()),
        out_specs=(placed, placed, P(), P()),
        check_vma=False,
    )
```

```python
import functools

import jax
import jax.numpy as jnp
import numpy as np
from jax import lax
from jax.experimental import pallas as pl
from jax.experimental.pallas import tpu as pltpu
from jax.sharding import PartitionSpec as P

M = 8
GROUP = 16
SPAN = 128
SLICE = 256
GROUPS = SLICE // GROUP
WIDE = 2048
F32 = jnp.float32
BF16 = jnp.bfloat16


def split_np(values):
    high = values.astype(np.float32).astype(jnp.bfloat16)
    low = (values - high.astype(np.float64)).astype(np.float32).astype(jnp.bfloat16)
    return high, low


def transforms():
    time = np.arange(SPAN)
    angle = 2 * np.pi * np.outer(np.arange(SPAN) + 0.5, time) / (2 * SPAN)
    forward = np.concatenate([np.cos(angle), -np.sin(angle)], 0)
    inverse = np.concatenate([np.cos(angle.T), -np.sin(angle.T)], 1) / SPAN
    fh, fl = split_np(forward)
    ih, il = split_np(inverse)
    return np.concatenate([fh, fl], 1), np.concatenate([ih, il, ih], 1)


def split(values):
    high = values.astype(BF16)
    return high, (values - high.astype(F32)).astype(BF16)


def dot(a, b):
    return jnp.dot(a, b, preferred_element_type=F32)


def twice(values):
    return jnp.concatenate([values, values], 0)


def stacked(values):
    high, low = split(values)
    return jnp.concatenate([high, high, low], 0)


def lane_group(rows, lanes):
    return lax.broadcasted_iota(jnp.int32, (rows, lanes), 1) // GROUP


def spread(values):
    high = values.astype(BF16).astype(F32)
    low = values - high
    owner = lane_group(M, SLICE)

    def rows(part):
        return jnp.concatenate([jnp.where(owner == g, part, 0.0) for g in range(GROUPS)], 0).astype(BF16)

    top, bottom = rows(high), rows(low)
    return jnp.concatenate([top, top, bottom, bottom], 0)


def powers(rate_row, reverse):
    t = lax.broadcasted_iota(jnp.int32, (SPAN, SPAN), 0)
    t = (SPAN - 1 - t if reverse else t).astype(F32)
    high, low = split(jnp.exp(-rate_row[0:1, :] * t))
    return jnp.concatenate([high, low, high, low], 1)


def first_kernel(x_ref, g_ref, log_ref, res_ref, fwd_ref, inv_ref, send_ref):
    x, g = x_ref[0], g_ref[0]
    xx, gg = twice(x), twice(g)
    forward = fwd_ref[...]
    xf = dot(forward, xx)
    gf = dot(forward, gg)
    xr, xi, gr, gi = xf[:SPAN], xf[SPAN:], gf[:SPAN], gf[SPAN:]
    lags = dot(inv_ref[...], stacked(jnp.concatenate([gr * xr + gi * xi, gi * xr - gr * xi], 0)))
    lag_high, lag_low = split(lags)
    lag_high, lag_low = twice(lag_high), twice(lag_low)
    flip = jnp.where(lax.broadcasted_iota(jnp.int32, (SPAN, SPAN), 0) + lax.broadcasted_iota(jnp.int32, (SPAN, SPAN), 1) == SPAN - 1, 1.0, 0.0).astype(BF16)
    backward = twice(dot(flip, x).astype(BF16))
    lag = lax.broadcasted_iota(jnp.int32, (SPAN, SPAN), 1).astype(F32)
    half = SPAN // GROUP
    owner = lane_group(M, SPAN)
    row = lax.broadcasted_iota(jnp.int32, (SPAN, SPAN), 0) // GROUP
    col = lax.broadcasted_iota(jnp.int32, (SPAN, SPAN), 1)

    def pick(values, q):
        at = q * half * M
        chosen = values[at : at + M]
        for k in range(1, half):
            chosen = jnp.where(owner == k, values[at + k * M : at + (k + 1) * M], chosen)
        return chosen

    count = log_ref.shape[1] // GROUPS
    rate = jnp.exp(log_ref[...])
    weighted = ([], [])
    for s in range(count):
        at = s * GROUPS
        rates = jnp.concatenate([jnp.broadcast_to(rate[:, k : k + 1], (M, SPAN)) for k in range(at, at + GROUPS)], 0)
        early = jnp.exp(-rates * lag)
        for h in range(2):
            rows = slice(h * half * M, (h + 1) * half * M)
            cols = slice(s * SLICE + h * SPAN, s * SLICE + (h + 1) * SPAN)
            eh, el = split(jnp.concatenate([early[rows], lag[rows] * early[rows]], 0))
            found = dot(
                jnp.concatenate([eh, el], 1),
                jnp.concatenate([backward[:, cols], gg[:, cols], lag_high[:, cols], lag_low[:, cols]], 1),
            )
            ends, starts = found[:, :SPAN], found[:, SPAN : 2 * SPAN]
            sums = found[:, 2 * SPAN : 3 * SPAN] + found[:, 3 * SPAN :]
            for q, values in enumerate((pick(ends, 0), pick(starts, 0), pick(ends, 1), pick(starts, 1), pick(sums, 0))):
                at = (2 * q + h) * M
                send_ref[s, at : at + M, :] = values
            weighted[h].append(res_ref[:, cols] * pick(sums, 1))
    total = jnp.zeros((count * M, SPAN), F32)
    for h in range(2):
        place = jnp.where(row + h * half == col, 1.0, 0.0).astype(BF16)
        wh, wl = split(jnp.concatenate(weighted[h], 0))
        total = total + dot(jnp.concatenate([wh, wl], 1), twice(place))
    for s in range(count):
        send_ref[s, 10 * M : 11 * M, :] = total[s * M : (s + 1) * M]


def second_kernel(x_ref, g_ref, rate_ref, res_ref, fwd_ref, inv_ref, mixed_ref, grad_ref):
    forward = fwd_ref[...]
    taps = [
        dot(powers(rate_ref[s], False), spread(res_ref[:, s * SLICE : (s + 1) * SLICE]))
        for s in range(rate_ref.shape[0])
    ]
    high, low = split(jnp.concatenate(taps, 1))
    kf = dot(forward, twice(high)) + dot(fwd_ref[:, :SPAN], low)
    xf = dot(forward, twice(x_ref[0]))
    gf = dot(forward, twice(g_ref[0]))
    kr, ki, xr, xi, gr, gi = kf[:SPAN], kf[SPAN:], xf[:SPAN], xf[SPAN:], gf[:SPAN], gf[SPAN:]
    mixed_ref[...] = dot(inv_ref[...], stacked(jnp.concatenate([kr * xr - ki * xi, kr * xi + ki * xr], 0)))
    grad_ref[...] = dot(inv_ref[...], stacked(jnp.concatenate([kr * gr + ki * gi, kr * gi - ki * gr], 0)))


def carry_kernel(chunks, got_ref, rate_ref, res_ref, back_ref):
    for h in range(2):
        cols = slice(h * SPAN, (h + 1) * SPAN)
        rate = rate_ref[:, cols]
        across = jnp.exp(-rate * SPAN)
        handed = res_ref[:, cols] * jnp.exp(-rate)
        state = jnp.zeros((M, SPAN), F32)
        adjoint = state
        for k in range(chunks):
            last = chunks - 1 - k
            back_ref[k, h * M : (h + 1) * M, :] = handed * state
            back_ref[last, (2 + h) * M : (3 + h) * M, :] = handed * adjoint
            state = across * state + got_ref[k, h * M : (h + 1) * M, :]
            adjoint = across * adjoint + got_ref[last, (2 + h) * M : (3 + h) * M, :]


def sums_kernel(chunks, scale, index_ref, got_ref, rate_ref, res_ref, sums_ref):
    offset = lax.rem(index_ref[0], SPAN // GROUPS) * GROUPS
    rate_sum = jnp.zeros((M, SPAN), F32)
    for k in range(chunks):
        rate_sum = rate_sum + got_ref[k, 10 * M : 11 * M, :]
    rate_sum = pltpu.roll(rate_sum, offset, 1)
    row = lax.broadcasted_iota(jnp.int32, (SPAN, SPAN), 0) // GROUP
    col = lax.broadcasted_iota(jnp.int32, (SPAN, SPAN), 1)
    for h in range(2):
        cols = slice(h * SPAN, (h + 1) * SPAN)
        rate, res = rate_ref[:, cols], res_ref[:, cols]
        pole = jnp.exp(-rate)
        across = jnp.exp(-rate * SPAN)

        def part(k, q):
            at = (2 * q + h) * M
            return got_ref[k, at : at + M, :]

        zero = jnp.zeros((M, SPAN), F32)
        state, moment, res_part, res_carry, rate_carry = zero, zero, zero, zero, zero
        for k in range(chunks):
            start = part(k, 1)
            res_part = res_part + part(k, 4)
            res_carry = res_carry + state * start
            rate_carry = rate_carry + state * (part(k, 3) + start) + moment * start
            moment = across * (moment + SPAN * state) + part(k, 2)
            state = across * state + part(k, 0)
        sums_ref[h * M : (h + 1) * M, :] = scale * (res_part + pole * res_carry)
        place = jnp.where(row + (h * (SPAN // GROUP) + offset) == col, 1.0, 0.0).astype(BF16)
        wh, wl = split(res * pole * rate_carry)
        rate_sum = rate_sum + dot(wh, place) + dot(wl, place)
    sums_ref[2 * M : 3 * M, :] = scale * rate_sum


def last_kernel(mixed_ref, grad_ref, rate_ref, got_ref, mixed_out, grad_out):
    for s in range(rate_ref.shape[0]):
        cols = slice(s * SLICE, (s + 1) * SLICE)
        state = jnp.concatenate([got_ref[s, 0:M, :], got_ref[s, M : 2 * M, :]], 1)
        adjoint = jnp.concatenate([got_ref[s, 2 * M : 3 * M, :], got_ref[s, 3 * M : 4 * M, :]], 1)
        more = dot(powers(rate_ref[s], False), spread(state))
        mixed_out[0, :, cols] = (mixed_ref[:, cols] + more).astype(BF16)
        more = dot(powers(rate_ref[s], True), spread(adjoint))
        grad_out[0, :, cols] = (grad_ref[:, cols] + more).astype(BF16)


def gather_kernel(chunks, all_ref, log_ref, res_out, rate_out):
    for k in range(chunks):
        for h in range(2):
            res_out[:, k * SLICE + h * SPAN : k * SLICE + (h + 1) * SPAN] = all_ref[k, h * M : (h + 1) * M, :]
    width = min(SPAN, chunks * GROUPS)
    per = width // GROUPS
    for j in range(chunks // per):
        parts = all_ref[j * per, 2 * M : 3 * M, :]
        for k in range(j * per + 1, (j + 1) * per):
            parts = parts + all_ref[k, 2 * M : 3 * M, :]
        cols = slice(j * width, (j + 1) * width)
        rate_out[:, cols] = -jnp.exp(log_ref[:, cols]) * parts[:, :width]


def local(signal, out_grad, residues, log_rates):
    channels = signal.shape[2]
    chunks, rows = lax.axis_size("seq"), lax.axis_size("batch")
    index = lax.axis_index("seq")
    wide = min(WIDE, channels)
    steps = channels // wide
    fwd, inv = (jnp.asarray(v) for v in transforms())
    log_block = pl.BlockSpec((M, wide // GROUP), lambda i: (0, i))
    seq_block = pl.BlockSpec((1, SPAN, wide), lambda i: (0, 0, i))
    flat_block = pl.BlockSpec((SPAN, wide), lambda i: (0, i))
    rate_block = pl.BlockSpec((wide // SLICE, M, SPAN), lambda i: (i, 0, 0))
    res_block = pl.BlockSpec((M, wide), lambda i: (0, i))
    whole = lambda a: pl.BlockSpec(a.shape, lambda i: (0,) * a.ndim)
    params = pltpu.CompilerParams(vmem_limit_bytes=58 * 2**20)
    both = 2 * SPAN * channels

    send = pl.pallas_call(
        first_kernel,
        grid=(steps,),
        in_specs=[seq_block, seq_block, log_block, res_block, whole(fwd), whole(inv)],
        out_specs=pl.BlockSpec((wide // SLICE, 11 * M, SPAN), lambda i: (i, 0, 0)),
        out_shape=jax.ShapeDtypeStruct((chunks, 11 * M, SPAN), F32),
        compiler_params=params,
        name="ends_and_lags",
    )(signal, out_grad, log_rates, residues, fwd, inv)
    send, later_rates, later_res = lax.optimization_barrier((send, log_rates, residues))
    decay_rate = jnp.exp(later_rates)
    rate_rows = jnp.broadcast_to(decay_rate.T.reshape(chunks, 1, SPAN), (chunks, M, SPAN))
    own_rate = jnp.repeat(lax.dynamic_slice_in_dim(decay_rate, index * GROUPS, GROUPS, 1), GROUP, axis=1)
    own_res = lax.dynamic_slice_in_dim(later_res, index * SLICE, SLICE, 1)

    got = lax.all_to_all(send, "seq", 0, 0, tiled=True)

    mixed_part, grad_part = pl.pallas_call(
        second_kernel,
        grid=(steps,),
        in_specs=[seq_block, seq_block, rate_block, res_block, whole(fwd), whole(inv)],
        out_specs=[flat_block, flat_block],
        out_shape=[jax.ShapeDtypeStruct((SPAN, channels), F32)] * 2,
        compiler_params=params,
        cost_estimate=pl.CostEstimate(flops=both * 3000, bytes_accessed=both * 8, transcendentals=both),
        name="local_convolutions",
    )(signal, out_grad, rate_rows, residues, fwd, inv)

    got, mixed_part, grad_part = lax.optimization_barrier((got, mixed_part, grad_part))
    vmem = pl.BlockSpec(memory_space=pltpu.VMEM)
    back = pl.pallas_call(
        functools.partial(carry_kernel, chunks),
        out_shape=jax.ShapeDtypeStruct((chunks, 4 * M, SPAN), F32),
        compiler_params=pltpu.CompilerParams(vmem_limit_bytes=8 * 2**20),
        name="carries",
    )(got, own_rate, own_res)
    back, got = lax.optimization_barrier((back, got))
    carried = lax.all_to_all(back, "seq", 0, 0, tiled=True)
    sums = pl.pallas_call(
        functools.partial(sums_kernel, chunks, 1.0 / (rows * chunks * SPAN)),
        out_shape=jax.ShapeDtypeStruct((3 * M, SPAN), F32),
        in_specs=[pl.BlockSpec(memory_space=pltpu.SMEM), vmem, vmem, vmem],
        compiler_params=pltpu.CompilerParams(vmem_limit_bytes=8 * 2**20),
        name="gradient_sums",
    )(index.astype(jnp.int32)[None], got, own_rate, own_res)
    total = sums
    for k in range(1, rows):
        total = total + lax.ppermute(sums, "batch", [(i, (i + k) % rows) for i in range(rows)])
    total = jnp.broadcast_to(total[None], (chunks, 3 * M, SPAN))
    carried, total = lax.optimization_barrier((carried, total))
    everyone = lax.all_to_all(total, "seq", 0, 0, tiled=True)

    mixed, grad_signal = pl.pallas_call(
        last_kernel,
        grid=(steps,),
        in_specs=[
            flat_block,
            flat_block,
            rate_block,
            pl.BlockSpec((wide // SLICE, 4 * M, SPAN), lambda i: (i, 0, 0)),
        ],
        out_specs=[seq_block, seq_block],
        out_shape=[jax.ShapeDtypeStruct(signal.shape, BF16)] * 2,
        compiler_params=params,
        cost_estimate=pl.CostEstimate(flops=both * 800, bytes_accessed=both * 6, transcendentals=both),
        name="add_carries",
    )(mixed_part, grad_part, rate_rows, carried)
    grad_residues, grad_rates = pl.pallas_call(
        functools.partial(gather_kernel, chunks),
        out_shape=[jax.ShapeDtypeStruct(residues.shape, F32), jax.ShapeDtypeStruct(log_rates.shape, F32)],
        compiler_params=pltpu.CompilerParams(vmem_limit_bytes=8 * 2**20),
        name="unpack",
    )(everyone, log_rates)
    return mixed, grad_signal, grad_residues, grad_rates


def solution(mesh):
    placed = P("batch", "seq", None)
    return jax.shard_map(
        local,
        mesh=mesh,
        in_specs=(placed, placed, P(), P()),
        out_specs=(placed, placed, P(), P()),
        check_vma=False,
    )
```

```python
import functools

import jax
import jax.numpy as jnp
import numpy as np
from jax import lax
from jax.experimental import pallas as pl
from jax.experimental.pallas import tpu as pltpu
from jax.sharding import PartitionSpec as P

M = 8
GROUP = 16
SPAN = 128
SLICE = 256
GROUPS = SLICE // GROUP
WIDE = 2048
F32 = jnp.float32
BF16 = jnp.bfloat16


def split_np(values):
    high = values.astype(np.float32).astype(jnp.bfloat16)
    low = (values - high.astype(np.float64)).astype(np.float32).astype(jnp.bfloat16)
    return high, low


def transforms():
    time = np.arange(SPAN)
    angle = 2 * np.pi * np.outer(np.arange(SPAN) + 0.5, time) / (2 * SPAN)
    forward = np.concatenate([np.cos(angle), -np.sin(angle)], 0)
    inverse = np.concatenate([np.cos(angle.T), -np.sin(angle.T)], 1) / SPAN
    fh, fl = split_np(forward)
    ih, il = split_np(inverse)
    return np.concatenate([fh, fl], 1), np.concatenate([ih, il, ih], 1)


def split(values):
    high = values.astype(BF16)
    return high, (values - high.astype(F32)).astype(BF16)


def dot(a, b):
    return jnp.dot(a, b, preferred_element_type=F32)


def twice(values):
    return jnp.concatenate([values, values], 0)


def stacked(values):
    high, low = split(values)
    return jnp.concatenate([high, high, low], 0)


def lane_group(rows, lanes):
    return lax.broadcasted_iota(jnp.int32, (rows, lanes), 1) // GROUP


def spread(values):
    high = values.astype(BF16).astype(F32)
    low = values - high
    owner = lane_group(M, SLICE)

    def rows(part):
        return jnp.concatenate([jnp.where(owner == g, part, 0.0) for g in range(GROUPS)], 0).astype(BF16)

    top, bottom = rows(high), rows(low)
    return jnp.concatenate([top, top, bottom, bottom], 0)


def powers(rate_row, reverse):
    t = lax.broadcasted_iota(jnp.int32, (SPAN, SPAN), 0)
    t = (SPAN - 1 - t if reverse else t).astype(F32)
    high, low = split(jnp.exp(-rate_row[0:1, :] * t))
    return jnp.concatenate([high, low, high, low], 1)


def first_kernel(half_ref, x_ref, g_ref, log_ref, res_ref, fwd_ref, inv_ref, send_ref):
    x, g = x_ref[0], g_ref[0]
    xx, gg = twice(x), twice(g)
    forward = fwd_ref[...]
    xf = dot(forward, xx)
    gf = dot(forward, gg)
    xr, xi, gr, gi = xf[:SPAN], xf[SPAN:], gf[:SPAN], gf[SPAN:]
    lags = dot(inv_ref[...], stacked(jnp.concatenate([gr * xr + gi * xi, gi * xr - gr * xi], 0)))
    lag_high, lag_low = split(lags)
    lag_high, lag_low = twice(lag_high), twice(lag_low)
    flip = jnp.where(lax.broadcasted_iota(jnp.int32, (SPAN, SPAN), 0) + lax.broadcasted_iota(jnp.int32, (SPAN, SPAN), 1) == SPAN - 1, 1.0, 0.0).astype(BF16)
    backward = twice(dot(flip, x).astype(BF16))
    lag = lax.broadcasted_iota(jnp.int32, (SPAN, SPAN), 1).astype(F32)
    half = SPAN // GROUP
    owner = lane_group(M, SPAN)
    row = lax.broadcasted_iota(jnp.int32, (SPAN, SPAN), 0) // GROUP
    col = lax.broadcasted_iota(jnp.int32, (SPAN, SPAN), 1)

    def pick(values, q):
        at = q * half * M
        chosen = values[at : at + M]
        for k in range(1, half):
            chosen = jnp.where(owner == k, values[at + k * M : at + (k + 1) * M], chosen)
        return chosen

    count = log_ref.shape[1] // GROUPS
    rate = jnp.exp(log_ref[...])
    weighted = ([], [])
    for s in range(count):
        at = s * GROUPS
        rates = jnp.concatenate([jnp.broadcast_to(rate[:, k : k + 1], (M, SPAN)) for k in range(at, at + GROUPS)], 0)
        early = jnp.exp(-rates * lag)
        for h in range(2):
            rows = slice(h * half * M, (h + 1) * half * M)
            cols = slice(s * SLICE + h * SPAN, s * SLICE + (h + 1) * SPAN)
            eh, el = split(jnp.concatenate([early[rows], lag[rows] * early[rows]], 0))
            found = dot(
                jnp.concatenate([eh, el], 1),
                jnp.concatenate([backward[:, cols], gg[:, cols], lag_high[:, cols], lag_low[:, cols]], 1),
            )
            ends, starts = found[:, :SPAN], found[:, SPAN : 2 * SPAN]
            sums = found[:, 2 * SPAN : 3 * SPAN] + found[:, 3 * SPAN :]
            for q, values in enumerate((pick(ends, 0), pick(starts, 0), pick(ends, 1), pick(starts, 1), pick(sums, 0))):
                at = (2 * q + h) * M
                send_ref[s, at : at + M, :] = values
            weighted[h].append(res_ref[:, cols] * pick(sums, 1))
    total = jnp.zeros((count * M, SPAN), F32)
    for h in range(2):
        place = jnp.where(row + h * half == col, 1.0, 0.0).astype(BF16)
        wh, wl = split(jnp.concatenate(weighted[h], 0))
        total = total + dot(jnp.concatenate([wh, wl], 1), twice(place))
    for s in range(count):
        send_ref[s, 10 * M : 11 * M, :] = total[s * M : (s + 1) * M]


def second_kernel(x_ref, g_ref, rate_ref, res_ref, fwd_ref, inv_ref, *rest):
    mixed_ref, grad_ref = rest[-2:]
    forward = fwd_ref[...]
    taps = [
        dot(powers(rate_ref[s], False), spread(res_ref[:, s * SLICE : (s + 1) * SLICE]))
        for s in range(rate_ref.shape[0])
    ]
    high, low = split(jnp.concatenate(taps, 1))
    kf = dot(forward, twice(high)) + dot(fwd_ref[:, :SPAN], low)
    xf = dot(forward, twice(x_ref[0]))
    gf = dot(forward, twice(g_ref[0]))
    kr, ki, xr, xi, gr, gi = kf[:SPAN], kf[SPAN:], xf[:SPAN], xf[SPAN:], gf[:SPAN], gf[SPAN:]
    mixed_ref[...] = dot(inv_ref[...], stacked(jnp.concatenate([kr * xr - ki * xi, kr * xi + ki * xr], 0)))
    grad_ref[...] = dot(inv_ref[...], stacked(jnp.concatenate([kr * gr + ki * gi, kr * gi - ki * gr], 0)))


def per_channel(values, at):
    owner = lane_group(M, SPAN)
    chosen = jnp.broadcast_to(values[:, at : at + 1], (M, SPAN))
    for k in range(1, SPAN // GROUP):
        chosen = jnp.where(owner == k, values[:, at + k : at + k + 1], chosen)
    return chosen


def placed(parts, h, offset):
    row = lax.broadcasted_iota(jnp.int32, (SPAN, SPAN), 0) // GROUP
    col = lax.broadcasted_iota(jnp.int32, (SPAN, SPAN), 1)
    place = jnp.where(row + (h * (SPAN // GROUP) + offset) == col, 1.0, 0.0).astype(BF16)
    high, low = split(parts)
    return dot(jnp.concatenate([high, low], 1), twice(place))


def pair_kernel(core_ref, kept_ref, arrived_ref, log_ref, res_ref, pair_ref):
    even = core_ref[0] == 0
    count = kept_ref.shape[0]
    rate = jnp.exp(log_ref[...])
    pole, across = jnp.exp(-rate), jnp.exp(-rate * SPAN)
    weighted = ([], [])
    for s in range(count):
        for h in range(2):

            def both(q):
                rows = slice((2 * q + h) * M, (2 * q + h + 1) * M)
                kept, arrived = kept_ref[s, rows, :], arrived_ref[s, rows, :]
                return jnp.where(even, kept, arrived), jnp.where(even, arrived, kept)

            def put(q, values):
                pair_ref[s, (2 * q + h) * M : (2 * q + h + 1) * M, :] = values

            lanes = s * GROUPS + h * (SPAN // GROUP)
            p, far = per_channel(pole, lanes), per_channel(across, lanes)
            (s1, s2), (t1, t2), (u1, u2), (w1, w2), (r1, r2) = (both(q) for q in range(5))
            put(0, far * s1 + s2)
            put(1, t1 + far * t2)
            put(2, far * (u1 + SPAN * s1) + u2)
            put(3, w1 + far * (w2 + SPAN * t2))
            put(4, r1 + r2 + p * s1 * t2)
            cols = slice(s * SLICE + h * SPAN, s * SLICE + (h + 1) * SPAN)
            weighted[h].append(res_ref[:, cols] * p * (s1 * (w2 + t2) + u1 * t2))
    total = placed(jnp.concatenate(weighted[0], 0), 0, 0) + placed(jnp.concatenate(weighted[1], 0), 1, 0)
    for s in range(count):
        rows = slice(10 * M, 11 * M)
        pair_ref[s, rows, :] = kept_ref[s, rows, :] + arrived_ref[s, rows, :] + total[s * M : (s + 1) * M]


def carry_kernel(pairs, got_ref, rate_ref, res_ref, back_ref):
    for h in range(2):
        cols = slice(h * SPAN, (h + 1) * SPAN)
        rate = rate_ref[:, cols]
        across = jnp.exp(-rate * (2 * SPAN))
        handed = res_ref[:, cols] * jnp.exp(-rate)
        state = jnp.zeros((M, SPAN), F32)
        adjoint = state
        for k in range(pairs):
            last = pairs - 1 - k
            back_ref[k, h * M : (h + 1) * M, :] = handed * state
            back_ref[last, (2 + h) * M : (3 + h) * M, :] = handed * adjoint
            state = across * state + got_ref[k, h * M : (h + 1) * M, :]
            adjoint = across * adjoint + got_ref[last, (2 + h) * M : (3 + h) * M, :]


def sums_kernel(pairs, scale, index_ref, got_ref, rate_ref, res_ref, sums_ref):
    offset = lax.rem(index_ref[0], SPAN // GROUPS) * GROUPS
    rate_sum = jnp.zeros((M, SPAN), F32)
    for k in range(pairs):
        rate_sum = rate_sum + got_ref[k, 10 * M : 11 * M, :]
    rate_sum = pltpu.roll(rate_sum, offset, 1)
    for h in range(2):
        cols = slice(h * SPAN, (h + 1) * SPAN)
        rate, res = rate_ref[:, cols], res_ref[:, cols]
        pole = jnp.exp(-rate)
        across = jnp.exp(-rate * (2 * SPAN))

        def part(k, q):
            at = (2 * q + h) * M
            return got_ref[k, at : at + M, :]

        zero = jnp.zeros((M, SPAN), F32)
        state, moment, res_part, res_carry, rate_carry = zero, zero, zero, zero, zero
        for k in range(pairs):
            start = part(k, 1)
            res_part = res_part + part(k, 4)
            res_carry = res_carry + state * start
            rate_carry = rate_carry + state * (part(k, 3) + start) + moment * start
            moment = across * (moment + 2 * SPAN * state) + part(k, 2)
            state = across * state + part(k, 0)
        sums_ref[h * M : (h + 1) * M, :] = scale * (res_part + pole * res_carry)
        rate_sum = rate_sum + placed(res * pole * rate_carry, h, offset)
    sums_ref[2 * M : 3 * M, :] = scale * rate_sum


def last_kernel(
    core_ref, mixed_ref, grad_ref, rate_ref, log_ref, res_ref, mine_ref, other_ref, near_ref, far_ref, mixed_out, grad_out
):
    core = core_ref[0]
    even = core == 0
    here = pl.program_id(0) // (pl.num_programs(0) // 2) == core
    rate = jnp.exp(log_ref[...])
    pole, across = jnp.exp(-rate), jnp.exp(-rate * SPAN)
    for s in range(rate_ref.shape[0]):
        cols = slice(s * SLICE, (s + 1) * SLICE)
        states, adjoints = [], []
        for h in range(2):

            def chosen(a_ref, b_ref, q):
                rows = slice((2 * q + h) * M, (2 * q + h + 1) * M)
                return jnp.where(here, a_ref[s, rows, :], b_ref[s, rows, :])

            lanes = s * GROUPS + h * (SPAN // GROUP)
            p, far = per_channel(pole, lanes), per_channel(across, lanes)
            handed = res_ref[:, s * SLICE + h * SPAN : s * SLICE + (h + 1) * SPAN] * p
            state, adjoint = chosen(mine_ref, other_ref, 0), chosen(mine_ref, other_ref, 1)
            end, start = chosen(near_ref, far_ref, 0), chosen(near_ref, far_ref, 1)
            states.append(jnp.where(even, state, far * state + handed * end))
            adjoints.append(jnp.where(even, far * adjoint + handed * start, adjoint))
        more = dot(powers(rate_ref[s], False), spread(jnp.concatenate(states, 1)))
        mixed_out[0, :, cols] = (mixed_ref[:, cols] + more).astype(BF16)
        more = dot(powers(rate_ref[s], True), spread(jnp.concatenate(adjoints, 1)))
        grad_out[0, :, cols] = (grad_ref[:, cols] + more).astype(BF16)


def gather_kernel(pairs, core_ref, mine_ref, other_ref, log_ref, res_out, rate_out):
    chunks = 2 * pairs

    def part(k, rows):
        return jnp.where(core_ref[0] == k // pairs, mine_ref[k % pairs, rows, :], other_ref[k % pairs, rows, :])

    for k in range(chunks):
        for h in range(2):
            res_out[:, k * SLICE + h * SPAN : k * SLICE + (h + 1) * SPAN] = part(k, slice(h * M, (h + 1) * M))
    width = min(SPAN, chunks * GROUPS)
    per = width // GROUPS
    rows = slice(2 * M, 3 * M)
    for j in range(chunks // per):
        parts = part(j * per, rows)
        for k in range(j * per + 1, (j + 1) * per):
            parts = parts + part(k, rows)
        cols = slice(j * width, (j + 1) * width)
        rate_out[:, cols] = -jnp.exp(log_ref[:, cols]) * parts[:, :width]


def local(signal, out_grad, residues, log_rates):
    channels = signal.shape[2]
    chunks, rows = lax.axis_size("seq"), lax.axis_size("batch")
    index = lax.axis_index("seq").astype(jnp.int32)
    pairs = chunks // 2
    core = lax.rem(index, 2)
    own = core * pairs + index // 2
    swap = [(i, i ^ 1) for i in range(chunks)]
    same_core = [[2 * j + c for j in range(pairs)] for c in range(2)]
    wide = min(WIDE, channels // 2)
    steps = channels // wide
    part = steps // 2
    block = wide // SLICE
    fwd, inv = (jnp.asarray(v) for v in transforms())
    params = pltpu.CompilerParams(vmem_limit_bytes=58 * 2**20)
    little = pltpu.CompilerParams(vmem_limit_bytes=8 * 2**20)
    vmem, smem = pl.BlockSpec(memory_space=pltpu.VMEM), pl.BlockSpec(memory_space=pltpu.SMEM)
    states_shape = jax.ShapeDtypeStruct((pairs, 11 * M, SPAN), F32)
    core_scalar = core[None]

    def whole(a):
        return pl.BlockSpec(a.shape, lambda i, *_: (0,) * a.ndim)

    def exchange(values):
        return lax.all_to_all(values, "seq", 0, 0, axis_index_groups=same_core, tiled=True)

    def other_core(values):
        return lax.ppermute(values, "seq", swap)

    def ends_and_lags(half, x, g):
        return pl.pallas_call(
            first_kernel,
            grid_spec=pltpu.PrefetchScalarGridSpec(
                num_scalar_prefetch=1,
                grid=(part,),
                in_specs=[
                    pl.BlockSpec((1, SPAN, wide), lambda i, at: (0, 0, at[0] * part + i)),
                    pl.BlockSpec((1, SPAN, wide), lambda i, at: (0, 0, at[0] * part + i)),
                    pl.BlockSpec((M, wide // GROUP), lambda i, at: (0, at[0] * part + i)),
                    pl.BlockSpec((M, wide), lambda i, at: (0, at[0] * part + i)),
                    whole(fwd),
                    whole(inv),
                ],
                out_specs=pl.BlockSpec((block, 11 * M, SPAN), lambda i, at: (i, 0, 0)),
            ),
            out_shape=states_shape,
            compiler_params=params,
            name="ends_and_lags",
        )(half, x, g, log_rates, residues, fwd, inv)

    away = ends_and_lags(1 - core_scalar, signal, out_grad)
    away, x2, g2 = lax.optimization_barrier((away, signal, out_grad))
    arrived = other_core(away)
    kept = ends_and_lags(core_scalar, x2, g2)
    state_block = pl.BlockSpec((block, 11 * M, SPAN), lambda i, at: (i, 0, 0))
    pair = pl.pallas_call(
        pair_kernel,
        grid_spec=pltpu.PrefetchScalarGridSpec(
            num_scalar_prefetch=1,
            grid=(part,),
            in_specs=[
                state_block,
                state_block,
                pl.BlockSpec((M, wide // GROUP), lambda i, at: (0, at[0] * part + i)),
                pl.BlockSpec((M, wide), lambda i, at: (0, at[0] * part + i)),
            ],
            out_specs=state_block,
        ),
        out_shape=states_shape,
        compiler_params=little,
        name="join_pair",
    )(core_scalar, kept, arrived, log_rates, residues)
    pair, later_rates, later_res, kept = lax.optimization_barrier((pair, log_rates, residues, kept))
    got = exchange(pair)
    arrived_far = other_core(kept)

    decay_rate = jnp.exp(later_rates)
    rate_rows = jnp.broadcast_to(decay_rate.T.reshape(chunks, 1, SPAN), (chunks, M, SPAN))
    own_rate = jnp.repeat(lax.dynamic_slice_in_dim(decay_rate, own * GROUPS, GROUPS, 1), GROUP, axis=1)
    own_res = lax.dynamic_slice_in_dim(later_res, own * SLICE, SLICE, 1)

    work = SPAN * channels

    def convolutions(half, x, g, *earlier):
        at = half * part
        kernel_blocks = [
            pl.BlockSpec((1, SPAN, wide), lambda i: (0, 0, at + i)),
            pl.BlockSpec((1, SPAN, wide), lambda i: (0, 0, at + i)),
            pl.BlockSpec((block, M, SPAN), lambda i: (at + i, 0, 0)),
            pl.BlockSpec((M, wide), lambda i: (0, at + i)),
            whole(fwd),
            whole(inv),
        ]
        return pl.pallas_call(
            second_kernel,
            grid=(part,),
            in_specs=kernel_blocks + [pl.BlockSpec(memory_space=pl.ANY)] * len(earlier),
            out_specs=[pl.BlockSpec((SPAN, wide), lambda i: (0, at + i))] * 2,
            out_shape=[jax.ShapeDtypeStruct((SPAN, channels), F32)] * 2,
            input_output_aliases={6: 0, 7: 1} if earlier else {},
            compiler_params=params,
            cost_estimate=pl.CostEstimate(flops=work * 300, bytes_accessed=work * 2, transcendentals=0),
            name="local_convolutions",
        )(x, g, rate_rows, residues, fwd, inv, *earlier)

    mixed_part, grad_part = convolutions(0, signal, out_grad)
    got, mixed_part, grad_part, arrived_far = lax.optimization_barrier((got, mixed_part, grad_part, arrived_far))
    back = pl.pallas_call(
        functools.partial(carry_kernel, pairs),
        out_shape=jax.ShapeDtypeStruct((pairs, 4 * M, SPAN), F32),
        compiler_params=little,
        name="carries",
    )(got, own_rate, own_res)
    back, got, x3, g3 = lax.optimization_barrier((back, got, signal, out_grad))
    carried = exchange(back)
    sums = pl.pallas_call(
        functools.partial(sums_kernel, pairs, 1.0 / (rows * chunks * SPAN)),
        out_shape=jax.ShapeDtypeStruct((3 * M, SPAN), F32),
        in_specs=[smem, vmem, vmem, vmem],
        compiler_params=little,
        cost_estimate=pl.CostEstimate(flops=10**10, bytes_accessed=10**7, transcendentals=0),
        name="gradient_sums",
    )(own[None], got, own_rate, own_res)
    arriving = [lax.ppermute(sums, "batch", [(i, (i + k) % rows) for i in range(rows)]) for k in range(1, rows)]
    mixed_part, grad_part = convolutions(1, x3, g3, mixed_part, grad_part)

    def total_kernel(*refs):
        total = refs[0][...]
        for ref in refs[1:-1]:
            total = total + ref[...]
        for k in range(pairs):
            refs[-1][k] = total

    total = pl.pallas_call(
        total_kernel,
        out_shape=jax.ShapeDtypeStruct((pairs, 3 * M, SPAN), F32),
        compiler_params=little,
        name="total",
    )(sums, *arriving)
    carried, total, mixed_part, grad_part = lax.optimization_barrier((carried, total, mixed_part, grad_part))
    carried_far = other_core(carried)
    everyone = exchange(total)

    flat_block = pl.BlockSpec((SPAN, wide), lambda i, at: (0, i))
    seq_block = pl.BlockSpec((1, SPAN, wide), lambda i, at: (0, 0, i))
    half_block = pl.BlockSpec((block, 4 * M, SPAN), lambda i, at: (lax.rem(i, part), 0, 0))
    mixed, grad_signal = pl.pallas_call(
        last_kernel,
        grid_spec=pltpu.PrefetchScalarGridSpec(
            num_scalar_prefetch=1,
            grid=(steps,),
            in_specs=[
                flat_block,
                flat_block,
                pl.BlockSpec((block, M, SPAN), lambda i, at: (i, 0, 0)),
                pl.BlockSpec((M, wide // GROUP), lambda i, at: (0, i)),
                pl.BlockSpec((M, wide), lambda i, at: (0, i)),
                half_block,
                half_block,
                half_block,
                half_block,
            ],
            out_specs=[seq_block, seq_block],
        ),
        out_shape=[jax.ShapeDtypeStruct(signal.shape, BF16)] * 2,
        compiler_params=params,
        cost_estimate=pl.CostEstimate(flops=work * 1600, bytes_accessed=work * 12, transcendentals=work),
        name="add_carries",
    )(core_scalar, mixed_part, grad_part, rate_rows, log_rates, residues, carried, carried_far, arrived, arrived_far)
    everyone, mixed, grad_signal = lax.optimization_barrier((everyone, mixed, grad_signal))
    grad_residues, grad_rates = pl.pallas_call(
        functools.partial(gather_kernel, pairs),
        out_shape=[jax.ShapeDtypeStruct(residues.shape, F32), jax.ShapeDtypeStruct(log_rates.shape, F32)],
        in_specs=[smem, vmem, vmem, vmem],
        compiler_params=little,
        name="unpack",
    )(core_scalar, everyone, other_core(everyone), log_rates)
    return mixed, grad_signal, grad_residues, grad_rates


def solution(mesh):
    sharded = P("batch", "seq", None)
    return jax.shard_map(
        local,
        mesh=mesh,
        in_specs=(sharded, sharded, P(), P()),
        out_specs=(sharded, sharded, P(), P()),
        check_vma=False,
    )
```

```python
import functools

import jax
import jax.numpy as jnp
import numpy as np
from jax import lax
from jax.experimental import pallas as pl
from jax.experimental.pallas import tpu as pltpu
from jax.sharding import PartitionSpec as P

M = 8
GROUP = 16
SPAN = 128
SLICE = 256
GROUPS = SLICE // GROUP
WIDE = 2048
F32 = jnp.float32
BF16 = jnp.bfloat16


def split_np(values):
    high = values.astype(np.float32).astype(jnp.bfloat16)
    low = (values - high.astype(np.float64)).astype(np.float32).astype(jnp.bfloat16)
    return high, low


def transforms():
    time = np.arange(SPAN)
    angle = 2 * np.pi * np.outer(np.arange(SPAN) + 0.5, time) / (2 * SPAN)
    forward = np.concatenate([np.cos(angle), -np.sin(angle)], 0)
    inverse = np.concatenate([np.cos(angle.T), -np.sin(angle.T)], 1) / SPAN
    fh, fl = split_np(forward)
    ih, il = split_np(inverse)
    return np.concatenate([fh, fl], 1), np.concatenate([ih, il, ih], 1)


def split(values):
    high = values.astype(BF16)
    return high, (values - high.astype(F32)).astype(BF16)


def dot(a, b):
    return jnp.dot(a, b, preferred_element_type=F32)


def twice(values):
    return jnp.concatenate([values, values], 0)


def stacked(values):
    high, low = split(values)
    return jnp.concatenate([high, high, low], 0)


def lane_group(rows, lanes):
    return lax.broadcasted_iota(jnp.int32, (rows, lanes), 1) // GROUP


def spread(values):
    high = values.astype(BF16).astype(F32)
    low = values - high
    owner = lane_group(M, SLICE)

    def rows(part):
        return jnp.concatenate([jnp.where(owner == g, part, 0.0) for g in range(GROUPS)], 0).astype(BF16)

    top, bottom = rows(high), rows(low)
    return jnp.concatenate([top, top, bottom, bottom], 0)


def powers(rate_row, reverse):
    t = lax.broadcasted_iota(jnp.int32, (SPAN, SPAN), 0)
    t = (SPAN - 1 - t if reverse else t).astype(F32)
    high, low = split(jnp.exp(-rate_row[0:1, :] * t))
    return jnp.concatenate([high, low, high, low], 1)


def first_kernel(half_ref, x_ref, g_ref, log_ref, res_ref, fwd_ref, inv_ref, send_ref, rate_out):
    x, g = x_ref[0], g_ref[0]
    xx, gg = twice(x), twice(g)
    forward = fwd_ref[...]
    xf = dot(forward, xx)
    gf = dot(forward, gg)
    xr, xi, gr, gi = xf[:SPAN], xf[SPAN:], gf[:SPAN], gf[SPAN:]
    lags = dot(inv_ref[...], stacked(jnp.concatenate([gr * xr + gi * xi, gi * xr - gr * xi], 0)))
    lag_high, lag_low = split(lags)
    lag_high, lag_low = twice(lag_high), twice(lag_low)
    flip = jnp.where(lax.broadcasted_iota(jnp.int32, (SPAN, SPAN), 0) + lax.broadcasted_iota(jnp.int32, (SPAN, SPAN), 1) == SPAN - 1, 1.0, 0.0).astype(BF16)
    backward = twice(dot(flip, x).astype(BF16))
    lag = lax.broadcasted_iota(jnp.int32, (SPAN, SPAN), 1).astype(F32)
    half = SPAN // GROUP
    owner = lane_group(M, SPAN)
    row = lax.broadcasted_iota(jnp.int32, (SPAN, SPAN), 0) // GROUP
    col = lax.broadcasted_iota(jnp.int32, (SPAN, SPAN), 1)

    def pick(values, q):
        at = q * half * M
        chosen = values[at : at + M]
        for k in range(1, half):
            chosen = jnp.where(owner == k, values[at + k * M : at + (k + 1) * M], chosen)
        return chosen

    count = log_ref.shape[1] // GROUPS
    rate = jnp.exp(log_ref[...])
    weighted = ([], [])
    for s in range(count):
        at = s * GROUPS
        rates = jnp.concatenate([jnp.broadcast_to(rate[:, k : k + 1], (M, SPAN)) for k in range(at, at + GROUPS)], 0)
        early = jnp.exp(-rates * lag)
        for h in range(2):
            rate_out[s, h * M : (h + 1) * M, :] = pick(rates[h * half * M : (h + 1) * half * M], 0)
        for h in range(2):
            rows = slice(h * half * M, (h + 1) * half * M)
            cols = slice(s * SLICE + h * SPAN, s * SLICE + (h + 1) * SPAN)
            eh, el = split(jnp.concatenate([early[rows], lag[rows] * early[rows]], 0))
            found = dot(
                jnp.concatenate([eh, el], 1),
                jnp.concatenate([backward[:, cols], gg[:, cols], lag_high[:, cols], lag_low[:, cols]], 1),
            )
            ends, starts = found[:, :SPAN], found[:, SPAN : 2 * SPAN]
            sums = found[:, 2 * SPAN : 3 * SPAN] + found[:, 3 * SPAN :]
            for q, values in enumerate((pick(ends, 0), pick(starts, 0), pick(ends, 1), pick(starts, 1), pick(sums, 0))):
                at = (2 * q + h) * M
                send_ref[s, at : at + M, :] = values
            weighted[h].append(res_ref[:, cols] * pick(sums, 1))
    total = jnp.zeros((count * M, SPAN), F32)
    for h in range(2):
        place = jnp.where(row + h * half == col, 1.0, 0.0).astype(BF16)
        wh, wl = split(jnp.concatenate(weighted[h], 0))
        total = total + dot(jnp.concatenate([wh, wl], 1), twice(place))
    for s in range(count):
        send_ref[s, 10 * M : 11 * M, :] = total[s * M : (s + 1) * M]


def second_kernel(x_ref, g_ref, rate_ref, res_ref, fwd_ref, inv_ref, *rest):
    mixed_ref, grad_ref = rest[-2:]
    forward = fwd_ref[...]
    taps = [
        dot(powers(rate_ref[s], False), spread(res_ref[:, s * SLICE : (s + 1) * SLICE]))
        for s in range(rate_ref.shape[0])
    ]
    high, low = split(jnp.concatenate(taps, 1))
    kf = dot(forward, twice(high)) + dot(fwd_ref[:, :SPAN], low)
    xf = dot(forward, twice(x_ref[0]))
    gf = dot(forward, twice(g_ref[0]))
    kr, ki, xr, xi, gr, gi = kf[:SPAN], kf[SPAN:], xf[:SPAN], xf[SPAN:], gf[:SPAN], gf[SPAN:]
    mixed_ref[...] = dot(inv_ref[...], stacked(jnp.concatenate([kr * xr - ki * xi, kr * xi + ki * xr], 0)))
    grad_ref[...] = dot(inv_ref[...], stacked(jnp.concatenate([kr * gr + ki * gi, kr * gi - ki * gr], 0)))


def per_channel(values, at):
    owner = lane_group(M, SPAN)
    chosen = jnp.broadcast_to(values[:, at : at + 1], (M, SPAN))
    for k in range(1, SPAN // GROUP):
        chosen = jnp.where(owner == k, values[:, at + k : at + k + 1], chosen)
    return chosen


def placed(parts, h, offset):
    row = lax.broadcasted_iota(jnp.int32, (SPAN, SPAN), 0) // GROUP
    col = lax.broadcasted_iota(jnp.int32, (SPAN, SPAN), 1)
    place = jnp.where(row + (h * (SPAN // GROUP) + offset) == col, 1.0, 0.0).astype(BF16)
    high, low = split(parts)
    return dot(jnp.concatenate([high, low], 1), twice(place))


def pair_kernel(core_ref, kept_ref, arrived_ref, rate_ref, res_ref, pair_ref):
    even = core_ref[0] == 0
    count = kept_ref.shape[0]
    weighted = ([], [])
    for s in range(count):
        for h in range(2):

            def both(q):
                rows = slice((2 * q + h) * M, (2 * q + h + 1) * M)
                kept, arrived = kept_ref[s, rows, :], arrived_ref[s, rows, :]
                return jnp.where(even, kept, arrived), jnp.where(even, arrived, kept)

            def put(q, values):
                pair_ref[s, (2 * q + h) * M : (2 * q + h + 1) * M, :] = values

            rate = rate_ref[s, h * M : (h + 1) * M, :]
            p, far = jnp.exp(-rate), jnp.exp(-rate * SPAN)
            (s1, s2), (t1, t2), (u1, u2), (w1, w2), (r1, r2) = (both(q) for q in range(5))
            put(0, far * s1 + s2)
            put(1, t1 + far * t2)
            put(2, far * (u1 + SPAN * s1) + u2)
            put(3, w1 + far * (w2 + SPAN * t2))
            put(4, r1 + r2 + p * s1 * t2)
            cols = slice(s * SLICE + h * SPAN, s * SLICE + (h + 1) * SPAN)
            weighted[h].append(res_ref[:, cols] * p * (s1 * (w2 + t2) + u1 * t2))
    total = placed(jnp.concatenate(weighted[0], 0), 0, 0) + placed(jnp.concatenate(weighted[1], 0), 1, 0)
    for s in range(count):
        rows = slice(10 * M, 11 * M)
        pair_ref[s, rows, :] = kept_ref[s, rows, :] + arrived_ref[s, rows, :] + total[s * M : (s + 1) * M]


def carry_kernel(pairs, got_ref, rate_ref, res_ref, back_ref):
    for h in range(2):
        cols = slice(h * SPAN, (h + 1) * SPAN)
        rate = rate_ref[:, cols]
        across = jnp.exp(-rate * (2 * SPAN))
        handed = res_ref[:, cols] * jnp.exp(-rate)
        state = jnp.zeros((M, SPAN), F32)
        adjoint = state
        for k in range(pairs):
            last = pairs - 1 - k
            for c in range(2):
                back_ref[2 * k + c, h * M : (h + 1) * M, :] = handed * state
                back_ref[2 * last + c, (2 + h) * M : (3 + h) * M, :] = handed * adjoint
            state = across * state + got_ref[k, h * M : (h + 1) * M, :]
            adjoint = across * adjoint + got_ref[last, (2 + h) * M : (3 + h) * M, :]


def sums_kernel(pairs, scale, index_ref, got_ref, rate_ref, res_ref, sums_ref):
    offset = lax.rem(index_ref[0], SPAN // GROUPS) * GROUPS
    rate_sum = jnp.zeros((M, SPAN), F32)
    for k in range(pairs):
        rate_sum = rate_sum + got_ref[k, 10 * M : 11 * M, :]
    rate_sum = pltpu.roll(rate_sum, offset, 1)
    for h in range(2):
        cols = slice(h * SPAN, (h + 1) * SPAN)
        rate, res = rate_ref[:, cols], res_ref[:, cols]
        pole = jnp.exp(-rate)
        across = jnp.exp(-rate * (2 * SPAN))

        def part(k, q):
            at = (2 * q + h) * M
            return got_ref[k, at : at + M, :]

        zero = jnp.zeros((M, SPAN), F32)
        state, moment, res_part, res_carry, rate_carry = zero, zero, zero, zero, zero
        for k in range(pairs):
            start = part(k, 1)
            res_part = res_part + part(k, 4)
            res_carry = res_carry + state * start
            rate_carry = rate_carry + state * (part(k, 3) + start) + moment * start
            moment = across * (moment + 2 * SPAN * state) + part(k, 2)
            state = across * state + part(k, 0)
        sums_ref[h * M : (h + 1) * M, :] = scale * (res_part + pole * res_carry)
        rate_sum = rate_sum + placed(res * pole * rate_carry, h, offset)
    sums_ref[2 * M : 3 * M, :] = scale * rate_sum


def last_kernel(
    core_ref, mixed_ref, grad_ref, rate_ref, log_ref, res_ref, got_ref, near_ref, far_ref, mixed_out, grad_out
):
    core = core_ref[0]
    even = core == 0
    here = pl.program_id(0) // (pl.num_programs(0) // 2) == core
    rate = jnp.exp(log_ref[...])
    pole, across = jnp.exp(-rate), jnp.exp(-rate * SPAN)
    for s in range(rate_ref.shape[0]):
        cols = slice(s * SLICE, (s + 1) * SLICE)
        states, adjoints = [], []
        for h in range(2):

            def chosen(q):
                rows = slice((2 * q + h) * M, (2 * q + h + 1) * M)
                return jnp.where(here, near_ref[s, rows, :], far_ref[s, rows, :])

            lanes = s * GROUPS + h * (SPAN // GROUP)
            p, far = per_channel(pole, lanes), per_channel(across, lanes)
            handed = res_ref[:, s * SLICE + h * SPAN : s * SLICE + (h + 1) * SPAN] * p
            state, adjoint = got_ref[s, h * M : (h + 1) * M, :], got_ref[s, (2 + h) * M : (3 + h) * M, :]
            end, start = chosen(0), chosen(1)
            states.append(jnp.where(even, state, far * state + handed * end))
            adjoints.append(jnp.where(even, far * adjoint + handed * start, adjoint))
        more = dot(powers(rate_ref[s], False), spread(jnp.concatenate(states, 1)))
        mixed_out[0, :, cols] = (mixed_ref[:, cols] + more).astype(BF16)
        more = dot(powers(rate_ref[s], True), spread(jnp.concatenate(adjoints, 1)))
        grad_out[0, :, cols] = (grad_ref[:, cols] + more).astype(BF16)


def gather_kernel(pairs, all_ref, log_ref, res_out, rate_out):
    chunks = 2 * pairs

    def part(k, rows):
        return all_ref[2 * (k % pairs) + k // pairs, rows, :]

    for k in range(chunks):
        for h in range(2):
            res_out[:, k * SLICE + h * SPAN : k * SLICE + (h + 1) * SPAN] = part(k, slice(h * M, (h + 1) * M))
    width = min(SPAN, chunks * GROUPS)
    per = width // GROUPS
    rows = slice(2 * M, 3 * M)
    for j in range(chunks // per):
        parts = part(j * per, rows)
        for k in range(j * per + 1, (j + 1) * per):
            parts = parts + part(k, rows)
        cols = slice(j * width, (j + 1) * width)
        rate_out[:, cols] = -jnp.exp(log_ref[:, cols]) * parts[:, :width]


def local(signal, out_grad, residues, log_rates):
    channels = signal.shape[2]
    chunks, rows = lax.axis_size("seq"), lax.axis_size("batch")
    index = lax.axis_index("seq").astype(jnp.int32)
    pairs = chunks // 2
    core = lax.rem(index, 2)
    own = core * pairs + index // 2
    swap = [(i, i ^ 1) for i in range(chunks)]
    same_core = [[2 * j + c for j in range(pairs)] for c in range(2)]
    wide = min(WIDE, channels // 2)
    steps = channels // wide
    part = steps // 2
    block = wide // SLICE
    fwd, inv = (jnp.asarray(v) for v in transforms())
    params = pltpu.CompilerParams(vmem_limit_bytes=58 * 2**20)
    little = pltpu.CompilerParams(vmem_limit_bytes=8 * 2**20)
    vmem, smem = pl.BlockSpec(memory_space=pltpu.VMEM), pl.BlockSpec(memory_space=pltpu.SMEM)
    states_shape = jax.ShapeDtypeStruct((pairs, 11 * M, SPAN), F32)
    core_scalar = core[None]

    def whole(a):
        return pl.BlockSpec(a.shape, lambda i, *_: (0,) * a.ndim)

    def exchange(values):
        return lax.all_to_all(values, "seq", 0, 0, axis_index_groups=same_core, tiled=True)

    def other_core(values):
        return lax.ppermute(values, "seq", swap)

    def ends_and_lags(half, x, g):
        return pl.pallas_call(
            first_kernel,
            grid_spec=pltpu.PrefetchScalarGridSpec(
                num_scalar_prefetch=1,
                grid=(part,),
                in_specs=[
                    pl.BlockSpec((1, SPAN, wide), lambda i, at: (0, 0, at[0] * part + i)),
                    pl.BlockSpec((1, SPAN, wide), lambda i, at: (0, 0, at[0] * part + i)),
                    pl.BlockSpec((M, wide // GROUP), lambda i, at: (0, at[0] * part + i)),
                    pl.BlockSpec((M, wide), lambda i, at: (0, at[0] * part + i)),
                    whole(fwd),
                    whole(inv),
                ],
                out_specs=[
                    pl.BlockSpec((block, 11 * M, SPAN), lambda i, at: (i, 0, 0)),
                    pl.BlockSpec((block, 2 * M, SPAN), lambda i, at: (i, 0, 0)),
                ],
            ),
            out_shape=[states_shape, jax.ShapeDtypeStruct((pairs, 2 * M, SPAN), F32)],
            compiler_params=params,
            name="ends_and_lags",
        )(half, x, g, log_rates, residues, fwd, inv)

    away, _ = ends_and_lags(1 - core_scalar, signal, out_grad)
    away, x2, g2 = lax.optimization_barrier((away, signal, out_grad))
    arrived = other_core(away)
    kept, channel_rates = ends_and_lags(core_scalar, x2, g2)
    state_block = pl.BlockSpec((block, 11 * M, SPAN), lambda i, at: (i, 0, 0))
    pair = pl.pallas_call(
        pair_kernel,
        grid_spec=pltpu.PrefetchScalarGridSpec(
            num_scalar_prefetch=1,
            grid=(part,),
            in_specs=[
                state_block,
                state_block,
                pl.BlockSpec((block, 2 * M, SPAN), lambda i, at: (i, 0, 0)),
                pl.BlockSpec((M, wide), lambda i, at: (0, at[0] * part + i)),
            ],
            out_specs=state_block,
        ),
        out_shape=states_shape,
        compiler_params=little,
        name="join_pair",
    )(core_scalar, kept, arrived, channel_rates, residues)
    pair, later_rates, later_res, kept = lax.optimization_barrier((pair, log_rates, residues, kept))
    got = exchange(pair)
    arrived_far = other_core(kept)

    decay_rate = jnp.exp(later_rates)
    rate_rows = jnp.broadcast_to(decay_rate.T.reshape(chunks, 1, SPAN), (chunks, M, SPAN))
    own_rate = jnp.repeat(lax.dynamic_slice_in_dim(decay_rate, own * GROUPS, GROUPS, 1), GROUP, axis=1)
    own_res = lax.dynamic_slice_in_dim(later_res, own * SLICE, SLICE, 1)

    work = SPAN * channels

    def convolutions(half, x, g, *earlier):
        at = half * part
        kernel_blocks = [
            pl.BlockSpec((1, SPAN, wide), lambda i: (0, 0, at + i)),
            pl.BlockSpec((1, SPAN, wide), lambda i: (0, 0, at + i)),
            pl.BlockSpec((block, M, SPAN), lambda i: (at + i, 0, 0)),
            pl.BlockSpec((M, wide), lambda i: (0, at + i)),
            whole(fwd),
            whole(inv),
        ]
        return pl.pallas_call(
            second_kernel,
            grid=(part,),
            in_specs=kernel_blocks + [pl.BlockSpec(memory_space=pl.ANY)] * len(earlier),
            out_specs=[pl.BlockSpec((SPAN, wide), lambda i: (0, at + i))] * 2,
            out_shape=[jax.ShapeDtypeStruct((SPAN, channels), F32)] * 2,
            input_output_aliases={6: 0, 7: 1} if earlier else {},
            compiler_params=params,
            cost_estimate=pl.CostEstimate(flops=work * 300, bytes_accessed=work * 2, transcendentals=0),
            name="local_convolutions",
        )(x, g, rate_rows, residues, fwd, inv, *earlier)

    mixed_part, grad_part = convolutions(0, signal, out_grad)
    got, mixed_part, grad_part, arrived_far = lax.optimization_barrier((got, mixed_part, grad_part, arrived_far))
    back = pl.pallas_call(
        functools.partial(carry_kernel, pairs),
        out_shape=jax.ShapeDtypeStruct((chunks, 4 * M, SPAN), F32),
        compiler_params=little,
        name="carries",
    )(got, own_rate, own_res)
    back, got, x3, g3 = lax.optimization_barrier((back, got, signal, out_grad))
    carried = lax.all_to_all(back, "seq", 0, 0, tiled=True).reshape(pairs, 2, 4 * M, SPAN)
    sums = pl.pallas_call(
        functools.partial(sums_kernel, pairs, 1.0 / (rows * chunks * SPAN)),
        out_shape=jax.ShapeDtypeStruct((3 * M, SPAN), F32),
        in_specs=[smem, vmem, vmem, vmem],
        compiler_params=little,
        cost_estimate=pl.CostEstimate(flops=10**10, bytes_accessed=10**7, transcendentals=0),
        name="gradient_sums",
    )(own[None], got, own_rate, own_res)
    arriving = [lax.ppermute(sums, "batch", [(i, (i + k) % rows) for i in range(rows)]) for k in range(1, rows)]
    mixed_part, grad_part = convolutions(1, x3, g3, mixed_part, grad_part)

    def total_kernel(*refs):
        total = refs[0][...]
        for ref in refs[1:-1]:
            total = total + ref[...]
        for k in range(chunks):
            refs[-1][k] = total

    total = pl.pallas_call(
        total_kernel,
        out_shape=jax.ShapeDtypeStruct((chunks, 3 * M, SPAN), F32),
        compiler_params=little,
        name="total",
    )(sums, *arriving)
    carried, total, mixed_part, grad_part = lax.optimization_barrier((carried, total, mixed_part, grad_part))
    everyone = lax.all_to_all(total, "seq", 0, 0, tiled=True)

    flat_block = pl.BlockSpec((SPAN, wide), lambda i, at: (0, i))
    seq_block = pl.BlockSpec((1, SPAN, wide), lambda i, at: (0, 0, i))
    half_block = pl.BlockSpec((block, 4 * M, SPAN), lambda i, at: (lax.rem(i, part), 0, 0))
    mixed, grad_signal = pl.pallas_call(
        last_kernel,
        grid_spec=pltpu.PrefetchScalarGridSpec(
            num_scalar_prefetch=1,
            grid=(steps,),
            in_specs=[
                flat_block,
                flat_block,
                pl.BlockSpec((block, M, SPAN), lambda i, at: (i, 0, 0)),
                pl.BlockSpec((M, wide // GROUP), lambda i, at: (0, i)),
                pl.BlockSpec((M, wide), lambda i, at: (0, i)),
                pl.BlockSpec((block, None, 4 * M, SPAN), lambda i, at: (lax.rem(i, part), i // part, 0, 0)),
                half_block,
                half_block,
            ],
            out_specs=[seq_block, seq_block],
        ),
        out_shape=[jax.ShapeDtypeStruct(signal.shape, BF16)] * 2,
        compiler_params=params,
        cost_estimate=pl.CostEstimate(flops=work * 1600, bytes_accessed=work * 12, transcendentals=work),
        name="add_carries",
    )(core_scalar, mixed_part, grad_part, rate_rows, log_rates, residues, carried, arrived, arrived_far)
    grad_residues, grad_rates = pl.pallas_call(
        functools.partial(gather_kernel, pairs),
        out_shape=[jax.ShapeDtypeStruct(residues.shape, F32), jax.ShapeDtypeStruct(log_rates.shape, F32)],
        compiler_params=little,
        name="unpack",
    )(everyone, log_rates)
    return mixed, grad_signal, grad_residues, grad_rates


def solution(mesh):
    sharded = P("batch", "seq", None)
    return jax.shard_map(
        local,
        mesh=mesh,
        in_specs=(sharded, sharded, P(), P()),
        out_specs=(sharded, sharded, P(), P()),
        check_vma=False,
    )
```

```python
import functools

import jax
import jax.numpy as jnp
import numpy as np
from jax import lax
from jax.experimental import pallas as pl
from jax.experimental.pallas import tpu as pltpu
from jax.sharding import PartitionSpec as P

M = 8
GROUP = 16
SPAN = 128
SLICE = 256
GROUPS = SLICE // GROUP
WIDE = 2048
F32 = jnp.float32
BF16 = jnp.bfloat16


def split_np(values):
    high = values.astype(np.float32).astype(jnp.bfloat16)
    low = (values - high.astype(np.float64)).astype(np.float32).astype(jnp.bfloat16)
    return high, low


def transforms():
    time = np.arange(SPAN)
    angle = 2 * np.pi * np.outer(np.arange(SPAN) + 0.5, time) / (2 * SPAN)
    forward = np.concatenate([np.cos(angle), -np.sin(angle)], 0)
    inverse = np.concatenate([np.cos(angle.T), -np.sin(angle.T)], 1) / SPAN
    fh, fl = split_np(forward)
    ih, il = split_np(inverse)
    return np.concatenate([fh, fl], 1), np.concatenate([ih, il, ih], 1)


def split(values):
    high = values.astype(BF16)
    return high, (values - high.astype(F32)).astype(BF16)


def dot(a, b):
    return jnp.dot(a, b, preferred_element_type=F32)


def twice(values):
    return jnp.concatenate([values, values], 0)


def stacked(values):
    high, low = split(values)
    return jnp.concatenate([high, high, low], 0)


def lane_group(rows, lanes):
    return lax.broadcasted_iota(jnp.int32, (rows, lanes), 1) // GROUP


def spread(values):
    high = values.astype(BF16).astype(F32)
    low = values - high
    owner = lane_group(M, SLICE)

    def rows(part):
        return jnp.concatenate([jnp.where(owner == g, part, 0.0) for g in range(GROUPS)], 0).astype(BF16)

    top, bottom = rows(high), rows(low)
    return jnp.concatenate([top, top, bottom, bottom], 0)


def powers(rate_row, reverse):
    t = lax.broadcasted_iota(jnp.int32, (SPAN, SPAN), 0)
    t = (SPAN - 1 - t if reverse else t).astype(F32)
    high, low = split(jnp.exp(-rate_row[0:1, :] * t))
    return jnp.concatenate([high, low, high, low], 1)


def first_kernel(x_ref, g_ref, log_ref, res_ref, fwd_ref, inv_ref, send_ref):
    x, g = x_ref[0], g_ref[0]
    xx, gg = twice(x), twice(g)
    forward = fwd_ref[...]
    xf = dot(forward, xx)
    gf = dot(forward, gg)
    xr, xi, gr, gi = xf[:SPAN], xf[SPAN:], gf[:SPAN], gf[SPAN:]
    lags = dot(inv_ref[...], stacked(jnp.concatenate([gr * xr + gi * xi, gi * xr - gr * xi], 0)))
    lag_high, lag_low = split(lags)
    lag_high, lag_low = twice(lag_high), twice(lag_low)
    flip = jnp.where(lax.broadcasted_iota(jnp.int32, (SPAN, SPAN), 0) + lax.broadcasted_iota(jnp.int32, (SPAN, SPAN), 1) == SPAN - 1, 1.0, 0.0).astype(BF16)
    backward = twice(dot(flip, x).astype(BF16))
    lag = lax.broadcasted_iota(jnp.int32, (SPAN, SPAN), 1).astype(F32)
    half = SPAN // GROUP
    owner = lane_group(M, SPAN)
    row = lax.broadcasted_iota(jnp.int32, (SPAN, SPAN), 0) // GROUP
    col = lax.broadcasted_iota(jnp.int32, (SPAN, SPAN), 1)

    def pick(values, q):
        at = q * half * M
        chosen = values[at : at + M]
        for k in range(1, half):
            chosen = jnp.where(owner == k, values[at + k * M : at + (k + 1) * M], chosen)
        return chosen

    count = log_ref.shape[1] // GROUPS
    rate = jnp.exp(log_ref[...])
    weighted = ([], [])
    for s in range(count):
        at = s * GROUPS
        rates = jnp.concatenate([jnp.broadcast_to(rate[:, k : k + 1], (M, SPAN)) for k in range(at, at + GROUPS)], 0)
        early = jnp.exp(-rates * lag)
        for h in range(2):
            rows = slice(h * half * M, (h + 1) * half * M)
            cols = slice(s * SLICE + h * SPAN, s * SLICE + (h + 1) * SPAN)
            eh, el = split(jnp.concatenate([early[rows], lag[rows] * early[rows]], 0))
            found = dot(
                jnp.concatenate([eh, el], 1),
                jnp.concatenate([backward[:, cols], gg[:, cols], lag_high[:, cols], lag_low[:, cols]], 1),
            )
            ends, starts = found[:, :SPAN], found[:, SPAN : 2 * SPAN]
            sums = found[:, 2 * SPAN : 3 * SPAN] + found[:, 3 * SPAN :]
            for q, values in enumerate((pick(ends, 0), pick(starts, 0), pick(ends, 1), pick(starts, 1), pick(sums, 0))):
                at = (2 * q + h) * M
                send_ref[s, at : at + M, :] = values
            weighted[h].append(res_ref[:, cols] * pick(sums, 1))
    total = jnp.zeros((count * M, SPAN), F32)
    for h in range(2):
        place = jnp.where(row + h * half == col, 1.0, 0.0).astype(BF16)
        wh, wl = split(jnp.concatenate(weighted[h], 0))
        total = total + dot(jnp.concatenate([wh, wl], 1), twice(place))
    for s in range(count):
        send_ref[s, 10 * M : 11 * M, :] = total[s * M : (s + 1) * M]


def second_kernel(x_ref, g_ref, rate_ref, res_ref, fwd_ref, inv_ref, mixed_ref, grad_ref):
    forward = fwd_ref[...]
    taps = [
        dot(powers(rate_ref[s], False), spread(res_ref[:, s * SLICE : (s + 1) * SLICE]))
        for s in range(rate_ref.shape[0])
    ]
    high, low = split(jnp.concatenate(taps, 1))
    kf = dot(forward, twice(high)) + dot(fwd_ref[:, :SPAN], low)
    xf = dot(forward, twice(x_ref[0]))
    gf = dot(forward, twice(g_ref[0]))
    kr, ki, xr, xi, gr, gi = kf[:SPAN], kf[SPAN:], xf[:SPAN], xf[SPAN:], gf[:SPAN], gf[SPAN:]
    mixed_ref[...] = dot(inv_ref[...], stacked(jnp.concatenate([kr * xr - ki * xi, kr * xi + ki * xr], 0)))
    grad_ref[...] = dot(inv_ref[...], stacked(jnp.concatenate([kr * gr + ki * gi, kr * gi - ki * gr], 0)))


def carry_kernel(chunks, got_ref, rate_ref, res_ref, back_ref):
    for h in range(2):
        cols = slice(h * SPAN, (h + 1) * SPAN)
        rate = rate_ref[:, cols]
        across = jnp.exp(-rate * SPAN)
        handed = res_ref[:, cols] * jnp.exp(-rate)
        state = jnp.zeros((M, SPAN), F32)
        adjoint = state
        for k in range(chunks):
            last = chunks - 1 - k
            back_ref[k, h * M : (h + 1) * M, :] = handed * state
            back_ref[last, (2 + h) * M : (3 + h) * M, :] = handed * adjoint
            state = across * state + got_ref[k, h * M : (h + 1) * M, :]
            adjoint = across * adjoint + got_ref[last, (2 + h) * M : (3 + h) * M, :]


def sums_kernel(chunks, scale, index_ref, got_ref, rate_ref, res_ref, sums_ref):
    offset = lax.rem(index_ref[0], SPAN // GROUPS) * GROUPS
    rate_sum = jnp.zeros((M, SPAN), F32)
    for k in range(chunks):
        rate_sum = rate_sum + got_ref[k, 10 * M : 11 * M, :]
    rate_sum = pltpu.roll(rate_sum, offset, 1)
    row = lax.broadcasted_iota(jnp.int32, (SPAN, SPAN), 0) // GROUP
    col = lax.broadcasted_iota(jnp.int32, (SPAN, SPAN), 1)
    for h in range(2):
        cols = slice(h * SPAN, (h + 1) * SPAN)
        rate, res = rate_ref[:, cols], res_ref[:, cols]
        pole = jnp.exp(-rate)
        across = jnp.exp(-rate * SPAN)

        def part(k, q):
            at = (2 * q + h) * M
            return got_ref[k, at : at + M, :]

        zero = jnp.zeros((M, SPAN), F32)
        state, moment, res_part, res_carry, rate_carry = zero, zero, zero, zero, zero
        for k in range(chunks):
            start = part(k, 1)
            res_part = res_part + part(k, 4)
            res_carry = res_carry + state * start
            rate_carry = rate_carry + state * (part(k, 3) + start) + moment * start
            moment = across * (moment + SPAN * state) + part(k, 2)
            state = across * state + part(k, 0)
        sums_ref[h * M : (h + 1) * M, :] = scale * (res_part + pole * res_carry)
        place = jnp.where(row + (h * (SPAN // GROUP) + offset) == col, 1.0, 0.0).astype(BF16)
        wh, wl = split(res * pole * rate_carry)
        rate_sum = rate_sum + dot(wh, place) + dot(wl, place)
    sums_ref[2 * M : 3 * M, :] = scale * rate_sum


def last_kernel(mixed_ref, grad_ref, rate_ref, got_ref, mixed_out, grad_out):
    for s in range(rate_ref.shape[0]):
        cols = slice(s * SLICE, (s + 1) * SLICE)
        state = jnp.concatenate([got_ref[s, 0:M, :], got_ref[s, M : 2 * M, :]], 1)
        adjoint = jnp.concatenate([got_ref[s, 2 * M : 3 * M, :], got_ref[s, 3 * M : 4 * M, :]], 1)
        more = dot(powers(rate_ref[s], False), spread(state))
        mixed_out[0, :, cols] = (mixed_ref[:, cols] + more).astype(BF16)
        more = dot(powers(rate_ref[s], True), spread(adjoint))
        grad_out[0, :, cols] = (grad_ref[:, cols] + more).astype(BF16)


def gather_kernel(chunks, all_ref, log_ref, res_out, rate_out):
    for k in range(chunks):
        for h in range(2):
            res_out[:, k * SLICE + h * SPAN : k * SLICE + (h + 1) * SPAN] = all_ref[k, h * M : (h + 1) * M, :]
    width = min(SPAN, chunks * GROUPS)
    per = width // GROUPS
    for j in range(chunks // per):
        parts = all_ref[j * per, 2 * M : 3 * M, :]
        for k in range(j * per + 1, (j + 1) * per):
            parts = parts + all_ref[k, 2 * M : 3 * M, :]
        cols = slice(j * width, (j + 1) * width)
        rate_out[:, cols] = -jnp.exp(log_ref[:, cols]) * parts[:, :width]


def local(signal, out_grad, residues, log_rates):
    channels = signal.shape[2]
    chunks, rows = lax.axis_size("seq"), lax.axis_size("batch")
    index = lax.axis_index("seq")
    wide = min(WIDE, channels)
    steps = channels // wide
    fwd, inv = (jnp.asarray(v) for v in transforms())
    log_block = pl.BlockSpec((M, wide // GROUP), lambda i: (0, i))
    seq_block = pl.BlockSpec((1, SPAN, wide), lambda i: (0, 0, i))
    flat_block = pl.BlockSpec((SPAN, wide), lambda i: (0, i))
    rate_block = pl.BlockSpec((wide // SLICE, M, SPAN), lambda i: (i, 0, 0))
    res_block = pl.BlockSpec((M, wide), lambda i: (0, i))
    whole = lambda a: pl.BlockSpec(a.shape, lambda i: (0,) * a.ndim)
    params = pltpu.CompilerParams(vmem_limit_bytes=58 * 2**20)
    both = 2 * SPAN * channels

    send = pl.pallas_call(
        first_kernel,
        grid=(steps,),
        in_specs=[seq_block, seq_block, log_block, res_block, whole(fwd), whole(inv)],
        out_specs=pl.BlockSpec((wide // SLICE, 11 * M, SPAN), lambda i: (i, 0, 0)),
        out_shape=jax.ShapeDtypeStruct((chunks, 11 * M, SPAN), F32),
        compiler_params=params,
        name="ends_and_lags",
    )(signal, out_grad, log_rates, residues, fwd, inv)
    send, later_rates, later_res = lax.optimization_barrier((send, log_rates, residues))
    decay_rate = jnp.exp(later_rates)
    rate_rows = jnp.broadcast_to(decay_rate.T.reshape(chunks, 1, SPAN), (chunks, M, SPAN))
    own_rate = jnp.repeat(lax.dynamic_slice_in_dim(decay_rate, index * GROUPS, GROUPS, 1), GROUP, axis=1)
    own_res = lax.dynamic_slice_in_dim(later_res, index * SLICE, SLICE, 1)

    got = lax.all_to_all(send, "seq", 0, 0, tiled=True)

    mixed_part, grad_part = pl.pallas_call(
        second_kernel,
        grid=(steps,),
        in_specs=[seq_block, seq_block, rate_block, res_block, whole(fwd), whole(inv)],
        out_specs=[flat_block, flat_block],
        out_shape=[jax.ShapeDtypeStruct((SPAN, channels), F32)] * 2,
        compiler_params=params,
        cost_estimate=pl.CostEstimate(flops=both * 3000, bytes_accessed=both * 8, transcendentals=both),
        name="local_convolutions",
    )(signal, out_grad, rate_rows, residues, fwd, inv)

    got, mixed_part, grad_part = lax.optimization_barrier((got, mixed_part, grad_part))
    vmem = pl.BlockSpec(memory_space=pltpu.VMEM)
    back = pl.pallas_call(
        functools.partial(carry_kernel, chunks),
        out_shape=jax.ShapeDtypeStruct((chunks, 4 * M, SPAN), F32),
        compiler_params=pltpu.CompilerParams(vmem_limit_bytes=8 * 2**20),
        name="carries",
    )(got, own_rate, own_res)
    back, got = lax.optimization_barrier((back, got))
    carried = lax.all_to_all(back, "seq", 0, 0, tiled=True)
    sums = pl.pallas_call(
        functools.partial(sums_kernel, chunks, 1.0 / (rows * chunks * SPAN)),
        out_shape=jax.ShapeDtypeStruct((3 * M, SPAN), F32),
        in_specs=[pl.BlockSpec(memory_space=pltpu.SMEM), vmem, vmem, vmem],
        compiler_params=pltpu.CompilerParams(vmem_limit_bytes=8 * 2**20),
        name="gradient_sums",
    )(index.astype(jnp.int32)[None], got, own_rate, own_res)
    arriving = [lax.ppermute(sums, "batch", [(i, (i + k) % rows) for i in range(rows)]) for k in range(1, rows)]

    def total_kernel(*refs):
        total = refs[0][...]
        for ref in refs[1:-1]:
            total = total + ref[...]
        for k in range(chunks):
            refs[-1][k] = total

    total = pl.pallas_call(
        total_kernel,
        out_shape=jax.ShapeDtypeStruct((chunks, 3 * M, SPAN), F32),
        compiler_params=pltpu.CompilerParams(vmem_limit_bytes=8 * 2**20),
        name="total",
    )(sums, *arriving)
    carried, total = lax.optimization_barrier((carried, total))
    everyone = lax.all_to_all(total, "seq", 0, 0, tiled=True)

    mixed, grad_signal = pl.pallas_call(
        last_kernel,
        grid=(steps,),
        in_specs=[
            flat_block,
            flat_block,
            rate_block,
            pl.BlockSpec((wide // SLICE, 4 * M, SPAN), lambda i: (i, 0, 0)),
        ],
        out_specs=[seq_block, seq_block],
        out_shape=[jax.ShapeDtypeStruct(signal.shape, BF16)] * 2,
        compiler_params=params,
        cost_estimate=pl.CostEstimate(flops=both * 800, bytes_accessed=both * 6, transcendentals=both),
        name="add_carries",
    )(mixed_part, grad_part, rate_rows, carried)
    grad_residues, grad_rates = pl.pallas_call(
        functools.partial(gather_kernel, chunks),
        out_shape=[jax.ShapeDtypeStruct(residues.shape, F32), jax.ShapeDtypeStruct(log_rates.shape, F32)],
        compiler_params=pltpu.CompilerParams(vmem_limit_bytes=8 * 2**20),
        name="unpack",
    )(everyone, log_rates)
    return mixed, grad_signal, grad_residues, grad_rates


def solution(mesh):
    placed = P("batch", "seq", None)
    return jax.shard_map(
        local,
        mesh=mesh,
        in_specs=(placed, placed, P(), P()),
        out_specs=(placed, placed, P(), P()),
        check_vma=False,
    )
```

```python
import functools

import jax
import jax.numpy as jnp
import numpy as np
from jax import lax
from jax.experimental import pallas as pl
from jax.experimental.pallas import tpu as pltpu
from jax.sharding import PartitionSpec as P

M = 8
GROUP = 16
SPAN = 128
SLICE = 256
GROUPS = SLICE // GROUP
WIDE = 2048
F32 = jnp.float32
BF16 = jnp.bfloat16


def split_np(values):
    high = values.astype(np.float32).astype(jnp.bfloat16)
    low = (values - high.astype(np.float64)).astype(np.float32).astype(jnp.bfloat16)
    return high, low


def transforms():
    time = np.arange(SPAN)
    angle = 2 * np.pi * np.outer(np.arange(SPAN) + 0.5, time) / (2 * SPAN)
    forward = np.concatenate([np.cos(angle), -np.sin(angle)], 0)
    inverse = np.concatenate([np.cos(angle.T), -np.sin(angle.T)], 1) / SPAN
    fh, fl = split_np(forward)
    ih, il = split_np(inverse)
    return np.concatenate([fh, fl], 1), np.concatenate([ih, il, ih], 1)


def split(values):
    high = values.astype(BF16)
    return high, (values - high.astype(F32)).astype(BF16)


def dot(a, b):
    return jnp.dot(a, b, preferred_element_type=F32)


def twice(values):
    return jnp.concatenate([values, values], 0)


def stacked(values):
    high, low = split(values)
    return jnp.concatenate([high, high, low], 0)


def lane_group(rows, lanes):
    return lax.broadcasted_iota(jnp.int32, (rows, lanes), 1) // GROUP


def spread(values):
    high = values.astype(BF16).astype(F32)
    low = values - high
    owner = lane_group(M, SLICE)

    def rows(part):
        return jnp.concatenate([jnp.where(owner == g, part, 0.0) for g in range(GROUPS)], 0).astype(BF16)

    top, bottom = rows(high), rows(low)
    return jnp.concatenate([top, top, bottom, bottom], 0)


def powers(rate_row, reverse):
    t = lax.broadcasted_iota(jnp.int32, (SPAN, SPAN), 0)
    t = (SPAN - 1 - t if reverse else t).astype(F32)
    high, low = split(jnp.exp(-rate_row[0:1, :] * t))
    return jnp.concatenate([high, low, high, low], 1)


def first_kernel(half_ref, x_ref, g_ref, log_ref, res_ref, fwd_ref, inv_ref, send_ref):
    x, g = x_ref[0], g_ref[0]
    xx, gg = twice(x), twice(g)
    forward = fwd_ref[...]
    xf = dot(forward, xx)
    gf = dot(forward, gg)
    xr, xi, gr, gi = xf[:SPAN], xf[SPAN:], gf[:SPAN], gf[SPAN:]
    lags = dot(inv_ref[...], stacked(jnp.concatenate([gr * xr + gi * xi, gi * xr - gr * xi], 0)))
    lag_high, lag_low = split(lags)
    lag_high, lag_low = twice(lag_high), twice(lag_low)
    flip = jnp.where(lax.broadcasted_iota(jnp.int32, (SPAN, SPAN), 0) + lax.broadcasted_iota(jnp.int32, (SPAN, SPAN), 1) == SPAN - 1, 1.0, 0.0).astype(BF16)
    backward = twice(dot(flip, x).astype(BF16))
    lag = lax.broadcasted_iota(jnp.int32, (SPAN, SPAN), 1).astype(F32)
    half = SPAN // GROUP
    owner = lane_group(M, SPAN)
    row = lax.broadcasted_iota(jnp.int32, (SPAN, SPAN), 0) // GROUP
    col = lax.broadcasted_iota(jnp.int32, (SPAN, SPAN), 1)

    def pick(values, q):
        at = q * half * M
        chosen = values[at : at + M]
        for k in range(1, half):
            chosen = jnp.where(owner == k, values[at + k * M : at + (k + 1) * M], chosen)
        return chosen

    count = log_ref.shape[1] // GROUPS
    rate = jnp.exp(log_ref[...])
    weighted = ([], [])
    for s in range(count):
        at = s * GROUPS
        rates = jnp.concatenate([jnp.broadcast_to(rate[:, k : k + 1], (M, SPAN)) for k in range(at, at + GROUPS)], 0)
        early = jnp.exp(-rates * lag)
        for h in range(2):
            send_ref[s, (11 + h) * M : (12 + h) * M, :] = pick(rates[h * half * M : (h + 1) * half * M], 0)
        for h in range(2):
            rows = slice(h * half * M, (h + 1) * half * M)
            cols = slice(s * SLICE + h * SPAN, s * SLICE + (h + 1) * SPAN)
            eh, el = split(jnp.concatenate([early[rows], lag[rows] * early[rows]], 0))
            found = dot(
                jnp.concatenate([eh, el], 1),
                jnp.concatenate([backward[:, cols], gg[:, cols], lag_high[:, cols], lag_low[:, cols]], 1),
            )
            ends, starts = found[:, :SPAN], found[:, SPAN : 2 * SPAN]
            sums = found[:, 2 * SPAN : 3 * SPAN] + found[:, 3 * SPAN :]
            for q, values in enumerate((pick(ends, 0), pick(starts, 0), pick(ends, 1), pick(starts, 1), pick(sums, 0))):
                at = (2 * q + h) * M
                send_ref[s, at : at + M, :] = values
            weighted[h].append(res_ref[:, cols] * pick(sums, 1))
    total = jnp.zeros((count * M, SPAN), F32)
    for h in range(2):
        place = jnp.where(row + h * half == col, 1.0, 0.0).astype(BF16)
        wh, wl = split(jnp.concatenate(weighted[h], 0))
        total = total + dot(jnp.concatenate([wh, wl], 1), twice(place))
    for s in range(count):
        send_ref[s, 10 * M : 11 * M, :] = total[s * M : (s + 1) * M]


def second_kernel(x_ref, g_ref, rate_ref, res_ref, fwd_ref, inv_ref, *rest):
    mixed_ref, grad_ref = rest[-2:]
    forward = fwd_ref[...]
    taps = [
        dot(powers(rate_ref[s], False), spread(res_ref[:, s * SLICE : (s + 1) * SLICE]))
        for s in range(rate_ref.shape[0])
    ]
    high, low = split(jnp.concatenate(taps, 1))
    kf = dot(forward, twice(high)) + dot(fwd_ref[:, :SPAN], low)
    xf = dot(forward, twice(x_ref[0]))
    gf = dot(forward, twice(g_ref[0]))
    kr, ki, xr, xi, gr, gi = kf[:SPAN], kf[SPAN:], xf[:SPAN], xf[SPAN:], gf[:SPAN], gf[SPAN:]
    mixed_ref[...] = dot(inv_ref[...], stacked(jnp.concatenate([kr * xr - ki * xi, kr * xi + ki * xr], 0)))
    grad_ref[...] = dot(inv_ref[...], stacked(jnp.concatenate([kr * gr + ki * gi, kr * gi - ki * gr], 0)))


def per_channel(values, at):
    owner = lane_group(M, SPAN)
    chosen = jnp.broadcast_to(values[:, at : at + 1], (M, SPAN))
    for k in range(1, SPAN // GROUP):
        chosen = jnp.where(owner == k, values[:, at + k : at + k + 1], chosen)
    return chosen


def placed(parts, h, offset):
    row = lax.broadcasted_iota(jnp.int32, (SPAN, SPAN), 0) // GROUP
    col = lax.broadcasted_iota(jnp.int32, (SPAN, SPAN), 1)
    place = jnp.where(row + (h * (SPAN // GROUP) + offset) == col, 1.0, 0.0).astype(BF16)
    high, low = split(parts)
    return dot(jnp.concatenate([high, low], 1), twice(place))


def pair_kernel(core_ref, kept_ref, arrived_ref, res_ref, pair_ref):
    even = core_ref[0] == 0
    count = kept_ref.shape[0]
    weighted = ([], [])
    for s in range(count):
        for h in range(2):

            def both(q):
                rows = slice((2 * q + h) * M, (2 * q + h + 1) * M)
                kept, arrived = kept_ref[s, rows, :], arrived_ref[s, rows, :]
                return jnp.where(even, kept, arrived), jnp.where(even, arrived, kept)

            def put(q, values):
                pair_ref[s, (2 * q + h) * M : (2 * q + h + 1) * M, :] = values

            rate = kept_ref[s, (11 + h) * M : (12 + h) * M, :]
            p, far = jnp.exp(-rate), jnp.exp(-rate * SPAN)
            (s1, s2), (t1, t2), (u1, u2), (w1, w2), (r1, r2) = (both(q) for q in range(5))
            put(0, far * s1 + s2)
            put(1, t1 + far * t2)
            put(2, far * (u1 + SPAN * s1) + u2)
            put(3, w1 + far * (w2 + SPAN * t2))
            put(4, r1 + r2 + p * s1 * t2)
            cols = slice(s * SLICE + h * SPAN, s * SLICE + (h + 1) * SPAN)
            weighted[h].append(res_ref[:, cols] * p * (s1 * (w2 + t2) + u1 * t2))
    total = placed(jnp.concatenate(weighted[0], 0), 0, 0) + placed(jnp.concatenate(weighted[1], 0), 1, 0)
    for s in range(count):
        rows = slice(10 * M, 11 * M)
        pair_ref[s, rows, :] = kept_ref[s, rows, :] + arrived_ref[s, rows, :] + total[s * M : (s + 1) * M]


def carry_kernel(pairs, got_ref, rate_ref, res_ref, back_ref):
    for h in range(2):
        cols = slice(h * SPAN, (h + 1) * SPAN)
        rate = rate_ref[:, cols]
        across = jnp.exp(-rate * (2 * SPAN))
        handed = res_ref[:, cols] * jnp.exp(-rate)
        state = jnp.zeros((M, SPAN), F32)
        adjoint = state
        for k in range(pairs):
            last = pairs - 1 - k
            for c in range(2):
                back_ref[2 * k + c, h * M : (h + 1) * M, :] = handed * state
                back_ref[2 * last + c, (2 + h) * M : (3 + h) * M, :] = handed * adjoint
            state = across * state + got_ref[k, h * M : (h + 1) * M, :]
            adjoint = across * adjoint + got_ref[last, (2 + h) * M : (3 + h) * M, :]


def sums_kernel(pairs, scale, index_ref, got_ref, rate_ref, res_ref, sums_ref):
    offset = lax.rem(index_ref[0], SPAN // GROUPS) * GROUPS
    rate_sum = jnp.zeros((M, SPAN), F32)
    for k in range(pairs):
        rate_sum = rate_sum + got_ref[k, 10 * M : 11 * M, :]
    rate_sum = pltpu.roll(rate_sum, offset, 1)
    for h in range(2):
        cols = slice(h * SPAN, (h + 1) * SPAN)
        rate, res = rate_ref[:, cols], res_ref[:, cols]
        pole = jnp.exp(-rate)
        across = jnp.exp(-rate * (2 * SPAN))

        def part(k, q):
            at = (2 * q + h) * M
            return got_ref[k, at : at + M, :]

        zero = jnp.zeros((M, SPAN), F32)
        state, moment, res_part, res_carry, rate_carry = zero, zero, zero, zero, zero
        for k in range(pairs):
            start = part(k, 1)
            res_part = res_part + part(k, 4)
            res_carry = res_carry + state * start
            rate_carry = rate_carry + state * (part(k, 3) + start) + moment * start
            moment = across * (moment + 2 * SPAN * state) + part(k, 2)
            state = across * state + part(k, 0)
        sums_ref[h * M : (h + 1) * M, :] = scale * (res_part + pole * res_carry)
        rate_sum = rate_sum + placed(res * pole * rate_carry, h, offset)
    sums_ref[2 * M : 3 * M, :] = scale * rate_sum


def last_kernel(
    core_ref, mixed_ref, grad_ref, rate_ref, log_ref, res_ref, got_ref, near_ref, far_ref, mixed_out, grad_out
):
    core = core_ref[0]
    even = core == 0
    here = pl.program_id(0) // (pl.num_programs(0) // 2) == core
    rate = jnp.exp(log_ref[...])
    pole, across = jnp.exp(-rate), jnp.exp(-rate * SPAN)
    for s in range(rate_ref.shape[0]):
        cols = slice(s * SLICE, (s + 1) * SLICE)
        states, adjoints = [], []
        for h in range(2):

            def chosen(q):
                rows = slice((2 * q + h) * M, (2 * q + h + 1) * M)
                return jnp.where(here, near_ref[s, rows, :], far_ref[s, rows, :])

            lanes = s * GROUPS + h * (SPAN // GROUP)
            p, far = per_channel(pole, lanes), per_channel(across, lanes)
            handed = res_ref[:, s * SLICE + h * SPAN : s * SLICE + (h + 1) * SPAN] * p
            state, adjoint = got_ref[s, h * M : (h + 1) * M, :], got_ref[s, (2 + h) * M : (3 + h) * M, :]
            end, start = chosen(0), chosen(1)
            states.append(jnp.where(even, state, far * state + handed * end))
            adjoints.append(jnp.where(even, far * adjoint + handed * start, adjoint))
        more = dot(powers(rate_ref[s], False), spread(jnp.concatenate(states, 1)))
        mixed_out[0, :, cols] = (mixed_ref[:, cols] + more).astype(BF16)
        more = dot(powers(rate_ref[s], True), spread(jnp.concatenate(adjoints, 1)))
        grad_out[0, :, cols] = (grad_ref[:, cols] + more).astype(BF16)


def gather_kernel(pairs, all_ref, log_ref, res_out, rate_out):
    chunks = 2 * pairs

    def part(k, rows):
        return all_ref[2 * (k % pairs) + k // pairs, rows, :]

    for k in range(chunks):
        for h in range(2):
            res_out[:, k * SLICE + h * SPAN : k * SLICE + (h + 1) * SPAN] = part(k, slice(h * M, (h + 1) * M))
    width = min(SPAN, chunks * GROUPS)
    per = width // GROUPS
    rows = slice(2 * M, 3 * M)
    for j in range(chunks // per):
        parts = part(j * per, rows)
        for k in range(j * per + 1, (j + 1) * per):
            parts = parts + part(k, rows)
        cols = slice(j * width, (j + 1) * width)
        rate_out[:, cols] = -jnp.exp(log_ref[:, cols]) * parts[:, :width]


def local(signal, out_grad, residues, log_rates):
    channels = signal.shape[2]
    chunks, rows = lax.axis_size("seq"), lax.axis_size("batch")
    index = lax.axis_index("seq").astype(jnp.int32)
    pairs = chunks // 2
    core = lax.rem(index, 2)
    own = core * pairs + index // 2
    swap = [(i, i ^ 1) for i in range(chunks)]
    same_core = [[2 * j + c for j in range(pairs)] for c in range(2)]
    wide = min(WIDE, channels // 2)
    steps = channels // wide
    part = steps // 2
    block = wide // SLICE
    fwd, inv = (jnp.asarray(v) for v in transforms())
    params = pltpu.CompilerParams(vmem_limit_bytes=58 * 2**20)
    little = pltpu.CompilerParams(vmem_limit_bytes=8 * 2**20)
    vmem, smem = pl.BlockSpec(memory_space=pltpu.VMEM), pl.BlockSpec(memory_space=pltpu.SMEM)
    states_shape = jax.ShapeDtypeStruct((pairs, 11 * M, SPAN), F32)
    core_scalar = core[None]

    def whole(a):
        return pl.BlockSpec(a.shape, lambda i, *_: (0,) * a.ndim)

    def exchange(values):
        return lax.all_to_all(values, "seq", 0, 0, axis_index_groups=same_core, tiled=True)

    def other_core(values):
        return lax.ppermute(values, "seq", swap)

    def ends_and_lags(half, x, g, room):
        return pl.pallas_call(
            first_kernel,
            grid_spec=pltpu.PrefetchScalarGridSpec(
                num_scalar_prefetch=1,
                grid=(part,),
                in_specs=[
                    pl.BlockSpec((1, SPAN, wide), lambda i, at: (0, 0, at[0] * part + i)),
                    pl.BlockSpec((1, SPAN, wide), lambda i, at: (0, 0, at[0] * part + i)),
                    pl.BlockSpec((M, wide // GROUP), lambda i, at: (0, at[0] * part + i)),
                    pl.BlockSpec((M, wide), lambda i, at: (0, at[0] * part + i)),
                    whole(fwd),
                    whole(inv),
                ],
                out_specs=pl.BlockSpec((block, 13 * M, SPAN), lambda i, at: (i, 0, 0)),
            ),
            out_shape=jax.ShapeDtypeStruct((pairs, 13 * M, SPAN), F32),
            compiler_params=room,
            name="ends_and_lags",
        )(half, x, g, log_rates, residues, fwd, inv)

    away = ends_and_lags(1 - core_scalar, signal, out_grad, params)
    away, x2, g2 = lax.optimization_barrier((away, signal, out_grad))
    arrived = other_core(away)
    kept = ends_and_lags(core_scalar, x2, g2, pltpu.CompilerParams(vmem_limit_bytes=40 * 2**20))
    state_block = pl.BlockSpec((block, 11 * M, SPAN), lambda i, at: (i, 0, 0))
    pair = pl.pallas_call(
        pair_kernel,
        grid_spec=pltpu.PrefetchScalarGridSpec(
            num_scalar_prefetch=1,
            grid=(part,),
            in_specs=[
                pl.BlockSpec((block, 13 * M, SPAN), lambda i, at: (i, 0, 0)),
                pl.BlockSpec((block, 11 * M, SPAN), lambda i, at: (i, 0, 0)),
                pl.BlockSpec((M, wide), lambda i, at: (0, at[0] * part + i)),
            ],
            out_specs=state_block,
        ),
        out_shape=states_shape,
        compiler_params=little,
        name="join_pair",
    )(core_scalar, kept, arrived, residues)
    pair, later_rates, later_res, kept = lax.optimization_barrier((pair, log_rates, residues, kept))
    got = exchange(pair)

    decay_rate = jnp.exp(later_rates)
    rate_rows = jnp.broadcast_to(decay_rate.T.reshape(chunks, 1, SPAN), (chunks, M, SPAN))
    own_rate = jnp.repeat(lax.dynamic_slice_in_dim(decay_rate, own * GROUPS, GROUPS, 1), GROUP, axis=1)
    own_res = lax.dynamic_slice_in_dim(later_res, own * SLICE, SLICE, 1)

    work = SPAN * channels

    def convolutions(at, count, x, g, *earlier):
        kernel_blocks = [
            pl.BlockSpec((1, SPAN, wide), lambda i: (0, 0, at + i)),
            pl.BlockSpec((1, SPAN, wide), lambda i: (0, 0, at + i)),
            pl.BlockSpec((block, M, SPAN), lambda i: (at + i, 0, 0)),
            pl.BlockSpec((M, wide), lambda i: (0, at + i)),
            whole(fwd),
            whole(inv),
        ]
        return pl.pallas_call(
            second_kernel,
            grid=(count,),
            in_specs=kernel_blocks + [pl.BlockSpec(memory_space=pl.ANY)] * len(earlier),
            out_specs=[pl.BlockSpec((SPAN, wide), lambda i: (0, at + i))] * 2,
            out_shape=[jax.ShapeDtypeStruct((SPAN, channels), F32)] * 2,
            input_output_aliases={6: 0, 7: 1} if earlier else {},
            compiler_params=params,
            cost_estimate=pl.CostEstimate(flops=work * 300, bytes_accessed=work * 2, transcendentals=0),
            name="local_convolutions",
        )(x, g, rate_rows, residues, fwd, inv, *earlier)

    early = steps - max(1, steps // 4)
    mixed_part, grad_part = convolutions(0, early, signal, out_grad)
    got, mixed_part, grad_part = lax.optimization_barrier((got, mixed_part, grad_part))
    back = pl.pallas_call(
        functools.partial(carry_kernel, pairs),
        out_shape=jax.ShapeDtypeStruct((chunks, 4 * M, SPAN), F32),
        compiler_params=little,
        name="carries",
    )(got, own_rate, own_res)
    back, got, x3, g3, kept = lax.optimization_barrier((back, got, signal, out_grad, kept))
    carried = lax.all_to_all(back, "seq", 0, 0, tiled=True).reshape(pairs, 2, 4 * M, SPAN)
    sums = pl.pallas_call(
        functools.partial(sums_kernel, pairs, 1.0 / (rows * chunks * SPAN)),
        out_shape=jax.ShapeDtypeStruct((3 * M, SPAN), F32),
        in_specs=[smem, vmem, vmem, vmem],
        compiler_params=little,
        cost_estimate=pl.CostEstimate(flops=10**10, bytes_accessed=10**7, transcendentals=0),
        name="gradient_sums",
    )(own[None], got, own_rate, own_res)
    arriving = [lax.ppermute(sums, "batch", [(i, (i + k) % rows) for i in range(rows)]) for k in range(1, rows)]
    arrived_far = other_core(kept)
    mixed_part, grad_part = convolutions(early, steps - early, x3, g3, mixed_part, grad_part)

    def total_kernel(*refs):
        total = refs[0][...]
        for ref in refs[1:-1]:
            total = total + ref[...]
        for k in range(chunks):
            refs[-1][k] = total

    total = pl.pallas_call(
        total_kernel,
        out_shape=jax.ShapeDtypeStruct((chunks, 3 * M, SPAN), F32),
        compiler_params=little,
        name="total",
    )(sums, *arriving)
    carried, total, mixed_part, grad_part, arrived_far = lax.optimization_barrier(
        (carried, total, mixed_part, grad_part, arrived_far)
    )
    everyone = lax.all_to_all(total, "seq", 0, 0, tiled=True)

    flat_block = pl.BlockSpec((SPAN, wide), lambda i, at: (0, i))
    seq_block = pl.BlockSpec((1, SPAN, wide), lambda i, at: (0, 0, i))
    half_block = pl.BlockSpec((block, 4 * M, SPAN), lambda i, at: (lax.rem(i, part), 0, 0))
    mixed, grad_signal = pl.pallas_call(
        last_kernel,
        grid_spec=pltpu.PrefetchScalarGridSpec(
            num_scalar_prefetch=1,
            grid=(steps,),
            in_specs=[
                flat_block,
                flat_block,
                pl.BlockSpec((block, M, SPAN), lambda i, at: (i, 0, 0)),
                pl.BlockSpec((M, wide // GROUP), lambda i, at: (0, i)),
                pl.BlockSpec((M, wide), lambda i, at: (0, i)),
                pl.BlockSpec((block, None, 4 * M, SPAN), lambda i, at: (lax.rem(i, part), i // part, 0, 0)),
                half_block,
                half_block,
            ],
            out_specs=[seq_block, seq_block],
        ),
        out_shape=[jax.ShapeDtypeStruct(signal.shape, BF16)] * 2,
        compiler_params=params,
        cost_estimate=pl.CostEstimate(flops=work * 1600, bytes_accessed=work * 12, transcendentals=work),
        name="add_carries",
    )(core_scalar, mixed_part, grad_part, rate_rows, log_rates, residues, carried, arrived, arrived_far)
    grad_residues, grad_rates = pl.pallas_call(
        functools.partial(gather_kernel, pairs),
        out_shape=[jax.ShapeDtypeStruct(residues.shape, F32), jax.ShapeDtypeStruct(log_rates.shape, F32)],
        compiler_params=little,
        name="unpack",
    )(everyone, log_rates)
    return mixed, grad_signal, grad_residues, grad_rates


def solution(mesh):
    sharded = P("batch", "seq", None)
    return jax.shard_map(
        local,
        mesh=mesh,
        in_specs=(sharded, sharded, P(), P()),
        out_specs=(sharded, sharded, P(), P()),
        check_vma=False,
    )
```

```python
import functools

import jax
import jax.numpy as jnp
import numpy as np
from jax import lax
from jax.experimental import pallas as pl
from jax.experimental.pallas import tpu as pltpu
from jax.sharding import PartitionSpec as P

M = 8
GROUP = 16
SPAN = 128
SLICE = 256
GROUPS = SLICE // GROUP
WIDE = 2048
F32 = jnp.float32
BF16 = jnp.bfloat16


def split_np(values):
    high = values.astype(np.float32).astype(jnp.bfloat16)
    low = (values - high.astype(np.float64)).astype(np.float32).astype(jnp.bfloat16)
    return high, low


def transforms():
    time = np.arange(SPAN)
    angle = 2 * np.pi * np.outer(np.arange(SPAN) + 0.5, time) / (2 * SPAN)
    forward = np.concatenate([np.cos(angle), -np.sin(angle)], 0)
    inverse = np.concatenate([np.cos(angle.T), -np.sin(angle.T)], 1) / SPAN
    fh, fl = split_np(forward)
    ih, il = split_np(inverse)
    return np.concatenate([fh, fl], 1), np.concatenate([ih, il, ih], 1)


def split(values):
    high = values.astype(BF16)
    return high, (values - high.astype(F32)).astype(BF16)


def dot(a, b):
    return jnp.dot(a, b, preferred_element_type=F32)


def twice(values):
    return jnp.concatenate([values, values], 0)


def stacked(values):
    high, low = split(values)
    return jnp.concatenate([high, high, low], 0)


def lane_group(rows, lanes):
    return lax.broadcasted_iota(jnp.int32, (rows, lanes), 1) // GROUP


def spread(values):
    high = values.astype(BF16).astype(F32)
    low = values - high
    owner = lane_group(M, SLICE)

    def rows(part):
        return jnp.concatenate([jnp.where(owner == g, part, 0.0) for g in range(GROUPS)], 0).astype(BF16)

    top, bottom = rows(high), rows(low)
    return jnp.concatenate([top, top, bottom, bottom], 0)


def powers(rate_row, reverse):
    t = lax.broadcasted_iota(jnp.int32, (SPAN, SPAN), 0)
    t = (SPAN - 1 - t if reverse else t).astype(F32)
    high, low = split(jnp.exp(-rate_row[0:1, :] * t))
    return jnp.concatenate([high, low, high, low], 1)


def first_kernel(half_ref, x_ref, g_ref, log_ref, res_ref, fwd_ref, inv_ref, send_ref):
    x, g = x_ref[0], g_ref[0]
    xx, gg = twice(x), twice(g)
    forward = fwd_ref[...]
    xf = dot(forward, xx)
    gf = dot(forward, gg)
    xr, xi, gr, gi = xf[:SPAN], xf[SPAN:], gf[:SPAN], gf[SPAN:]
    lags = dot(inv_ref[...], stacked(jnp.concatenate([gr * xr + gi * xi, gi * xr - gr * xi], 0)))
    lag_high, lag_low = split(lags)
    lag_high, lag_low = twice(lag_high), twice(lag_low)
    flip = jnp.where(lax.broadcasted_iota(jnp.int32, (SPAN, SPAN), 0) + lax.broadcasted_iota(jnp.int32, (SPAN, SPAN), 1) == SPAN - 1, 1.0, 0.0).astype(BF16)
    backward = twice(dot(flip, x).astype(BF16))
    lag = lax.broadcasted_iota(jnp.int32, (SPAN, SPAN), 1).astype(F32)
    half = SPAN // GROUP
    owner = lane_group(M, SPAN)
    row = lax.broadcasted_iota(jnp.int32, (SPAN, SPAN), 0) // GROUP
    col = lax.broadcasted_iota(jnp.int32, (SPAN, SPAN), 1)

    def pick(values, q):
        at = q * half * M
        chosen = values[at : at + M]
        for k in range(1, half):
            chosen = jnp.where(owner == k, values[at + k * M : at + (k + 1) * M], chosen)
        return chosen

    count = log_ref.shape[1] // GROUPS
    rate = jnp.exp(log_ref[...])
    weighted = ([], [])
    for s in range(count):
        at = s * GROUPS
        rates = jnp.concatenate([jnp.broadcast_to(rate[:, k : k + 1], (M, SPAN)) for k in range(at, at + GROUPS)], 0)
        early = jnp.exp(-rates * lag)
        for h in range(2):
            send_ref[s, (11 + h) * M : (12 + h) * M, :] = pick(rates[h * half * M : (h + 1) * half * M], 0)
        for h in range(2):
            rows = slice(h * half * M, (h + 1) * half * M)
            cols = slice(s * SLICE + h * SPAN, s * SLICE + (h + 1) * SPAN)
            eh, el = split(jnp.concatenate([early[rows], lag[rows] * early[rows]], 0))
            found = dot(
                jnp.concatenate([eh, el], 1),
                jnp.concatenate([backward[:, cols], gg[:, cols], lag_high[:, cols], lag_low[:, cols]], 1),
            )
            ends, starts = found[:, :SPAN], found[:, SPAN : 2 * SPAN]
            sums = found[:, 2 * SPAN : 3 * SPAN] + found[:, 3 * SPAN :]
            for q, values in enumerate((pick(ends, 0), pick(starts, 0), pick(ends, 1), pick(starts, 1), pick(sums, 0))):
                at = (2 * q + h) * M
                send_ref[s, at : at + M, :] = values
            weighted[h].append(res_ref[:, cols] * pick(sums, 1))
    total = jnp.zeros((count * M, SPAN), F32)
    for h in range(2):
        place = jnp.where(row + h * half == col, 1.0, 0.0).astype(BF16)
        wh, wl = split(jnp.concatenate(weighted[h], 0))
        total = total + dot(jnp.concatenate([wh, wl], 1), twice(place))
    for s in range(count):
        send_ref[s, 10 * M : 11 * M, :] = total[s * M : (s + 1) * M]


def second_kernel(x_ref, g_ref, rate_ref, res_ref, fwd_ref, inv_ref, *rest):
    mixed_ref, grad_ref = rest[-2:]
    forward = fwd_ref[...]
    taps = [
        dot(powers(rate_ref[s], False), spread(res_ref[:, s * SLICE : (s + 1) * SLICE]))
        for s in range(rate_ref.shape[0])
    ]
    high, low = split(jnp.concatenate(taps, 1))
    kf = dot(forward, twice(high)) + dot(fwd_ref[:, :SPAN], low)
    xf = dot(forward, twice(x_ref[0]))
    gf = dot(forward, twice(g_ref[0]))
    kr, ki, xr, xi, gr, gi = kf[:SPAN], kf[SPAN:], xf[:SPAN], xf[SPAN:], gf[:SPAN], gf[SPAN:]
    mixed_ref[...] = dot(inv_ref[...], stacked(jnp.concatenate([kr * xr - ki * xi, kr * xi + ki * xr], 0)))
    grad_ref[...] = dot(inv_ref[...], stacked(jnp.concatenate([kr * gr + ki * gi, kr * gi - ki * gr], 0)))


def per_channel(values, at):
    owner = lane_group(M, SPAN)
    chosen = jnp.broadcast_to(values[:, at : at + 1], (M, SPAN))
    for k in range(1, SPAN // GROUP):
        chosen = jnp.where(owner == k, values[:, at + k : at + k + 1], chosen)
    return chosen


def placed(parts, h, offset):
    row = lax.broadcasted_iota(jnp.int32, (SPAN, SPAN), 0) // GROUP
    col = lax.broadcasted_iota(jnp.int32, (SPAN, SPAN), 1)
    place = jnp.where(row + (h * (SPAN // GROUP) + offset) == col, 1.0, 0.0).astype(BF16)
    high, low = split(parts)
    return dot(jnp.concatenate([high, low], 1), twice(place))


def pair_kernel(core_ref, kept_ref, arrived_ref, res_ref, pair_ref, mine_ref, near_ref):
    even = core_ref[0] == 0
    count = kept_ref.shape[0]
    mine_ref[...] = kept_ref[:, : 4 * M, :]
    near_ref[...] = arrived_ref[:, : 4 * M, :]
    weighted = ([], [])
    for s in range(count):
        for h in range(2):

            def both(q):
                rows = slice((2 * q + h) * M, (2 * q + h + 1) * M)
                kept, arrived = kept_ref[s, rows, :], arrived_ref[s, rows, :]
                return jnp.where(even, kept, arrived), jnp.where(even, arrived, kept)

            def put(q, values):
                pair_ref[s, (2 * q + h) * M : (2 * q + h + 1) * M, :] = values

            rate = kept_ref[s, (11 + h) * M : (12 + h) * M, :]
            p, far = jnp.exp(-rate), jnp.exp(-rate * SPAN)
            (s1, s2), (t1, t2), (u1, u2), (w1, w2), (r1, r2) = (both(q) for q in range(5))
            put(0, far * s1 + s2)
            put(1, t1 + far * t2)
            put(2, far * (u1 + SPAN * s1) + u2)
            put(3, w1 + far * (w2 + SPAN * t2))
            put(4, r1 + r2 + p * s1 * t2)
            cols = slice(s * SLICE + h * SPAN, s * SLICE + (h + 1) * SPAN)
            weighted[h].append(res_ref[:, cols] * p * (s1 * (w2 + t2) + u1 * t2))
    total = placed(jnp.concatenate(weighted[0], 0), 0, 0) + placed(jnp.concatenate(weighted[1], 0), 1, 0)
    for s in range(count):
        rows = slice(10 * M, 11 * M)
        pair_ref[s, rows, :] = kept_ref[s, rows, :] + arrived_ref[s, rows, :] + total[s * M : (s + 1) * M]


def carry_kernel(pairs, got_ref, rate_ref, res_ref, back_ref):
    for h in range(2):
        cols = slice(h * SPAN, (h + 1) * SPAN)
        rate = rate_ref[:, cols]
        across = jnp.exp(-rate * (2 * SPAN))
        handed = res_ref[:, cols] * jnp.exp(-rate)
        state = jnp.zeros((M, SPAN), F32)
        adjoint = state
        for k in range(pairs):
            last = pairs - 1 - k
            for c in range(2):
                back_ref[2 * k + c, h * M : (h + 1) * M, :] = handed * state
                back_ref[2 * last + c, (2 + h) * M : (3 + h) * M, :] = handed * adjoint
            state = across * state + got_ref[k, h * M : (h + 1) * M, :]
            adjoint = across * adjoint + got_ref[last, (2 + h) * M : (3 + h) * M, :]


def sums_kernel(pairs, scale, index_ref, got_ref, rate_ref, res_ref, sums_ref):
    offset = lax.rem(index_ref[0], SPAN // GROUPS) * GROUPS
    rate_sum = jnp.zeros((M, SPAN), F32)
    for k in range(pairs):
        rate_sum = rate_sum + got_ref[k, 10 * M : 11 * M, :]
    rate_sum = pltpu.roll(rate_sum, offset, 1)
    for h in range(2):
        cols = slice(h * SPAN, (h + 1) * SPAN)
        rate, res = rate_ref[:, cols], res_ref[:, cols]
        pole = jnp.exp(-rate)
        across = jnp.exp(-rate * (2 * SPAN))

        def part(k, q):
            at = (2 * q + h) * M
            return got_ref[k, at : at + M, :]

        zero = jnp.zeros((M, SPAN), F32)
        state, moment, res_part, res_carry, rate_carry = zero, zero, zero, zero, zero
        for k in range(pairs):
            start = part(k, 1)
            res_part = res_part + part(k, 4)
            res_carry = res_carry + state * start
            rate_carry = rate_carry + state * (part(k, 3) + start) + moment * start
            moment = across * (moment + 2 * SPAN * state) + part(k, 2)
            state = across * state + part(k, 0)
        sums_ref[h * M : (h + 1) * M, :] = scale * (res_part + pole * res_carry)
        rate_sum = rate_sum + placed(res * pole * rate_carry, h, offset)
    sums_ref[2 * M : 3 * M, :] = scale * rate_sum


def last_kernel(
    core_ref, mixed_ref, grad_ref, rate_ref, log_ref, res_ref, got_ref, near_ref, far_ref, mixed_out, grad_out
):
    core = core_ref[0]
    even = core == 0
    here = pl.program_id(0) // (pl.num_programs(0) // 2) == core
    rate = jnp.exp(log_ref[...])
    pole, across = jnp.exp(-rate), jnp.exp(-rate * SPAN)
    for s in range(rate_ref.shape[0]):
        cols = slice(s * SLICE, (s + 1) * SLICE)
        states, adjoints = [], []
        for h in range(2):

            def chosen(q):
                rows = slice((2 * q + h) * M, (2 * q + h + 1) * M)
                return jnp.where(here, near_ref[s, rows, :], far_ref[s, rows, :])

            lanes = s * GROUPS + h * (SPAN // GROUP)
            p, far = per_channel(pole, lanes), per_channel(across, lanes)
            handed = res_ref[:, s * SLICE + h * SPAN : s * SLICE + (h + 1) * SPAN] * p
            state, adjoint = got_ref[s, h * M : (h + 1) * M, :], got_ref[s, (2 + h) * M : (3 + h) * M, :]
            end, start = chosen(0), chosen(1)
            states.append(jnp.where(even, state, far * state + handed * end))
            adjoints.append(jnp.where(even, far * adjoint + handed * start, adjoint))
        more = dot(powers(rate_ref[s], False), spread(jnp.concatenate(states, 1)))
        mixed_out[0, :, cols] = (mixed_ref[:, cols] + more).astype(BF16)
        more = dot(powers(rate_ref[s], True), spread(jnp.concatenate(adjoints, 1)))
        grad_out[0, :, cols] = (grad_ref[:, cols] + more).astype(BF16)


def gather_kernel(pairs, all_ref, log_ref, res_out, rate_out):
    chunks = 2 * pairs

    def part(k, rows):
        return all_ref[2 * (k % pairs) + k // pairs, rows, :]

    for k in range(chunks):
        for h in range(2):
            res_out[:, k * SLICE + h * SPAN : k * SLICE + (h + 1) * SPAN] = part(k, slice(h * M, (h + 1) * M))
    width = min(SPAN, chunks * GROUPS)
    per = width // GROUPS
    rows = slice(2 * M, 3 * M)
    for j in range(chunks // per):
        parts = part(j * per, rows)
        for k in range(j * per + 1, (j + 1) * per):
            parts = parts + part(k, rows)
        cols = slice(j * width, (j + 1) * width)
        rate_out[:, cols] = -jnp.exp(log_ref[:, cols]) * parts[:, :width]


def local(signal, out_grad, residues, log_rates):
    channels = signal.shape[2]
    chunks, rows = lax.axis_size("seq"), lax.axis_size("batch")
    index = lax.axis_index("seq").astype(jnp.int32)
    pairs = chunks // 2
    core = lax.rem(index, 2)
    own = core * pairs + index // 2
    swap = [(i, i ^ 1) for i in range(chunks)]
    same_core = [[2 * j + c for j in range(pairs)] for c in range(2)]
    wide = min(WIDE, channels // 2)
    steps = channels // wide
    part = steps // 2
    block = wide // SLICE
    fwd, inv = (jnp.asarray(v) for v in transforms())
    params = pltpu.CompilerParams(vmem_limit_bytes=58 * 2**20)
    little = pltpu.CompilerParams(vmem_limit_bytes=8 * 2**20)
    vmem, smem = pl.BlockSpec(memory_space=pltpu.VMEM), pl.BlockSpec(memory_space=pltpu.SMEM)
    states_shape = jax.ShapeDtypeStruct((pairs, 11 * M, SPAN), F32)
    core_scalar = core[None]

    def whole(a):
        return pl.BlockSpec(a.shape, lambda i, *_: (0,) * a.ndim)

    def exchange(values):
        return lax.all_to_all(values, "seq", 0, 0, axis_index_groups=same_core, tiled=True)

    def other_core(values):
        return lax.ppermute(values, "seq", swap)

    def ends_and_lags(half, x, g, room):
        return pl.pallas_call(
            first_kernel,
            grid_spec=pltpu.PrefetchScalarGridSpec(
                num_scalar_prefetch=1,
                grid=(part,),
                in_specs=[
                    pl.BlockSpec((1, SPAN, wide), lambda i, at: (0, 0, at[0] * part + i)),
                    pl.BlockSpec((1, SPAN, wide), lambda i, at: (0, 0, at[0] * part + i)),
                    pl.BlockSpec((M, wide // GROUP), lambda i, at: (0, at[0] * part + i)),
                    pl.BlockSpec((M, wide), lambda i, at: (0, at[0] * part + i)),
                    whole(fwd),
                    whole(inv),
                ],
                out_specs=pl.BlockSpec((block, 13 * M, SPAN), lambda i, at: (i, 0, 0)),
            ),
            out_shape=jax.ShapeDtypeStruct((pairs, 13 * M, SPAN), F32),
            compiler_params=room,
            name="ends_and_lags",
        )(half, x, g, log_rates, residues, fwd, inv)

    away = ends_and_lags(1 - core_scalar, signal, out_grad, params)
    away, x2, g2 = lax.optimization_barrier((away, signal, out_grad))
    arrived = other_core(away)
    kept = ends_and_lags(core_scalar, x2, g2, pltpu.CompilerParams(vmem_limit_bytes=40 * 2**20))
    state_block = pl.BlockSpec((block, 11 * M, SPAN), lambda i, at: (i, 0, 0))
    edge_block = pl.BlockSpec((block, 4 * M, SPAN), lambda i, at: (i, 0, 0))
    edge_shape = jax.ShapeDtypeStruct((pairs, 4 * M, SPAN), F32)
    pair, mine, near = pl.pallas_call(
        pair_kernel,
        grid_spec=pltpu.PrefetchScalarGridSpec(
            num_scalar_prefetch=1,
            grid=(part,),
            in_specs=[
                pl.BlockSpec((block, 13 * M, SPAN), lambda i, at: (i, 0, 0)),
                pl.BlockSpec((block, 11 * M, SPAN), lambda i, at: (i, 0, 0)),
                pl.BlockSpec((M, wide), lambda i, at: (0, at[0] * part + i)),
            ],
            out_specs=[state_block, edge_block, edge_block],
        ),
        out_shape=[states_shape, edge_shape, edge_shape],
        compiler_params=little,
        name="join_pair",
    )(core_scalar, kept, arrived, residues)
    pair, later_rates, later_res = lax.optimization_barrier((pair, log_rates, residues))
    got = exchange(pair)

    decay_rate = jnp.exp(later_rates)
    rate_rows = jnp.broadcast_to(decay_rate.T.reshape(chunks, 1, SPAN), (chunks, M, SPAN))
    own_rate = jnp.repeat(lax.dynamic_slice_in_dim(decay_rate, own * GROUPS, GROUPS, 1), GROUP, axis=1)
    own_res = lax.dynamic_slice_in_dim(later_res, own * SLICE, SLICE, 1)

    work = SPAN * channels

    def convolutions(at, count, x, g, *earlier):
        kernel_blocks = [
            pl.BlockSpec((1, SPAN, wide), lambda i: (0, 0, at + i)),
            pl.BlockSpec((1, SPAN, wide), lambda i: (0, 0, at + i)),
            pl.BlockSpec((block, M, SPAN), lambda i: (at + i, 0, 0)),
            pl.BlockSpec((M, wide), lambda i: (0, at + i)),
            whole(fwd),
            whole(inv),
        ]
        return pl.pallas_call(
            second_kernel,
            grid=(count,),
            in_specs=kernel_blocks + [pl.BlockSpec(memory_space=pl.ANY)] * len(earlier),
            out_specs=[pl.BlockSpec((SPAN, wide), lambda i: (0, at + i))] * 2,
            out_shape=[jax.ShapeDtypeStruct((SPAN, channels), F32)] * 2,
            input_output_aliases={6: 0, 7: 1} if earlier else {},
            compiler_params=params,
            cost_estimate=pl.CostEstimate(flops=work * 300, bytes_accessed=work * 2, transcendentals=0),
            name="local_convolutions",
        )(x, g, rate_rows, residues, fwd, inv, *earlier)

    early = steps - max(1, steps // 4)
    mixed_part, grad_part = convolutions(0, early, signal, out_grad)
    got, mixed_part, grad_part = lax.optimization_barrier((got, mixed_part, grad_part))
    back = pl.pallas_call(
        functools.partial(carry_kernel, pairs),
        out_shape=jax.ShapeDtypeStruct((chunks, 4 * M, SPAN), F32),
        compiler_params=little,
        name="carries",
    )(got, own_rate, own_res)
    back, got, x3, g3, mine = lax.optimization_barrier((back, got, signal, out_grad, mine))
    carried = lax.all_to_all(back, "seq", 0, 0, tiled=True).reshape(pairs, 2, 4 * M, SPAN)
    sums = pl.pallas_call(
        functools.partial(sums_kernel, pairs, 1.0 / (rows * chunks * SPAN)),
        out_shape=jax.ShapeDtypeStruct((3 * M, SPAN), F32),
        in_specs=[smem, vmem, vmem, vmem],
        compiler_params=little,
        cost_estimate=pl.CostEstimate(flops=10**10, bytes_accessed=10**7, transcendentals=0),
        name="gradient_sums",
    )(own[None], got, own_rate, own_res)
    arriving = [lax.ppermute(sums, "batch", [(i, (i + k) % rows) for i in range(rows)]) for k in range(1, rows)]
    far = other_core(mine)
    mixed_part, grad_part = convolutions(early, steps - early, x3, g3, mixed_part, grad_part)

    def total_kernel(*refs):
        total = refs[0][...]
        for ref in refs[1:-1]:
            total = total + ref[...]
        for k in range(chunks):
            refs[-1][k] = total

    total = pl.pallas_call(
        total_kernel,
        out_shape=jax.ShapeDtypeStruct((chunks, 3 * M, SPAN), F32),
        compiler_params=little,
        name="total",
    )(sums, *arriving)
    carried, total, mixed_part, grad_part, far = lax.optimization_barrier((carried, total, mixed_part, grad_part, far))
    everyone = lax.all_to_all(total, "seq", 0, 0, tiled=True)

    flat_block = pl.BlockSpec((SPAN, wide), lambda i, at: (0, i))
    seq_block = pl.BlockSpec((1, SPAN, wide), lambda i, at: (0, 0, i))
    half_block = pl.BlockSpec((block, 4 * M, SPAN), lambda i, at: (lax.rem(i, part), 0, 0))
    mixed, grad_signal = pl.pallas_call(
        last_kernel,
        grid_spec=pltpu.PrefetchScalarGridSpec(
            num_scalar_prefetch=1,
            grid=(steps,),
            in_specs=[
                flat_block,
                flat_block,
                pl.BlockSpec((block, M, SPAN), lambda i, at: (i, 0, 0)),
                pl.BlockSpec((M, wide // GROUP), lambda i, at: (0, i)),
                pl.BlockSpec((M, wide), lambda i, at: (0, i)),
                pl.BlockSpec((block, None, 4 * M, SPAN), lambda i, at: (lax.rem(i, part), i // part, 0, 0)),
                half_block,
                half_block,
            ],
            out_specs=[seq_block, seq_block],
        ),
        out_shape=[jax.ShapeDtypeStruct(signal.shape, BF16)] * 2,
        compiler_params=params,
        cost_estimate=pl.CostEstimate(flops=work * 1600, bytes_accessed=work * 12, transcendentals=work),
        name="add_carries",
    )(core_scalar, mixed_part, grad_part, rate_rows, log_rates, residues, carried, near, far)
    grad_residues, grad_rates = pl.pallas_call(
        functools.partial(gather_kernel, pairs),
        out_shape=[jax.ShapeDtypeStruct(residues.shape, F32), jax.ShapeDtypeStruct(log_rates.shape, F32)],
        compiler_params=little,
        name="unpack",
    )(everyone, log_rates)
    return mixed, grad_signal, grad_residues, grad_rates


def solution(mesh):
    sharded = P("batch", "seq", None)
    return jax.shard_map(
        local,
        mesh=mesh,
        in_specs=(sharded, sharded, P(), P()),
        out_specs=(sharded, sharded, P(), P()),
        check_vma=False,
    )
```

```python
import functools

import jax
import jax.numpy as jnp
import numpy as np
from jax import lax
from jax.experimental import pallas as pl
from jax.experimental.pallas import tpu as pltpu
from jax.sharding import PartitionSpec as P

M = 8
GROUP = 16
SPAN = 128
SLICE = 256
GROUPS = SLICE // GROUP
WIDE = 2048
F32 = jnp.float32
BF16 = jnp.bfloat16


def split_np(values):
    high = values.astype(np.float32).astype(jnp.bfloat16)
    low = (values - high.astype(np.float64)).astype(np.float32).astype(jnp.bfloat16)
    return high, low


def transforms():
    time = np.arange(SPAN)
    angle = 2 * np.pi * np.outer(np.arange(SPAN) + 0.5, time) / (2 * SPAN)
    forward = np.concatenate([np.cos(angle), -np.sin(angle)], 0)
    inverse = np.concatenate([np.cos(angle.T), -np.sin(angle.T)], 1) / SPAN
    fh, fl = split_np(forward)
    ih, il = split_np(inverse)
    return np.concatenate([fh, fl], 1), np.concatenate([ih, il, ih], 1)


def split(values):
    high = values.astype(BF16)
    return high, (values - high.astype(F32)).astype(BF16)


def dot(a, b):
    return jnp.dot(a, b, preferred_element_type=F32)


def twice(values):
    return jnp.concatenate([values, values], 0)


def stacked(values):
    high, low = split(values)
    return jnp.concatenate([high, high, low], 0)


def lane_group(rows, lanes):
    return lax.broadcasted_iota(jnp.int32, (rows, lanes), 1) // GROUP


def spread(values):
    high = values.astype(BF16).astype(F32)
    low = values - high
    owner = lane_group(M, SLICE)

    def rows(part):
        return jnp.concatenate([jnp.where(owner == g, part, 0.0) for g in range(GROUPS)], 0).astype(BF16)

    top, bottom = rows(high), rows(low)
    return jnp.concatenate([top, top, bottom, bottom], 0)


def powers(rate_row, reverse):
    t = lax.broadcasted_iota(jnp.int32, (SPAN, SPAN), 0)
    t = (SPAN - 1 - t if reverse else t).astype(F32)
    high, low = split(jnp.exp(-rate_row[0:1, :] * t))
    return jnp.concatenate([high, low, high, low], 1)


def first_kernel(half_ref, x_ref, g_ref, log_ref, res_ref, fwd_ref, inv_ref, send_ref):
    x, g = x_ref[0], g_ref[0]
    xx, gg = twice(x), twice(g)
    forward = fwd_ref[...]
    xf = dot(forward, xx)
    gf = dot(forward, gg)
    xr, xi, gr, gi = xf[:SPAN], xf[SPAN:], gf[:SPAN], gf[SPAN:]
    lags = dot(inv_ref[...], stacked(jnp.concatenate([gr * xr + gi * xi, gi * xr - gr * xi], 0)))
    lag_high, lag_low = split(lags)
    lag_high, lag_low = twice(lag_high), twice(lag_low)
    flip = jnp.where(lax.broadcasted_iota(jnp.int32, (SPAN, SPAN), 0) + lax.broadcasted_iota(jnp.int32, (SPAN, SPAN), 1) == SPAN - 1, 1.0, 0.0).astype(BF16)
    backward = twice(dot(flip, x).astype(BF16))
    lag = lax.broadcasted_iota(jnp.int32, (SPAN, SPAN), 1).astype(F32)
    half = SPAN // GROUP
    owner = lane_group(M, SPAN)
    row = lax.broadcasted_iota(jnp.int32, (SPAN, SPAN), 0) // GROUP
    col = lax.broadcasted_iota(jnp.int32, (SPAN, SPAN), 1)

    def pick(values, q):
        at = q * half * M
        chosen = values[at : at + M]
        for k in range(1, half):
            chosen = jnp.where(owner == k, values[at + k * M : at + (k + 1) * M], chosen)
        return chosen

    count = log_ref.shape[1] // GROUPS
    rate = jnp.exp(log_ref[...])
    weighted = ([], [])
    for s in range(count):
        at = s * GROUPS
        rates = jnp.concatenate([jnp.broadcast_to(rate[:, k : k + 1], (M, SPAN)) for k in range(at, at + GROUPS)], 0)
        early = jnp.exp(-rates * lag)
        for h in range(2):
            send_ref[s, (11 + h) * M : (12 + h) * M, :] = pick(rates[h * half * M : (h + 1) * half * M], 0)
        for h in range(2):
            rows = slice(h * half * M, (h + 1) * half * M)
            cols = slice(s * SLICE + h * SPAN, s * SLICE + (h + 1) * SPAN)
            eh, el = split(jnp.concatenate([early[rows], lag[rows] * early[rows]], 0))
            found = dot(
                jnp.concatenate([eh, el], 1),
                jnp.concatenate([backward[:, cols], gg[:, cols], lag_high[:, cols], lag_low[:, cols]], 1),
            )
            ends, starts = found[:, :SPAN], found[:, SPAN : 2 * SPAN]
            sums = found[:, 2 * SPAN : 3 * SPAN] + found[:, 3 * SPAN :]
            for q, values in enumerate((pick(ends, 0), pick(starts, 0), pick(ends, 1), pick(starts, 1), pick(sums, 0))):
                at = (2 * q + h) * M
                send_ref[s, at : at + M, :] = values
            weighted[h].append(res_ref[:, cols] * pick(sums, 1))
    total = jnp.zeros((count * M, SPAN), F32)
    for h in range(2):
        place = jnp.where(row + h * half == col, 1.0, 0.0).astype(BF16)
        wh, wl = split(jnp.concatenate(weighted[h], 0))
        total = total + dot(jnp.concatenate([wh, wl], 1), twice(place))
    for s in range(count):
        send_ref[s, 10 * M : 11 * M, :] = total[s * M : (s + 1) * M]


def second_kernel(x_ref, g_ref, rate_ref, res_ref, fwd_ref, inv_ref, *rest):
    mixed_ref, grad_ref = rest[-2:]
    forward = fwd_ref[...]
    taps = [
        dot(powers(rate_ref[s], False), spread(res_ref[:, s * SLICE : (s + 1) * SLICE]))
        for s in range(rate_ref.shape[0])
    ]
    high, low = split(jnp.concatenate(taps, 1))
    kf = dot(forward, twice(high)) + dot(fwd_ref[:, :SPAN], low)
    xf = dot(forward, twice(x_ref[0]))
    gf = dot(forward, twice(g_ref[0]))
    kr, ki, xr, xi, gr, gi = kf[:SPAN], kf[SPAN:], xf[:SPAN], xf[SPAN:], gf[:SPAN], gf[SPAN:]
    mixed_ref[...] = dot(inv_ref[...], stacked(jnp.concatenate([kr * xr - ki * xi, kr * xi + ki * xr], 0)))
    grad_ref[...] = dot(inv_ref[...], stacked(jnp.concatenate([kr * gr + ki * gi, kr * gi - ki * gr], 0)))


def per_channel(values, at):
    owner = lane_group(M, SPAN)
    chosen = jnp.broadcast_to(values[:, at : at + 1], (M, SPAN))
    for k in range(1, SPAN // GROUP):
        chosen = jnp.where(owner == k, values[:, at + k : at + k + 1], chosen)
    return chosen


def placed(parts, h, offset):
    row = lax.broadcasted_iota(jnp.int32, (SPAN, SPAN), 0) // GROUP
    col = lax.broadcasted_iota(jnp.int32, (SPAN, SPAN), 1)
    place = jnp.where(row + (h * (SPAN // GROUP) + offset) == col, 1.0, 0.0).astype(BF16)
    high, low = split(parts)
    return dot(jnp.concatenate([high, low], 1), twice(place))


def pair_kernel(core_ref, kept_ref, arrived_ref, res_ref, pair_ref, mine_ref, near_ref):
    even = core_ref[0] == 0
    count = kept_ref.shape[0]
    mine_ref[...] = kept_ref[:, : 4 * M, :]
    near_ref[...] = arrived_ref[:, : 4 * M, :]
    weighted = ([], [])
    for s in range(count):
        for h in range(2):

            def both(q):
                rows = slice((2 * q + h) * M, (2 * q + h + 1) * M)
                kept, arrived = kept_ref[s, rows, :], arrived_ref[s, rows, :]
                return jnp.where(even, kept, arrived), jnp.where(even, arrived, kept)

            def put(q, values):
                pair_ref[s, (2 * q + h) * M : (2 * q + h + 1) * M, :] = values

            rate = kept_ref[s, (11 + h) * M : (12 + h) * M, :]
            p, far = jnp.exp(-rate), jnp.exp(-rate * SPAN)
            (s1, s2), (t1, t2), (u1, u2), (w1, w2), (r1, r2) = (both(q) for q in range(5))
            put(0, far * s1 + s2)
            put(1, t1 + far * t2)
            put(2, far * (u1 + SPAN * s1) + u2)
            put(3, w1 + far * (w2 + SPAN * t2))
            put(4, r1 + r2 + p * s1 * t2)
            cols = slice(s * SLICE + h * SPAN, s * SLICE + (h + 1) * SPAN)
            weighted[h].append(res_ref[:, cols] * p * (s1 * (w2 + t2) + u1 * t2))
    total = placed(jnp.concatenate(weighted[0], 0), 0, 0) + placed(jnp.concatenate(weighted[1], 0), 1, 0)
    for s in range(count):
        rows = slice(10 * M, 11 * M)
        pair_ref[s, rows, :] = kept_ref[s, rows, :] + arrived_ref[s, rows, :] + total[s * M : (s + 1) * M]


def carry_kernel(pairs, index_ref, got_ref, rate_ref, res_ref, back_ref):
    for h in range(2):
        cols = slice(h * SPAN, (h + 1) * SPAN)
        rate = rate_ref[:, cols]
        across = jnp.exp(-rate * (2 * SPAN))
        handed = res_ref[:, pl.ds(pl.multiple_of(index_ref[0] * SLICE + h * SPAN, SPAN), SPAN)] * jnp.exp(-rate)
        state = jnp.zeros((M, SPAN), F32)
        adjoint = state
        for k in range(pairs):
            last = pairs - 1 - k
            for c in range(2):
                back_ref[2 * k + c, h * M : (h + 1) * M, :] = handed * state
                back_ref[2 * last + c, (2 + h) * M : (3 + h) * M, :] = handed * adjoint
            state = across * state + got_ref[k, h * M : (h + 1) * M, :]
            adjoint = across * adjoint + got_ref[last, (2 + h) * M : (3 + h) * M, :]


def sums_kernel(pairs, scale, index_ref, got_ref, rate_ref, res_ref, sums_ref):
    offset = lax.rem(index_ref[0], SPAN // GROUPS) * GROUPS
    rate_sum = jnp.zeros((M, SPAN), F32)
    for k in range(pairs):
        rate_sum = rate_sum + got_ref[k, 10 * M : 11 * M, :]
    rate_sum = pltpu.roll(rate_sum, offset, 1)
    for h in range(2):
        cols = slice(h * SPAN, (h + 1) * SPAN)
        rate = rate_ref[:, cols]
        res = res_ref[:, pl.ds(pl.multiple_of(index_ref[0] * SLICE + h * SPAN, SPAN), SPAN)]
        pole = jnp.exp(-rate)
        across = jnp.exp(-rate * (2 * SPAN))

        def part(k, q):
            at = (2 * q + h) * M
            return got_ref[k, at : at + M, :]

        zero = jnp.zeros((M, SPAN), F32)
        state, moment, res_part, res_carry, rate_carry = zero, zero, zero, zero, zero
        for k in range(pairs):
            start = part(k, 1)
            res_part = res_part + part(k, 4)
            res_carry = res_carry + state * start
            rate_carry = rate_carry + state * (part(k, 3) + start) + moment * start
            moment = across * (moment + 2 * SPAN * state) + part(k, 2)
            state = across * state + part(k, 0)
        sums_ref[h * M : (h + 1) * M, :] = scale * (res_part + pole * res_carry)
        rate_sum = rate_sum + placed(res * pole * rate_carry, h, offset)
    sums_ref[2 * M : 3 * M, :] = scale * rate_sum


def last_kernel(
    core_ref, mixed_ref, grad_ref, rate_ref, log_ref, res_ref, got_ref, near_ref, far_ref, mixed_out, grad_out
):
    core = core_ref[0]
    even = core == 0
    here = pl.program_id(0) // (pl.num_programs(0) // 2) == core
    rate = jnp.exp(log_ref[...])
    pole, across = jnp.exp(-rate), jnp.exp(-rate * SPAN)
    for s in range(rate_ref.shape[0]):
        cols = slice(s * SLICE, (s + 1) * SLICE)
        states, adjoints = [], []
        for h in range(2):

            def chosen(q):
                rows = slice((2 * q + h) * M, (2 * q + h + 1) * M)
                return jnp.where(here, near_ref[s, rows, :], far_ref[s, rows, :])

            lanes = s * GROUPS + h * (SPAN // GROUP)
            p, far = per_channel(pole, lanes), per_channel(across, lanes)
            handed = res_ref[:, s * SLICE + h * SPAN : s * SLICE + (h + 1) * SPAN] * p
            state, adjoint = got_ref[s, h * M : (h + 1) * M, :], got_ref[s, (2 + h) * M : (3 + h) * M, :]
            end, start = chosen(0), chosen(1)
            states.append(jnp.where(even, state, far * state + handed * end))
            adjoints.append(jnp.where(even, far * adjoint + handed * start, adjoint))
        more = dot(powers(rate_ref[s], False), spread(jnp.concatenate(states, 1)))
        mixed_out[0, :, cols] = (mixed_ref[:, cols] + more).astype(BF16)
        more = dot(powers(rate_ref[s], True), spread(jnp.concatenate(adjoints, 1)))
        grad_out[0, :, cols] = (grad_ref[:, cols] + more).astype(BF16)


def gather_kernel(pairs, all_ref, log_ref, res_out, rate_out):
    chunks = 2 * pairs

    def part(k, rows):
        return all_ref[2 * (k % pairs) + k // pairs, rows, :]

    for k in range(chunks):
        for h in range(2):
            res_out[:, k * SLICE + h * SPAN : k * SLICE + (h + 1) * SPAN] = part(k, slice(h * M, (h + 1) * M))
    width = min(SPAN, chunks * GROUPS)
    per = width // GROUPS
    rows = slice(2 * M, 3 * M)
    for j in range(chunks // per):
        parts = part(j * per, rows)
        for k in range(j * per + 1, (j + 1) * per):
            parts = parts + part(k, rows)
        cols = slice(j * width, (j + 1) * width)
        rate_out[:, cols] = -jnp.exp(log_ref[:, cols]) * parts[:, :width]


def local(signal, out_grad, residues, log_rates):
    channels = signal.shape[2]
    chunks, rows = lax.axis_size("seq"), lax.axis_size("batch")
    index = lax.axis_index("seq").astype(jnp.int32)
    pairs = chunks // 2
    core = lax.rem(index, 2)
    own = core * pairs + index // 2
    swap = [(i, i ^ 1) for i in range(chunks)]
    same_core = [[2 * j + c for j in range(pairs)] for c in range(2)]
    wide = min(WIDE, channels // 2)
    steps = channels // wide
    part = steps // 2
    block = wide // SLICE
    fwd, inv = (jnp.asarray(v) for v in transforms())
    params = pltpu.CompilerParams(vmem_limit_bytes=58 * 2**20)
    little = pltpu.CompilerParams(vmem_limit_bytes=8 * 2**20)
    vmem, smem = pl.BlockSpec(memory_space=pltpu.VMEM), pl.BlockSpec(memory_space=pltpu.SMEM)
    states_shape = jax.ShapeDtypeStruct((pairs, 11 * M, SPAN), F32)
    core_scalar = core[None]

    def whole(a):
        return pl.BlockSpec(a.shape, lambda i, *_: (0,) * a.ndim)

    def exchange(values):
        return lax.all_to_all(values, "seq", 0, 0, axis_index_groups=same_core, tiled=True)

    def other_core(values):
        return lax.ppermute(values, "seq", swap)

    def ends_and_lags(half, x, g, room):
        return pl.pallas_call(
            first_kernel,
            grid_spec=pltpu.PrefetchScalarGridSpec(
                num_scalar_prefetch=1,
                grid=(part,),
                in_specs=[
                    pl.BlockSpec((1, SPAN, wide), lambda i, at: (0, 0, at[0] * part + i)),
                    pl.BlockSpec((1, SPAN, wide), lambda i, at: (0, 0, at[0] * part + i)),
                    pl.BlockSpec((M, wide // GROUP), lambda i, at: (0, at[0] * part + i)),
                    pl.BlockSpec((M, wide), lambda i, at: (0, at[0] * part + i)),
                    whole(fwd),
                    whole(inv),
                ],
                out_specs=pl.BlockSpec((block, 13 * M, SPAN), lambda i, at: (i, 0, 0)),
            ),
            out_shape=jax.ShapeDtypeStruct((pairs, 13 * M, SPAN), F32),
            compiler_params=room,
            name="ends_and_lags",
        )(half, x, g, log_rates, residues, fwd, inv)

    away = ends_and_lags(1 - core_scalar, signal, out_grad, params)
    away, x2, g2 = lax.optimization_barrier((away, signal, out_grad))
    arrived = other_core(away)
    kept = ends_and_lags(core_scalar, x2, g2, pltpu.CompilerParams(vmem_limit_bytes=40 * 2**20))
    state_block = pl.BlockSpec((block, 11 * M, SPAN), lambda i, at: (i, 0, 0))
    edge_block = pl.BlockSpec((block, 4 * M, SPAN), lambda i, at: (i, 0, 0))
    edge_shape = jax.ShapeDtypeStruct((pairs, 4 * M, SPAN), F32)
    pair, mine, near = pl.pallas_call(
        pair_kernel,
        grid_spec=pltpu.PrefetchScalarGridSpec(
            num_scalar_prefetch=1,
            grid=(part,),
            in_specs=[
                pl.BlockSpec((block, 13 * M, SPAN), lambda i, at: (i, 0, 0)),
                pl.BlockSpec((block, 11 * M, SPAN), lambda i, at: (i, 0, 0)),
                pl.BlockSpec((M, wide), lambda i, at: (0, at[0] * part + i)),
            ],
            out_specs=[state_block, edge_block, edge_block],
        ),
        out_shape=[states_shape, edge_shape, edge_shape],
        compiler_params=little,
        name="join_pair",
    )(core_scalar, kept, arrived, residues)
    pair, later_rates = lax.optimization_barrier((pair, log_rates))
    got = exchange(pair)

    decay_rate = jnp.exp(later_rates)
    rate_rows = decay_rate.T.reshape(chunks, 1, SPAN)
    own_rate = jnp.repeat(lax.dynamic_slice_in_dim(decay_rate, own * GROUPS, GROUPS, 1), GROUP, axis=1)

    work = SPAN * channels

    def convolutions(at, count, x, g, *earlier):
        kernel_blocks = [
            pl.BlockSpec((1, SPAN, wide), lambda i: (0, 0, at + i)),
            pl.BlockSpec((1, SPAN, wide), lambda i: (0, 0, at + i)),
            pl.BlockSpec((block, 1, SPAN), lambda i: (at + i, 0, 0)),
            pl.BlockSpec((M, wide), lambda i: (0, at + i)),
            whole(fwd),
            whole(inv),
        ]
        return pl.pallas_call(
            second_kernel,
            grid=(count,),
            in_specs=kernel_blocks + [pl.BlockSpec(memory_space=pl.ANY)] * len(earlier),
            out_specs=[pl.BlockSpec((SPAN, wide), lambda i: (0, at + i))] * 2,
            out_shape=[jax.ShapeDtypeStruct((SPAN, channels), F32)] * 2,
            input_output_aliases={6: 0, 7: 1} if earlier else {},
            compiler_params=params,
            cost_estimate=pl.CostEstimate(flops=work * 300, bytes_accessed=work * 2, transcendentals=0),
            name="local_convolutions",
        )(x, g, rate_rows, residues, fwd, inv, *earlier)

    early = steps - max(1, steps // 4)
    mixed_part, grad_part = convolutions(0, early, signal, out_grad)
    got, mixed_part, grad_part = lax.optimization_barrier((got, mixed_part, grad_part))
    back = pl.pallas_call(
        functools.partial(carry_kernel, pairs),
        out_shape=jax.ShapeDtypeStruct((chunks, 4 * M, SPAN), F32),
        in_specs=[smem, vmem, vmem, vmem],
        compiler_params=little,
        name="carries",
    )(own[None], got, own_rate, residues)
    back, got, x3, g3, mine = lax.optimization_barrier((back, got, signal, out_grad, mine))
    carried = lax.all_to_all(back, "seq", 0, 0, tiled=True).reshape(pairs, 2, 4 * M, SPAN)
    sums = pl.pallas_call(
        functools.partial(sums_kernel, pairs, 1.0 / (rows * chunks * SPAN)),
        out_shape=jax.ShapeDtypeStruct((3 * M, SPAN), F32),
        in_specs=[smem, vmem, vmem, vmem],
        compiler_params=little,
        cost_estimate=pl.CostEstimate(flops=10**10, bytes_accessed=10**7, transcendentals=0),
        name="gradient_sums",
    )(own[None], got, own_rate, residues)
    arriving = [lax.ppermute(sums, "batch", [(i, (i + k) % rows) for i in range(rows)]) for k in range(1, rows)]
    far = other_core(mine)
    mixed_part, grad_part = convolutions(early, steps - early, x3, g3, mixed_part, grad_part)

    def total_kernel(*refs):
        total = refs[0][...]
        for ref in refs[1:-1]:
            total = total + ref[...]
        for k in range(chunks):
            refs[-1][k] = total

    total = pl.pallas_call(
        total_kernel,
        out_shape=jax.ShapeDtypeStruct((chunks, 3 * M, SPAN), F32),
        compiler_params=little,
        name="total",
    )(sums, *arriving)
    carried, total, mixed_part, grad_part, far = lax.optimization_barrier((carried, total, mixed_part, grad_part, far))
    everyone = lax.all_to_all(total, "seq", 0, 0, tiled=True)

    flat_block = pl.BlockSpec((SPAN, wide), lambda i, at: (0, i))
    seq_block = pl.BlockSpec((1, SPAN, wide), lambda i, at: (0, 0, i))
    half_block = pl.BlockSpec((block, 4 * M, SPAN), lambda i, at: (lax.rem(i, part), 0, 0))
    mixed, grad_signal = pl.pallas_call(
        last_kernel,
        grid_spec=pltpu.PrefetchScalarGridSpec(
            num_scalar_prefetch=1,
            grid=(steps,),
            in_specs=[
                flat_block,
                flat_block,
                pl.BlockSpec((block, 1, SPAN), lambda i, at: (i, 0, 0)),
                pl.BlockSpec((M, wide // GROUP), lambda i, at: (0, i)),
                pl.BlockSpec((M, wide), lambda i, at: (0, i)),
                pl.BlockSpec((block, None, 4 * M, SPAN), lambda i, at: (lax.rem(i, part), i // part, 0, 0)),
                half_block,
                half_block,
            ],
            out_specs=[seq_block, seq_block],
        ),
        out_shape=[jax.ShapeDtypeStruct(signal.shape, BF16)] * 2,
        compiler_params=params,
        cost_estimate=pl.CostEstimate(flops=work * 1600, bytes_accessed=work * 12, transcendentals=work),
        name="add_carries",
    )(core_scalar, mixed_part, grad_part, rate_rows, log_rates, residues, carried, near, far)
    grad_residues, grad_rates = pl.pallas_call(
        functools.partial(gather_kernel, pairs),
        out_shape=[jax.ShapeDtypeStruct(residues.shape, F32), jax.ShapeDtypeStruct(log_rates.shape, F32)],
        compiler_params=little,
        name="unpack",
    )(everyone, log_rates)
    return mixed, grad_signal, grad_residues, grad_rates


def solution(mesh):
    sharded = P("batch", "seq", None)
    return jax.shard_map(
        local,
        mesh=mesh,
        in_specs=(sharded, sharded, P(), P()),
        out_specs=(sharded, sharded, P(), P()),
        check_vma=False,
    )
```

```python
import functools

import jax
import jax.numpy as jnp
import numpy as np
from jax import lax
from jax.experimental import pallas as pl
from jax.experimental.pallas import tpu as pltpu
from jax.sharding import PartitionSpec as P

M = 8
GROUP = 16
SPAN = 128
SLICE = 256
GROUPS = SLICE // GROUP
WIDE = 2048
F32 = jnp.float32
BF16 = jnp.bfloat16


def split_np(values):
    high = values.astype(np.float32).astype(jnp.bfloat16)
    low = (values - high.astype(np.float64)).astype(np.float32).astype(jnp.bfloat16)
    return high, low


def transforms():
    time = np.arange(SPAN)
    angle = 2 * np.pi * np.outer(np.arange(SPAN) + 0.5, time) / (2 * SPAN)
    forward = np.concatenate([np.cos(angle), -np.sin(angle)], 0)
    inverse = np.concatenate([np.cos(angle.T), -np.sin(angle.T)], 1) / SPAN
    fh, fl = split_np(forward)
    ih, il = split_np(inverse)
    return np.concatenate([fh, fl], 1), np.concatenate([ih, il, ih], 1)


def split(values):
    high = values.astype(BF16)
    return high, (values - high.astype(F32)).astype(BF16)


def dot(a, b):
    return jnp.dot(a, b, preferred_element_type=F32)


def twice(values):
    return jnp.concatenate([values, values], 0)


def stacked(values):
    high, low = split(values)
    return jnp.concatenate([high, high, low], 0)


def lane_group(rows, lanes):
    return lax.broadcasted_iota(jnp.int32, (rows, lanes), 1) // GROUP


def spread(values):
    high = values.astype(BF16).astype(F32)
    low = values - high
    owner = lane_group(M, SLICE)

    def rows(part):
        return jnp.concatenate([jnp.where(owner == g, part, 0.0) for g in range(GROUPS)], 0).astype(BF16)

    top, bottom = rows(high), rows(low)
    return jnp.concatenate([top, top, bottom, bottom], 0)


def powers(rate_row, reverse):
    t = lax.broadcasted_iota(jnp.int32, (SPAN, SPAN), 0)
    t = (SPAN - 1 - t if reverse else t).astype(F32)
    high, low = split(jnp.exp(-rate_row[0:1, :] * t))
    return jnp.concatenate([high, low, high, low], 1)


def first_kernel(half_ref, x_ref, g_ref, log_ref, res_ref, fwd_ref, inv_ref, send_ref):
    x, g = x_ref[0], g_ref[0]
    xx, gg = twice(x), twice(g)
    forward = fwd_ref[...]
    xf = dot(forward, xx)
    gf = dot(forward, gg)
    xr, xi, gr, gi = xf[:SPAN], xf[SPAN:], gf[:SPAN], gf[SPAN:]
    lags = dot(inv_ref[...], stacked(jnp.concatenate([gr * xr + gi * xi, gi * xr - gr * xi], 0)))
    lag_high, lag_low = split(lags)
    lag_high, lag_low = twice(lag_high), twice(lag_low)
    flip = jnp.where(lax.broadcasted_iota(jnp.int32, (SPAN, SPAN), 0) + lax.broadcasted_iota(jnp.int32, (SPAN, SPAN), 1) == SPAN - 1, 1.0, 0.0).astype(BF16)
    backward = twice(dot(flip, x).astype(BF16))
    lag = lax.broadcasted_iota(jnp.int32, (SPAN, SPAN), 1).astype(F32)
    half = SPAN // GROUP
    owner = lane_group(M, SPAN)
    row = lax.broadcasted_iota(jnp.int32, (SPAN, SPAN), 0) // GROUP
    col = lax.broadcasted_iota(jnp.int32, (SPAN, SPAN), 1)

    def pick(values, q):
        at = q * half * M
        chosen = values[at : at + M]
        for k in range(1, half):
            chosen = jnp.where(owner == k, values[at + k * M : at + (k + 1) * M], chosen)
        return chosen

    count = log_ref.shape[1] // GROUPS
    rate = jnp.exp(log_ref[...])
    weighted = ([], [])
    for s in range(count):
        at = s * GROUPS
        rates = jnp.concatenate([jnp.broadcast_to(rate[:, k : k + 1], (M, SPAN)) for k in range(at, at + GROUPS)], 0)
        early = jnp.exp(-rates * lag)
        for h in range(2):
            send_ref[s, (11 + h) * M : (12 + h) * M, :] = pick(rates[h * half * M : (h + 1) * half * M], 0)
        for h in range(2):
            rows = slice(h * half * M, (h + 1) * half * M)
            cols = slice(s * SLICE + h * SPAN, s * SLICE + (h + 1) * SPAN)
            eh, el = split(jnp.concatenate([early[rows], lag[rows] * early[rows]], 0))
            found = dot(
                jnp.concatenate([eh, el], 1),
                jnp.concatenate([backward[:, cols], gg[:, cols], lag_high[:, cols], lag_low[:, cols]], 1),
            )
            ends, starts = found[:, :SPAN], found[:, SPAN : 2 * SPAN]
            sums = found[:, 2 * SPAN : 3 * SPAN] + found[:, 3 * SPAN :]
            for q, values in enumerate((pick(ends, 0), pick(starts, 0), pick(ends, 1), pick(starts, 1), pick(sums, 0))):
                at = (2 * q + h) * M
                send_ref[s, at : at + M, :] = values
            weighted[h].append(res_ref[:, cols] * pick(sums, 1))
    total = jnp.zeros((count * M, SPAN), F32)
    for h in range(2):
        place = jnp.where(row + h * half == col, 1.0, 0.0).astype(BF16)
        wh, wl = split(jnp.concatenate(weighted[h], 0))
        total = total + dot(jnp.concatenate([wh, wl], 1), twice(place))
    for s in range(count):
        send_ref[s, 10 * M : 11 * M, :] = total[s * M : (s + 1) * M]


def second_kernel(x_ref, g_ref, rate_ref, res_ref, fwd_ref, inv_ref, *rest):
    mixed_ref, grad_ref = rest[-2:]
    forward = fwd_ref[...]
    taps = [
        dot(powers(rate_ref[s], False), spread(res_ref[:, s * SLICE : (s + 1) * SLICE]))
        for s in range(rate_ref.shape[0])
    ]
    high, low = split(jnp.concatenate(taps, 1))
    kf = dot(forward, twice(high)) + dot(fwd_ref[:, :SPAN], low)
    xf = dot(forward, twice(x_ref[0]))
    gf = dot(forward, twice(g_ref[0]))
    kr, ki, xr, xi, gr, gi = kf[:SPAN], kf[SPAN:], xf[:SPAN], xf[SPAN:], gf[:SPAN], gf[SPAN:]
    mixed_ref[...] = dot(inv_ref[...], stacked(jnp.concatenate([kr * xr - ki * xi, kr * xi + ki * xr], 0)))
    grad_ref[...] = dot(inv_ref[...], stacked(jnp.concatenate([kr * gr + ki * gi, kr * gi - ki * gr], 0)))


def per_channel(values, at):
    owner = lane_group(M, SPAN)
    chosen = jnp.broadcast_to(values[:, at : at + 1], (M, SPAN))
    for k in range(1, SPAN // GROUP):
        chosen = jnp.where(owner == k, values[:, at + k : at + k + 1], chosen)
    return chosen


def placed(parts, h, offset):
    row = lax.broadcasted_iota(jnp.int32, (SPAN, SPAN), 0) // GROUP
    col = lax.broadcasted_iota(jnp.int32, (SPAN, SPAN), 1)
    place = jnp.where(row + (h * (SPAN // GROUP) + offset) == col, 1.0, 0.0).astype(BF16)
    high, low = split(parts)
    return dot(jnp.concatenate([high, low], 1), twice(place))


def pair_kernel(core_ref, kept_ref, arrived_ref, res_ref, pair_ref, mine_ref, near_ref):
    even = core_ref[0] == 0
    count = kept_ref.shape[0]
    mine_ref[...] = kept_ref[:, : 4 * M, :]
    near_ref[...] = arrived_ref[:, : 4 * M, :]
    weighted = ([], [])
    for s in range(count):
        for h in range(2):

            def both(q):
                rows = slice((2 * q + h) * M, (2 * q + h + 1) * M)
                kept, arrived = kept_ref[s, rows, :], arrived_ref[s, rows, :]
                return jnp.where(even, kept, arrived), jnp.where(even, arrived, kept)

            def put(q, values):
                pair_ref[s, (2 * q + h) * M : (2 * q + h + 1) * M, :] = values

            rate = kept_ref[s, (11 + h) * M : (12 + h) * M, :]
            p, far = jnp.exp(-rate), jnp.exp(-rate * SPAN)
            (s1, s2), (t1, t2), (u1, u2), (w1, w2), (r1, r2) = (both(q) for q in range(5))
            put(0, far * s1 + s2)
            put(1, t1 + far * t2)
            put(2, far * (u1 + SPAN * s1) + u2)
            put(3, w1 + far * (w2 + SPAN * t2))
            put(4, r1 + r2 + p * s1 * t2)
            cols = slice(s * SLICE + h * SPAN, s * SLICE + (h + 1) * SPAN)
            weighted[h].append(res_ref[:, cols] * p * (s1 * (w2 + t2) + u1 * t2))
    total = placed(jnp.concatenate(weighted[0], 0), 0, 0) + placed(jnp.concatenate(weighted[1], 0), 1, 0)
    for s in range(count):
        rows = slice(10 * M, 11 * M)
        pair_ref[s, rows, :] = kept_ref[s, rows, :] + arrived_ref[s, rows, :] + total[s * M : (s + 1) * M]


def carry_kernel(pairs, index_ref, got_ref, rate_ref, res_ref, back_ref):
    for h in range(2):
        cols = slice(h * SPAN, (h + 1) * SPAN)
        rate = rate_ref[:, cols]
        across = jnp.exp(-rate * (2 * SPAN))
        handed = res_ref[:, pl.ds(pl.multiple_of(index_ref[0] * SLICE + h * SPAN, SPAN), SPAN)] * jnp.exp(-rate)
        state = jnp.zeros((M, SPAN), F32)
        adjoint = state
        for k in range(pairs):
            last = pairs - 1 - k
            for c in range(2):
                back_ref[2 * k + c, h * M : (h + 1) * M, :] = handed * state
                back_ref[2 * last + c, (2 + h) * M : (3 + h) * M, :] = handed * adjoint
            state = across * state + got_ref[k, h * M : (h + 1) * M, :]
            adjoint = across * adjoint + got_ref[last, (2 + h) * M : (3 + h) * M, :]


def sums_kernel(pairs, scale, index_ref, got_ref, rate_ref, res_ref, sums_ref):
    offset = lax.rem(index_ref[0], SPAN // GROUPS) * GROUPS
    rate_sum = jnp.zeros((M, SPAN), F32)
    for k in range(pairs):
        rate_sum = rate_sum + got_ref[k, 10 * M : 11 * M, :]
    rate_sum = pltpu.roll(rate_sum, offset, 1)
    for h in range(2):
        cols = slice(h * SPAN, (h + 1) * SPAN)
        rate = rate_ref[:, cols]
        res = res_ref[:, pl.ds(pl.multiple_of(index_ref[0] * SLICE + h * SPAN, SPAN), SPAN)]
        pole = jnp.exp(-rate)
        across = jnp.exp(-rate * (2 * SPAN))

        def part(k, q):
            at = (2 * q + h) * M
            return got_ref[k, at : at + M, :]

        zero = jnp.zeros((M, SPAN), F32)
        state, moment, res_part, res_carry, rate_carry = zero, zero, zero, zero, zero
        for k in range(pairs):
            start = part(k, 1)
            res_part = res_part + part(k, 4)
            res_carry = res_carry + state * start
            rate_carry = rate_carry + state * (part(k, 3) + start) + moment * start
            moment = across * (moment + 2 * SPAN * state) + part(k, 2)
            state = across * state + part(k, 0)
        sums_ref[h * M : (h + 1) * M, :] = scale * (res_part + pole * res_carry)
        rate_sum = rate_sum + placed(res * pole * rate_carry, h, offset)
    sums_ref[2 * M : 3 * M, :] = scale * rate_sum


def last_kernel(
    core_ref, mixed_ref, grad_ref, rate_ref, log_ref, res_ref, got_ref, near_ref, far_ref, mixed_out, grad_out
):
    core = core_ref[0]
    even = core == 0
    here = pl.program_id(0) // (pl.num_programs(0) // 2) == core
    rate = jnp.exp(log_ref[...])
    pole, across = jnp.exp(-rate), jnp.exp(-rate * SPAN)
    for s in range(rate_ref.shape[0]):
        cols = slice(s * SLICE, (s + 1) * SLICE)
        states, adjoints = [], []
        for h in range(2):

            def chosen(q):
                rows = slice((2 * q + h) * M, (2 * q + h + 1) * M)
                return jnp.where(here, near_ref[s, rows, :], far_ref[s, rows, :])

            lanes = s * GROUPS + h * (SPAN // GROUP)
            p, far = per_channel(pole, lanes), per_channel(across, lanes)
            handed = res_ref[:, s * SLICE + h * SPAN : s * SLICE + (h + 1) * SPAN] * p
            state, adjoint = got_ref[s, h * M : (h + 1) * M, :], got_ref[s, (2 + h) * M : (3 + h) * M, :]
            end, start = chosen(0), chosen(1)
            states.append(jnp.where(even, state, far * state + handed * end))
            adjoints.append(jnp.where(even, far * adjoint + handed * start, adjoint))
        more = dot(powers(rate_ref[s], False), spread(jnp.concatenate(states, 1)))
        mixed_out[0, :, cols] = (mixed_ref[:, cols] + more).astype(BF16)
        more = dot(powers(rate_ref[s], True), spread(jnp.concatenate(adjoints, 1)))
        grad_out[0, :, cols] = (grad_ref[:, cols] + more).astype(BF16)


def gather_kernel(pairs, all_ref, log_ref, res_out, rate_out):
    chunks = 2 * pairs

    def part(k, rows):
        return all_ref[2 * (k % pairs) + k // pairs, rows, :]

    for k in range(chunks):
        for h in range(2):
            res_out[:, k * SLICE + h * SPAN : k * SLICE + (h + 1) * SPAN] = part(k, slice(h * M, (h + 1) * M))
    width = min(SPAN, chunks * GROUPS)
    per = width // GROUPS
    rows = slice(2 * M, 3 * M)
    for j in range(chunks // per):
        parts = part(j * per, rows)
        for k in range(j * per + 1, (j + 1) * per):
            parts = parts + part(k, rows)
        cols = slice(j * width, (j + 1) * width)
        rate_out[:, cols] = -jnp.exp(log_ref[:, cols]) * parts[:, :width]


def local(signal, out_grad, residues, log_rates):
    channels = signal.shape[2]
    chunks, rows = lax.axis_size("seq"), lax.axis_size("batch")
    index = lax.axis_index("seq").astype(jnp.int32)
    pairs = chunks // 2
    core = lax.rem(index, 2)
    own = core * pairs + index // 2
    swap = [(i, i ^ 1) for i in range(chunks)]
    same_core = [[2 * j + c for j in range(pairs)] for c in range(2)]
    wide = min(WIDE, channels // 2)
    steps = channels // wide
    part = steps // 2
    block = wide // SLICE
    fwd, inv = (jnp.asarray(v) for v in transforms())
    params = pltpu.CompilerParams(vmem_limit_bytes=58 * 2**20)
    little = pltpu.CompilerParams(vmem_limit_bytes=8 * 2**20)
    vmem, smem = pl.BlockSpec(memory_space=pltpu.VMEM), pl.BlockSpec(memory_space=pltpu.SMEM)
    states_shape = jax.ShapeDtypeStruct((pairs, 11 * M, SPAN), F32)
    core_scalar = core[None]

    def whole(a):
        return pl.BlockSpec(a.shape, lambda i, *_: (0,) * a.ndim)

    def exchange(values):
        return lax.all_to_all(values, "seq", 0, 0, axis_index_groups=same_core, tiled=True)

    def other_core(values):
        return lax.ppermute(values, "seq", swap)

    def ends_and_lags(half, x, g, room):
        return pl.pallas_call(
            first_kernel,
            grid_spec=pltpu.PrefetchScalarGridSpec(
                num_scalar_prefetch=1,
                grid=(part,),
                in_specs=[
                    pl.BlockSpec((1, SPAN, wide), lambda i, at: (0, 0, at[0] * part + i)),
                    pl.BlockSpec((1, SPAN, wide), lambda i, at: (0, 0, at[0] * part + i)),
                    pl.BlockSpec((M, wide // GROUP), lambda i, at: (0, at[0] * part + i)),
                    pl.BlockSpec((M, wide), lambda i, at: (0, at[0] * part + i)),
                    whole(fwd),
                    whole(inv),
                ],
                out_specs=pl.BlockSpec((block, 13 * M, SPAN), lambda i, at: (i, 0, 0)),
            ),
            out_shape=jax.ShapeDtypeStruct((pairs, 13 * M, SPAN), F32),
            compiler_params=room,
            name="ends_and_lags",
        )(half, x, g, log_rates, residues, fwd, inv)

    away = ends_and_lags(1 - core_scalar, signal, out_grad, params)
    away, x2, g2 = lax.optimization_barrier((away, signal, out_grad))
    arrived = other_core(away)
    kept = ends_and_lags(core_scalar, x2, g2, pltpu.CompilerParams(vmem_limit_bytes=40 * 2**20))
    state_block = pl.BlockSpec((block, 11 * M, SPAN), lambda i, at: (i, 0, 0))
    edge_block = pl.BlockSpec((block, 4 * M, SPAN), lambda i, at: (i, 0, 0))
    edge_shape = jax.ShapeDtypeStruct((pairs, 4 * M, SPAN), F32)
    pair, mine, near = pl.pallas_call(
        pair_kernel,
        grid_spec=pltpu.PrefetchScalarGridSpec(
            num_scalar_prefetch=1,
            grid=(part,),
            in_specs=[
                pl.BlockSpec((block, 13 * M, SPAN), lambda i, at: (i, 0, 0)),
                pl.BlockSpec((block, 11 * M, SPAN), lambda i, at: (i, 0, 0)),
                pl.BlockSpec((M, wide), lambda i, at: (0, at[0] * part + i)),
            ],
            out_specs=[state_block, edge_block, edge_block],
        ),
        out_shape=[states_shape, edge_shape, edge_shape],
        compiler_params=little,
        name="join_pair",
    )(core_scalar, kept, arrived, residues)
    pair, later_rates = lax.optimization_barrier((pair, log_rates))
    got = exchange(pair)

    decay_rate = jnp.exp(later_rates)
    rate_rows = decay_rate.T.reshape(chunks, 1, SPAN)
    own_rate = jnp.repeat(lax.dynamic_slice_in_dim(decay_rate, own * GROUPS, GROUPS, 1), GROUP, axis=1)

    work = SPAN * channels

    def convolutions(at, count, x, g, *earlier):
        kernel_blocks = [
            pl.BlockSpec((1, SPAN, wide), lambda i: (0, 0, at + i)),
            pl.BlockSpec((1, SPAN, wide), lambda i: (0, 0, at + i)),
            pl.BlockSpec((block, 1, SPAN), lambda i: (at + i, 0, 0)),
            pl.BlockSpec((M, wide), lambda i: (0, at + i)),
            whole(fwd),
            whole(inv),
        ]
        return pl.pallas_call(
            second_kernel,
            grid=(count,),
            in_specs=kernel_blocks + [pl.BlockSpec(memory_space=pl.ANY)] * len(earlier),
            out_specs=[pl.BlockSpec((SPAN, wide), lambda i: (0, at + i))] * 2,
            out_shape=[jax.ShapeDtypeStruct((SPAN, channels), F32)] * 2,
            input_output_aliases={6: 0, 7: 1} if earlier else {},
            compiler_params=params,
            cost_estimate=pl.CostEstimate(flops=work * 300, bytes_accessed=work * 2, transcendentals=0),
            name="local_convolutions",
        )(x, g, rate_rows, residues, fwd, inv, *earlier)

    early = steps - max(1, steps // 4)
    mixed_part, grad_part = convolutions(0, early, signal, out_grad)
    got, mixed_part, grad_part = lax.optimization_barrier((got, mixed_part, grad_part))
    back = pl.pallas_call(
        functools.partial(carry_kernel, pairs),
        out_shape=jax.ShapeDtypeStruct((chunks, 4 * M, SPAN), F32),
        in_specs=[smem, vmem, vmem, vmem],
        compiler_params=little,
        name="carries",
    )(own[None], got, own_rate, residues)
    back, got, x3, g3, mine = lax.optimization_barrier((back, got, signal, out_grad, mine))
    carried = lax.all_to_all(back, "seq", 0, 0, tiled=True).reshape(pairs, 2, 4 * M, SPAN)
    sums = pl.pallas_call(
        functools.partial(sums_kernel, pairs, 1.0 / (rows * chunks * SPAN)),
        out_shape=jax.ShapeDtypeStruct((3 * M, SPAN), F32),
        in_specs=[smem, vmem, vmem, vmem],
        compiler_params=little,
        cost_estimate=pl.CostEstimate(flops=10**10, bytes_accessed=10**7, transcendentals=0),
        name="gradient_sums",
    )(own[None], got, own_rate, residues)
    arriving = [lax.ppermute(sums, "batch", [(i, (i + k) % rows) for i in range(rows)]) for k in range(rows - 1, 0, -1)]
    far = other_core(mine)
    mixed_part, grad_part = convolutions(early, steps - early, x3, g3, mixed_part, grad_part)

    def total_kernel(*refs):
        total = refs[0][...]
        for ref in refs[1:-1]:
            total = total + ref[...]
        for k in range(chunks):
            refs[-1][k] = total

    total = pl.pallas_call(
        total_kernel,
        out_shape=jax.ShapeDtypeStruct((chunks, 3 * M, SPAN), F32),
        compiler_params=little,
        name="total",
    )(sums, *arriving)
    carried, total, mixed_part, grad_part, far = lax.optimization_barrier((carried, total, mixed_part, grad_part, far))
    everyone = lax.all_to_all(total, "seq", 0, 0, tiled=True)

    flat_block = pl.BlockSpec((SPAN, wide), lambda i, at: (0, i))
    seq_block = pl.BlockSpec((1, SPAN, wide), lambda i, at: (0, 0, i))
    half_block = pl.BlockSpec((block, 4 * M, SPAN), lambda i, at: (lax.rem(i, part), 0, 0))
    mixed, grad_signal = pl.pallas_call(
        last_kernel,
        grid_spec=pltpu.PrefetchScalarGridSpec(
            num_scalar_prefetch=1,
            grid=(steps,),
            in_specs=[
                flat_block,
                flat_block,
                pl.BlockSpec((block, 1, SPAN), lambda i, at: (i, 0, 0)),
                pl.BlockSpec((M, wide // GROUP), lambda i, at: (0, i)),
                pl.BlockSpec((M, wide), lambda i, at: (0, i)),
                pl.BlockSpec((block, None, 4 * M, SPAN), lambda i, at: (lax.rem(i, part), i // part, 0, 0)),
                half_block,
                half_block,
            ],
            out_specs=[seq_block, seq_block],
        ),
        out_shape=[jax.ShapeDtypeStruct(signal.shape, BF16)] * 2,
        compiler_params=params,
        cost_estimate=pl.CostEstimate(flops=work * 1600, bytes_accessed=work * 12, transcendentals=work),
        name="add_carries",
    )(core_scalar, mixed_part, grad_part, rate_rows, log_rates, residues, carried, near, far)
    grad_residues, grad_rates = pl.pallas_call(
        functools.partial(gather_kernel, pairs),
        out_shape=[jax.ShapeDtypeStruct(residues.shape, F32), jax.ShapeDtypeStruct(log_rates.shape, F32)],
        compiler_params=little,
        name="unpack",
    )(everyone, log_rates)
    return mixed, grad_signal, grad_residues, grad_rates


def solution(mesh):
    sharded = P("batch", "seq", None)
    return jax.shard_map(
        local,
        mesh=mesh,
        in_specs=(sharded, sharded, P(), P()),
        out_specs=(sharded, sharded, P(), P()),
        check_vma=False,
    )
```
